256 devices in a mesh: ctx: 16 (over x, y), head: 8 (over z), fsdp: 2 (over core).
Axes of the slice: x: 4, y: 4, z: 8, core: 2. Of those that a mesh axis runs over, the one named last changes fastest.
Arguments:
- layer_input: bfloat16 [16384, 4096], P(('ctx', 'fsdp')), may hold values from -6 to 6
- query_act: bfloat16 [16384, 4096], P(('ctx', 'fsdp'), 'head'), may hold values from -6 to 6
- key_act: bfloat16 [16384, 4096], P(('ctx', 'fsdp'), 'head'), may hold values from -6 to 6
- out_grad: bfloat16 [16384, 4096], P(('ctx', 'fsdp'), 'head'), may hold values from -6 to 6
- value_weight: bfloat16 [4096, 4096], P('fsdp', 'head'), may hold values from -0.09375 to 0.09375
Outputs:
- query_grad: bfloat16 [16384, 4096], P(('ctx', 'fsdp'), 'head')
- key_grad: bfloat16 [16384, 4096], P(('ctx', 'fsdp'), 'head')
- input_grad: bfloat16 [16384, 4096], P(('ctx', 'fsdp'), 'head')
- weight_grad: float32 [4096, 4096], P(('ctx', 'fsdp'), 'head')
The draws below stay inside these ranges and needn't reach their ends.
All inputs are finite; a program needn't handle non-finite values.
Results may differ from the reference program's by a relative error of at most 0.018.
Values may be sent and summed in bfloat16 or wider, within the bound.
No kernel may reach another device: no remote copies, remote signals or barrier semaphores. Data moves between devices by JAX's collectives and lax.ppermute only.
A program may use at most 64 MiB of HBM per device.

```python
import math
import jax
import jax.numpy as jnp
from jax import lax

D = 4096
HEADS = 32
HDIM = 128
TOK_DEV = 512
HD = 4096
TOKENS = 16384
N_HEAD = 8


def with_spikes(entries, key, source, target, blocks, factor):
    owner, partner = [(jnp.arange(entries.shape[position]) // (entries.shape[position] // blocks)).reshape([-1 if axis == position else 1 for axis in range(entries.ndim)]) for position in (source, target)]
    chosen = jax.random.permutation(key, blocks)[partner]
    strong = (owner == chosen) | (owner == (partner + blocks // 2) % blocks)
    return jnp.where(strong, factor * entries, entries)


def block_scale(key, dims, split, smallest, high):
    factor_of, own = 1.0, jax.random.fold_in(key, 6)
    for position, shards_of in split:
        draws = jnp.exp(jax.random.uniform(jax.random.fold_in(own, position), (shards_of,), jnp.float32, smallest / len(split), high / len(split)))
        factor_of = factor_of * jnp.repeat(draws, dims[position] // shards_of).reshape([-1 if axis == position else 1 for axis in range(len(dims))])
    return factor_of


def normal_values(stream_key, dims, spread, most, split=(), kind=jnp.bfloat16):
    values = spread * jax.random.normal(stream_key, dims, jnp.float32)
    if split:
        values = values * block_scale(stream_key, dims, split, -0.22, 0.18)
    return jnp.clip(values, -most, most).astype(kind)


def noise_with(own_key, extent, deviation, most, shards, heavy, held_as=jnp.bfloat16):
    result = deviation * jax.random.normal(own_key, extent, jnp.float32)
    if shards:
        result = result * block_scale(own_key, extent, shards, -0.22, 0.18)
    return jnp.clip(with_spikes(result, jax.random.fold_in(own_key, 3), *heavy), -most, most).astype(held_as)


def setup_inputs(seed: int = 0) -> dict:
    seeds = jax.random.split(jax.random.key(seed), 6)
    return {
        "layer_input": noise_with(seeds[0], (TOKENS, D), 1.0, 6.0, ((0, 32),), (0, 1, 32, 2.75)),
        "query_act": normal_values(seeds[1], (TOKENS, HD), 1.0, 6.0, ((0, 32), (1, 8))),
        "key_act": normal_values(seeds[2], (TOKENS, HD), 1.0, 6.0, ((0, 32), (1, 8))),
        "out_grad": normal_values(seeds[3], (TOKENS, HD), 1.0, 6.0, ((0, 32), (1, 8))),
        "value_weight": normal_values(seeds[4], (D, HD), D ** -0.5, 0.09375, ((0, 2), (1, 8))),
    }


def product(pattern, former, latter):
    return jnp.einsum(pattern, former, latter, precision=lax.Precision.HIGHEST)

def lowered(source):
    return lax.optimization_barrier(source.astype(jnp.bfloat16)).astype(jnp.float32)

def norm_grad(attended, grad_blk):
    inverse_rms = lax.rsqrt(lax.optimization_barrier(jnp.mean(attended * attended, axis=-1, keepdims=True)) + 1e-05)
    normed = attended * inverse_rms
    return inverse_rms * (grad_blk - normed * lax.optimization_barrier(jnp.mean(grad_blk * normed, axis=-1, keepdims=True)))

def block_backward(query_blk, key_blk, value_blk, grad_blk, state_prev, state_grad, causal):
    scores = product('thi,shi->hts', query_blk, key_blk)
    masked = lowered(jnp.where(causal[None], scores, 0.0))
    attended = product('hts,shj->thj', masked, value_blk) + product('thi,hij->thj', query_blk, state_prev)
    attn_grad = norm_grad(attended, grad_blk)
    attn_low = lowered(attn_grad)
    cross_terms = lowered(jnp.where(causal[None], product('thj,shj->hts', attn_low, value_blk), 0.0))
    query_part = product('hts,shi->thi', cross_terms, key_blk) + product('hij,thj->thi', state_prev, attn_grad)
    key_part = product('hts,thi->shi', cross_terms, query_blk) + product('hij,shj->shi', state_grad, value_blk)
    value_part = product('hts,thj->shj', masked, attn_low) + product('shi,hij->shj', key_blk, state_grad)
    local_grad = product('thi,thj->hij', query_blk, attn_grad)
    return (query_part, key_part, value_part, local_grad)

def reference(layer_input, query_act, key_act, out_grad, value_weight):
    blocks = TOKENS // TOK_DEV
    value_act = jnp.dot(layer_input, value_weight, preferred_element_type=jnp.float32).astype(jnp.bfloat16)

    def split_heads(source):
        return source.astype(jnp.float32).reshape(blocks, TOK_DEV, HEADS, HDIM)
    query_all = split_heads(query_act)
    key_all = split_heads(key_act)
    value_all = split_heads(value_act)
    grad_all = split_heads(out_grad)
    causal = jnp.tril(jnp.ones((TOK_DEV, TOK_DEV), dtype=bool))
    zero_state = jnp.zeros((HEADS, HDIM, HDIM), jnp.float32)

    def forward_step(carried, pieces):
        key_blk, value_blk = pieces
        update = product('shi,shj->hij', key_blk, value_blk)
        return (carried + update, carried)
    final_state, prior_states = lax.scan(forward_step, zero_state, (key_all, value_all))

    def backward_step(state_grad, pieces):
        query_blk, key_blk, value_blk, grad_blk, state_prev = pieces
        query_part, key_part, value_part, local_grad = block_backward(query_blk, key_blk, value_blk, grad_blk, state_prev, state_grad, causal)
        return (state_grad + local_grad, (query_part.astype(jnp.bfloat16), key_part.astype(jnp.bfloat16), value_part.astype(jnp.bfloat16)))
    unused, results = lax.scan(backward_step, zero_state, (query_all, key_all, value_all, grad_all, prior_states), reverse=True)
    query_grad = results[0].reshape(TOKENS, HEADS * HDIM)
    key_grad = results[1].reshape(TOKENS, HEADS * HDIM)
    value_grad = results[2].reshape(TOKENS, HEADS * HDIM)
    group_cols = HEADS * HDIM // N_HEAD
    input_sum = jnp.zeros((TOKENS, D), jnp.float32)
    for group in range(N_HEAD):
        grad_cols = value_grad[:, group * group_cols:(group + 1) * group_cols]
        weight_cols = value_weight[:, group * group_cols:(group + 1) * group_cols]
        partial_input = jnp.dot(grad_cols, weight_cols.T, preferred_element_type=jnp.float32)
        input_sum = input_sum + lowered(partial_input)
    input_grad = input_sum.astype(jnp.bfloat16)
    grad_scale = 1.0 / math.sqrt(TOKENS)

    def weight_step(running, pieces):
        input_blk, grad_blk = pieces
        partial_sum = jnp.dot(input_blk.T, grad_blk, preferred_element_type=jnp.float32) * grad_scale
        rounded = lax.optimization_barrier(partial_sum.astype(jnp.bfloat16))
        return (running + rounded.astype(jnp.float32), None)
    weight_grad, unused_too = lax.scan(weight_step, jnp.zeros((D, HEADS * HDIM), jnp.float32), (layer_input.reshape(blocks, TOK_DEV, D), value_grad.reshape(blocks, TOK_DEV, HEADS * HDIM)))
    return (query_grad, key_grad, input_grad, weight_grad)
```

```python
import math

import jax
import jax.numpy as jnp
from jax import lax
from jax.experimental import pallas as pl
from jax.experimental.pallas import tpu as pltpu
from jax.sharding import PartitionSpec as P

HDIM = 128
F32 = jnp.float32
BF16 = jnp.bfloat16
NT = (((1,), (1,)), ((), ()))
TN = (((0,), (0,)), ((), ()))
NN = (((1,), (0,)), ((), ()))


def dot(a, b, dims=NN):
    return lax.dot_general(a, b, dims, preferred_element_type=F32)


def params(**more):
    return pltpu.CompilerParams(vmem_limit_bytes=40 * 2**20, **more)


def cost(flops, nbytes):
    return pl.CostEstimate(flops=int(flops), bytes_accessed=int(nbytes), transcendentals=0)


def sds(shape, dtype):
    return jax.ShapeDtypeStruct(shape, dtype)


def value_own_kernel(core, x_ref, w_ref, o_ref):
    prod = dot(x_ref[...], w_ref[...])

    @pl.when(pl.program_id(0) == 0)
    def _():
        o_ref[...] = prod

    @pl.when(pl.program_id(0) > 0)
    def _():
        o_ref[...] += prod


def value_own(core, x, w):
    tok, _ = x.shape
    rows, cols = w.shape
    steps = rows // 512
    return pl.pallas_call(
        value_own_kernel,
        out_shape=sds((tok, cols), F32),
        grid_spec=pltpu.PrefetchScalarGridSpec(
            num_scalar_prefetch=1,
            grid=(steps,),
            in_specs=[
                pl.BlockSpec((tok, 512), lambda s, core: (0, core[0] * steps + s)),
                pl.BlockSpec((512, cols), lambda s, core: (s, 0)),
            ],
            out_specs=pl.BlockSpec((tok, cols), lambda s, core: (0, 0)),
        ),
        compiler_params=params(),
        cost_estimate=cost(2 * tok * rows * cols, 2 * (tok * rows + rows * cols)),
        name="value_own",
    )(core, x, w)


def value_rest_kernel(core, x_ref, w_ref, part_ref, k_ref, v_ref, pair_ref, acc):
    step = pl.program_id(0)
    prod = dot(x_ref[...], w_ref[...])

    @pl.when(step == 0)
    def _():
        acc[...] = part_ref[...] + prod

    @pl.when(step > 0)
    def _():
        acc[...] += prod

    @pl.when(step == pl.num_programs(0) - 1)
    def _():
        v = acc[...].astype(BF16)
        v_ref[...] = v
        for h in range(v.shape[1] // HDIM):
            cols = slice(h * HDIM, (h + 1) * HDIM)
            pair_ref[cols, :] = dot(k_ref[:, cols], v[:, cols], TN).astype(BF16)


def value_rest(core, x, w, part, k):
    tok, _ = x.shape
    rows, cols = w.shape
    steps = rows // 512
    return pl.pallas_call(
        value_rest_kernel,
        out_shape=(sds((tok, cols), BF16), sds((cols, HDIM), BF16)),
        grid_spec=pltpu.PrefetchScalarGridSpec(
            num_scalar_prefetch=1,
            grid=(steps,),
            in_specs=[
                pl.BlockSpec((tok, 512), lambda s, core: (0, (1 - core[0]) * steps + s)),
                pl.BlockSpec((512, cols), lambda s, core: (s, 0)),
                pl.BlockSpec((tok, cols), lambda s, core: (0, 0)),
                pl.BlockSpec((tok, cols), lambda s, core: (0, 0)),
            ],
            out_specs=(
                pl.BlockSpec((tok, cols), lambda s, core: (0, 0)),
                pl.BlockSpec((cols, HDIM), lambda s, core: (0, 0)),
            ),
            scratch_shapes=[pltpu.VMEM((tok, cols), F32)],
        ),
        compiler_params=params(),
        cost_estimate=cost(2 * tok * rows * cols, 2 * (tok * rows + rows * cols)),
        name="value_rest",
    )(core, x, w, part, k)


def tril(scores):
    rows = lax.broadcasted_iota(jnp.int32, scores.shape, 0)
    cols = lax.broadcasted_iota(jnp.int32, scores.shape, 1)
    return jnp.where(rows >= cols, scores, 0.0).astype(BF16)


def head_spec(tok):
    return pl.BlockSpec((tok, HDIM), lambda h: (0, h))


def state_spec():
    return pl.BlockSpec((HDIM, HDIM), lambda h: (h, 0))


def mask_spec(tok):
    return pl.BlockSpec((1, tok, tok), lambda h: (h, 0, 0))


def inside_kernel(q_ref, k_ref, v_ref, m_ref, a_ref):
    m = tril(dot(q_ref[...], k_ref[...], NT))
    m_ref[0] = m
    a_ref[...] = dot(m, v_ref[...])


def inside(q, k, v):
    tok, cols = q.shape
    heads = cols // HDIM
    return pl.pallas_call(
        inside_kernel,
        out_shape=(sds((heads, tok, tok), BF16), sds((tok, cols), F32)),
        grid=(heads,),
        in_specs=[head_spec(tok)] * 3,
        out_specs=(mask_spec(tok), head_spec(tok)),
        compiler_params=params(),
        cost_estimate=cost(4 * tok * tok * cols, 10 * tok * cols + 2 * heads * tok * tok),
        name="inside",
    )(q, k, v)


def norm_kernel(q_ref, g_ref, a_ref, near_ref, far_ref, low_ref, state_ref, local_ref):
    state = (near_ref[...] + far_ref[...].astype(F32)).astype(BF16)
    state_ref[...] = state
    att = a_ref[...] + dot(q_ref[...], state)
    inv = lax.rsqrt(jnp.mean(att * att, axis=-1, keepdims=True) + 1e-05)
    normed = att * inv
    g = g_ref[...].astype(F32)
    low = (inv * (g - normed * jnp.mean(g * normed, axis=-1, keepdims=True))).astype(BF16)
    low_ref[...] = low
    local_ref[...] = dot(q_ref[...], low, TN).astype(BF16)


def norm_step(q, g, a, near, far):
    tok, cols = q.shape
    heads = cols // HDIM
    return pl.pallas_call(
        norm_kernel,
        out_shape=(sds((tok, cols), BF16), sds((cols, HDIM), BF16), sds((cols, HDIM), BF16)),
        grid=(heads,),
        in_specs=[head_spec(tok)] * 3 + [state_spec()] * 2,
        out_specs=(head_spec(tok), state_spec(), state_spec()),
        compiler_params=params(),
        cost_estimate=cost(4 * tok * cols * HDIM, 10 * tok * cols),
        name="norm_grad",
    )(q, g, a, near, far)


def cross_kernel(q_ref, k_ref, v_ref, low_ref, m_ref, state_ref, qg_ref, kp_ref, vp_ref):
    low = low_ref[...]
    c = tril(dot(low, v_ref[...], NT))
    qg_ref[...] = (dot(c, k_ref[...]) + dot(low, state_ref[...], NT)).astype(BF16)
    kp_ref[...] = dot(c, q_ref[...], TN)
    vp_ref[...] = dot(m_ref[0], low, TN)


def cross_step(q, k, v, low, m, state):
    tok, cols = q.shape
    heads = cols // HDIM
    return pl.pallas_call(
        cross_kernel,
        out_shape=(sds((tok, cols), BF16), sds((tok, cols), F32), sds((tok, cols), F32)),
        grid=(heads,),
        in_specs=[head_spec(tok)] * 4 + [mask_spec(tok), state_spec()],
        out_specs=(head_spec(tok),) * 3,
        compiler_params=params(),
        cost_estimate=cost(8 * tok * tok * cols, 18 * tok * cols + 2 * heads * tok * tok),
        name="cross",
    )(q, k, v, low, m, state)


def value_grad_kernel(core, k_ref, vp_ref, near_ref, far_ref, own_ref, other_ref, vg_ref, state_ref, out_ref):
    step = pl.program_id(0)
    half = pl.num_programs(0) // 2

    @pl.when(step == 0)
    def _():
        for h in range(k_ref.shape[1] // HDIM):
            cols = slice(h * HDIM, (h + 1) * HDIM)
            state = (near_ref[cols, :] + far_ref[cols, :].astype(F32)).astype(BF16)
            state_ref[cols, :] = state
            vg_ref[:, cols] = (vp_ref[:, cols] + dot(k_ref[:, cols], state)).astype(BF16)

    @pl.when(step < half)
    def _():
        out_ref[...] = dot(vg_ref[...], own_ref[...], NT).astype(BF16)

    @pl.when(step >= half)
    def _():
        out_ref[...] = dot(vg_ref[...], other_ref[...], NT).astype(BF16)


def value_grad_step(core, k, vp, near, far, w_own, w_other):
    tok, cols = k.shape
    rows = w_own.shape[0]
    half = rows // 512
    whole = pl.BlockSpec((tok, cols), lambda s, core: (0, 0))
    states = pl.BlockSpec((cols, HDIM), lambda s, core: (0, 0))
    return pl.pallas_call(
        value_grad_kernel,
        out_shape=(sds((tok, cols), BF16), sds((cols, HDIM), BF16), sds((tok, 2 * rows), BF16)),
        grid_spec=pltpu.PrefetchScalarGridSpec(
            num_scalar_prefetch=1,
            grid=(2 * half,),
            in_specs=[
                whole,
                whole,
                states,
                states,
                pl.BlockSpec((512, cols), lambda s, core: (jnp.minimum(s, half - 1), 0)),
                pl.BlockSpec((512, cols), lambda s, core: (jnp.maximum(s - half, 0), 0)),
            ],
            out_specs=(
                whole,
                states,
                pl.BlockSpec(
                    (tok, 512), lambda s, core: (0, lax.rem(s + core[0] * half, 2 * half))
                ),
            ),
        ),
        compiler_params=params(),
        cost_estimate=cost(4 * tok * rows * cols, 4 * tok * rows + 4 * rows * cols),
        name="value_grad",
    )(core, k, vp, near, far, w_own, w_other)


def key_grad_kernel(v_ref, kp_ref, state_ref, kg_ref):
    kg_ref[...] = (kp_ref[...] + dot(v_ref[...], state_ref[...], NT)).astype(BF16)


def key_grad_step(v, kp, state):
    tok, cols = v.shape
    return pl.pallas_call(
        key_grad_kernel,
        out_shape=sds((tok, cols), BF16),
        grid=(cols // HDIM,),
        in_specs=[head_spec(tok), head_spec(tok), state_spec()],
        out_specs=head_spec(tok),
        compiler_params=params(),
        cost_estimate=cost(2 * tok * cols * HDIM, 8 * tok * cols),
        name="key_grad",
    )(v, kp, state)


def weight_grad_kernel(scale, core, vg_ref, x_ref, mine_ref, other_ref, turned):
    @pl.when(pl.program_id(0) == 0)
    def _():
        turned[...] = vg_ref[...].T

    res = dot(turned[...], x_ref[...]) * scale
    first = core[0] == 0
    for p in range(x_ref.shape[1] // 256):
        a = res[:, p * 256 : p * 256 + 128]
        b = res[:, p * 256 + 128 : p * 256 + 256]
        mine_ref[p] = jnp.where(first, a, b).astype(BF16)
        other_ref[p] = jnp.where(first, b, a).astype(BF16)


def weight_grad_step(core, vg, x, scale):
    tok, cols = vg.shape
    width = x.shape[1]
    pieces = width // 256
    out = pl.BlockSpec((2, cols, 128), lambda s, core: (s, 0, 0))

    def body(*refs):
        weight_grad_kernel(scale, *refs)

    return pl.pallas_call(
        body,
        out_shape=(sds((pieces, cols, 128), BF16),) * 2,
        grid_spec=pltpu.PrefetchScalarGridSpec(
            num_scalar_prefetch=1,
            grid=(width // 512,),
            in_specs=[
                pl.BlockSpec((tok, cols), lambda s, core: (0, 0)),
                pl.BlockSpec((tok, 512), lambda s, core: (0, s)),
            ],
            out_specs=(out, out),
            scratch_shapes=[pltpu.VMEM((cols, tok), BF16)],
        ),
        compiler_params=params(),
        cost_estimate=cost(2 * tok * width * cols, 2 * tok * width + 2 * width * cols),
        name="weight_grad",
    )(core, vg, x)


SIDE = 4


def along_x(a, k):
    return lax.ppermute(
        a, "ctx", [(i, i + SIDE * k) for i in range(16) if 0 <= i + SIDE * k < 16]
    )


def along_x_ring(a, k):
    return lax.ppermute(a, "ctx", [(i, (i + SIDE * k) % 16) for i in range(16)])


def along_y_ring(a, k):
    return lax.ppermute(
        a, "ctx", [(i, i // SIDE * SIDE + (i + k) % SIDE) for i in range(16)]
    )


def swap(a):
    return lax.ppermute(a, "fsdp", [(0, 1), (1, 0)])


def total(*terms):
    return sum(t.astype(F32) for t in terms)


def exclusive(mine, y, core, sign):
    got = [along_x(mine, sign * k) for k in (1, 2, 3)]
    before = total(*got)
    both = (before + mine.astype(F32)).astype(BF16)
    alone = before.astype(BF16)
    got = []
    for k in (1, 2, 3):
        onward = (y + k < SIDE) if sign == 1 else (y - k >= 0)
        got.append(along_y_ring(jnp.where(onward, both, alone), sign * k))
    near = before + total(*got)
    ahead = (core == 0) if sign == 1 else (core == 1)
    far = swap(jnp.where(ahead, near + mine.astype(F32), near).astype(BF16))
    return near, far


def pick(a, place):
    return lax.dynamic_index_in_dim(a, lax.rem(place, SIDE), 0, False)


def local(layer_input, query_act, key_act, out_grad, value_weight):
    tok = layer_input.shape[0]
    core = lax.axis_index("fsdp")
    place = lax.axis_index("ctx")
    x, y = place // SIDE, lax.rem(place, SIDE)
    core_arr = core.reshape(1).astype(jnp.int32)

    weight_other = swap(value_weight)
    part = value_own(core_arr, layer_input, value_weight)
    value, pair = value_rest(core_arr, layer_input, weight_other, part, key_act)
    masked, attended = inside(query_act, key_act, value)
    near, far = exclusive(pair, y, core, 1)
    low, state, own_grad = norm_step(query_act, out_grad, attended, near, far)
    query_grad, key_part, value_part = cross_step(query_act, key_act, value, low, masked, state)
    near_g, far_g = exclusive(own_grad, y, core, -1)
    value_grad, state_grad, partial_input = value_grad_step(
        core_arr, key_act, value_part, near_g, far_g, value_weight, weight_other
    )
    input_grad = lax.psum_scatter(partial_input, "head", scatter_dimension=1, tiled=True)

    seq_devices = lax.axis_size(("ctx", "fsdp"))
    scale = 1.0 / math.sqrt(tok * seq_devices)
    mine, other = weight_grad_step(core_arr, value_grad, layer_input, scale)
    key_grad = key_grad_step(value, key_part, state_grad)
    chip = total(mine, swap(other)).astype(BF16).reshape((SIDE, SIDE) + mine.shape[1:])
    got = [along_x_ring(pick(chip, x + k), k) for k in (1, 2, 3)]
    line = total(pick(chip, x), *got).astype(BF16)
    got = [along_y_ring(pick(line, y + k), k) for k in (1, 2, 3)]
    weight_grad = total(pick(line, y), *got).T
    return (query_grad, key_grad, input_grad, weight_grad)


def solution(mesh):
    in_specs = (
        P(("ctx", "fsdp"), None),
        P(("ctx", "fsdp"), "head"),
        P(("ctx", "fsdp"), "head"),
        P(("ctx", "fsdp"), "head"),
        P("fsdp", "head"),
    )
    out_specs = (
        P(("ctx", "fsdp"), "head"),
        P(("ctx", "fsdp"), "head"),
        P(("ctx", "fsdp"), "head"),
        P(("ctx", "fsdp"), "head"),
    )
    return jax.shard_map(local, mesh=mesh, in_specs=in_specs, out_specs=out_specs, check_vma=False)
```

```python
import math

import jax
import jax.numpy as jnp
from jax import lax
from jax.experimental import pallas as pl
from jax.experimental.pallas import tpu as pltpu
from jax.sharding import PartitionSpec as P

HDIM = 128
F32 = jnp.float32
BF16 = jnp.bfloat16
NT = (((1,), (1,)), ((), ()))
TN = (((0,), (0,)), ((), ()))
NN = (((1,), (0,)), ((), ()))


def dot(a, b, dims=NN):
    return lax.dot_general(a, b, dims, preferred_element_type=F32)


def params(**more):
    return pltpu.CompilerParams(vmem_limit_bytes=58 * 2**20, **more)


def cost(flops, nbytes):
    return pl.CostEstimate(flops=int(flops), bytes_accessed=int(nbytes), transcendentals=0)


def sds(shape, dtype):
    return jax.ShapeDtypeStruct(shape, dtype)


def value_own_kernel(core, x_ref, w_ref, o_ref):
    prod = dot(x_ref[...], w_ref[...])

    @pl.when(pl.program_id(0) == 0)
    def _():
        o_ref[...] = prod

    @pl.when(pl.program_id(0) > 0)
    def _():
        o_ref[...] += prod


def value_own(core, x, w):
    tok, _ = x.shape
    rows, cols = w.shape
    steps = rows // 512
    return pl.pallas_call(
        value_own_kernel,
        out_shape=sds((tok, cols), F32),
        grid_spec=pltpu.PrefetchScalarGridSpec(
            num_scalar_prefetch=1,
            grid=(steps,),
            in_specs=[
                pl.BlockSpec((tok, 512), lambda s, core: (0, core[0] * steps + s)),
                pl.BlockSpec((512, cols), lambda s, core: (s, 0)),
            ],
            out_specs=pl.BlockSpec((tok, cols), lambda s, core: (0, 0)),
        ),
        compiler_params=params(),
        cost_estimate=cost(2 * tok * rows * cols, 2 * (tok * rows + rows * cols)),
        name="value_own",
    )(core, x, w)


def value_rest_kernel(core, x_ref, w_ref, part_ref, k_ref, v_ref, pair_ref, acc):
    step = pl.program_id(0)
    prod = dot(x_ref[...], w_ref[...])

    @pl.when(step == 0)
    def _():
        acc[...] = part_ref[...] + prod

    @pl.when(step > 0)
    def _():
        acc[...] += prod

    @pl.when(step == pl.num_programs(0) - 1)
    def _():
        v = acc[...].astype(BF16)
        v_ref[...] = v
        for h in range(v.shape[1] // HDIM):
            cols = slice(h * HDIM, (h + 1) * HDIM)
            pair_ref[cols, :] = dot(k_ref[:, cols], v[:, cols], TN).astype(BF16)


def value_rest(core, x, w, part, k):
    tok, _ = x.shape
    rows, cols = w.shape
    steps = rows // 512
    return pl.pallas_call(
        value_rest_kernel,
        out_shape=(sds((tok, cols), BF16), sds((cols, HDIM), BF16)),
        grid_spec=pltpu.PrefetchScalarGridSpec(
            num_scalar_prefetch=1,
            grid=(steps,),
            in_specs=[
                pl.BlockSpec((tok, 512), lambda s, core: (0, (1 - core[0]) * steps + s)),
                pl.BlockSpec((512, cols), lambda s, core: (s, 0)),
                pl.BlockSpec((tok, cols), lambda s, core: (0, 0)),
                pl.BlockSpec((tok, cols), lambda s, core: (0, 0)),
            ],
            out_specs=(
                pl.BlockSpec((tok, cols), lambda s, core: (0, 0)),
                pl.BlockSpec((cols, HDIM), lambda s, core: (0, 0)),
            ),
            scratch_shapes=[pltpu.VMEM((tok, cols), F32)],
        ),
        compiler_params=params(),
        cost_estimate=cost(2 * tok * rows * cols, 2 * (tok * rows + rows * cols)),
        name="value_rest",
    )(core, x, w, part, k)


def tril(scores):
    rows = lax.broadcasted_iota(jnp.int32, scores.shape, 0)
    cols = lax.broadcasted_iota(jnp.int32, scores.shape, 1)
    return jnp.where(rows >= cols, scores, 0.0).astype(BF16)


def head_spec(tok):
    return pl.BlockSpec((tok, HDIM), lambda h: (0, h))


def state_spec():
    return pl.BlockSpec((HDIM, HDIM), lambda h: (h, 0))


ANY = pl.BlockSpec(memory_space=pl.ANY)


def inside_kernel(q_ref, k_ref, v_ref, a_ref):
    a_ref[...] = dot(tril(dot(q_ref[...], k_ref[...], NT)), v_ref[...])


def inside(q, k, v):
    tok, cols = q.shape
    return pl.pallas_call(
        inside_kernel,
        out_shape=sds((tok, cols), F32),
        grid=(cols // HDIM,),
        in_specs=[head_spec(tok)] * 3,
        out_specs=head_spec(tok),
        compiler_params=params(),
        cost_estimate=cost(4 * tok * tok * cols, 10 * tok * cols),
        name="inside",
    )(q, k, v)


def norm_kernel(q_ref, g_ref, a_ref, near_ref, far_ref, low_ref, state_ref, local_ref):
    state = (near_ref[...] + far_ref[...].astype(F32)).astype(BF16)
    state_ref[...] = state
    att = a_ref[...] + dot(q_ref[...], state)
    inv = lax.rsqrt(jnp.mean(att * att, axis=-1, keepdims=True) + 1e-05)
    normed = att * inv
    g = g_ref[...].astype(F32)
    low = (inv * (g - normed * jnp.mean(g * normed, axis=-1, keepdims=True))).astype(BF16)
    low_ref[...] = low
    local_ref[...] = dot(q_ref[...], low, TN).astype(BF16)


def norm_step(q, g, a, near, far):
    tok, cols = q.shape
    return pl.pallas_call(
        norm_kernel,
        out_shape=(sds((tok, cols), BF16), sds((cols, HDIM), BF16), sds((cols, HDIM), BF16)),
        grid=(cols // HDIM,),
        in_specs=[head_spec(tok)] * 3 + [state_spec()] * 2,
        out_specs=(head_spec(tok), state_spec(), state_spec()),
        compiler_params=params(),
        cost_estimate=cost(4 * tok * cols * HDIM, 10 * tok * cols),
        name="norm_grad",
    )(q, g, a, near, far)


def cross_kernel(q_ref, k_ref, v_ref, low_ref, state_ref, qg_ref, kp_ref, vp_ref):
    low = low_ref[...]
    c = tril(dot(low, v_ref[...], NT))
    qg_ref[...] = (dot(c, k_ref[...]) + dot(low, state_ref[...], NT)).astype(BF16)
    kp_ref[...] = dot(c, q_ref[...], TN)
    m = tril(dot(q_ref[...], k_ref[...], NT))
    vp_ref[...] = dot(m, low, TN)


def cross_step(q, k, v, low, state):
    tok, cols = q.shape
    return pl.pallas_call(
        cross_kernel,
        out_shape=(sds((tok, cols), BF16), sds((tok, cols), F32), sds((tok, cols), F32)),
        grid=(cols // HDIM,),
        in_specs=[head_spec(tok)] * 4 + [state_spec()],
        out_specs=(head_spec(tok),) * 3,
        compiler_params=params(),
        cost_estimate=cost(10 * tok * tok * cols, 18 * tok * cols),
        name="cross",
    )(q, k, v, low, state)


def fold_x_kernel(keep, mine_ref, a_ref, b_ref, c_ref, _, before_ref, *msgs):
    before = a_ref[...].astype(F32) + b_ref[...].astype(F32) + c_ref[...].astype(F32)
    before_ref[...] = before
    both = (before + mine_ref[...].astype(F32)).astype(BF16)
    alone = before.astype(BF16)
    for i, ref in enumerate(msgs):
        ref[...] = jnp.where(keep[i] > 0, both, alone)


def fold_y_kernel(ahead, mine_ref, before_ref, a_ref, b_ref, c_ref, near_ref, far_ref):
    near = before_ref[...] + (
        a_ref[...].astype(F32) + b_ref[...].astype(F32) + c_ref[...].astype(F32)
    )
    near_ref[...] = near
    more = near + mine_ref[...].astype(F32)
    far_ref[...] = jnp.where(ahead[0] > 0, more, near).astype(BF16)


def whole(shape):
    return pl.BlockSpec(shape, lambda s, *_: (0,) * len(shape))


def single(body, scalars, ins, specs, outs, flops=0, scratch=(), name=None, grid=1, out_specs=None):
    nbytes = sum(math.prod(o.shape) * o.dtype.itemsize for o in outs) * 2
    return pl.pallas_call(
        body,
        out_shape=tuple(outs),
        grid_spec=pltpu.PrefetchScalarGridSpec(
            num_scalar_prefetch=1,
            grid=(grid,),
            in_specs=specs,
            out_specs=out_specs or tuple(whole(o.shape) for o in outs),
            scratch_shapes=list(scratch),
        ),
        compiler_params=params(),
        cost_estimate=cost(flops, nbytes),
        name=name,
    )(scalars, *ins)


SIDE = 4


def along_x(a, k):
    return lax.ppermute(
        a, "ctx", [(i, i + SIDE * k) for i in range(16) if 0 <= i + SIDE * k < 16]
    )


def along_x_ring(a, k):
    return lax.ppermute(a, "ctx", [(i, (i + SIDE * k) % 16) for i in range(16)])


def along_y_ring(a, k):
    return lax.ppermute(
        a, "ctx", [(i, i // SIDE * SIDE + (i + k) % SIDE) for i in range(16)]
    )


def along_z(a, k):
    return lax.ppermute(a, "head", [(i, (i + k) % 8) for i in range(8)])


def swap(a):
    return lax.ppermute(a, "fsdp", [(0, 1), (1, 0)])


def exclusive(mine, keep, ahead, sign, work):
    shape = mine.shape
    got = [along_x(mine, sign * k) for k in (1, 2, 3)]
    done = work()
    before, *msgs = single(
        fold_x_kernel,
        keep,
        [mine, *got, jax.tree.leaves(done)[0]],
        [whole(shape)] * 4 + [ANY],
        [sds(shape, F32)] + [sds(shape, BF16)] * 3,
        name="fold_x",
    )
    got = [along_y_ring(m, sign * k) for m, k in zip(msgs, (1, 2, 3))]
    near, far = single(
        fold_y_kernel,
        ahead,
        [mine, before, *got],
        [whole(shape)] * 5,
        [sds(shape, F32), sds(shape, BF16)],
        name="fold_y",
    )
    return near, swap(far), done


def chunk_product(dests, vg, own_ref, other_ref, step, rows, use):
    core = dests[8]
    mine = dests[step] // 4 == core

    @pl.when(mine)
    def _():
        use(dot(vg, own_ref[...], NT).astype(BF16))

    @pl.when(jnp.logical_not(mine))
    def _():
        use(dot(vg, other_ref[...], NT).astype(BF16))


def first_kernel(dests, k_ref, vp_ref, near_ref, far_ref, own_ref, other_ref, vg_ref, state_ref, right_ref, left_ref):
    for h in range(k_ref.shape[1] // HDIM):
        cols = slice(h * HDIM, (h + 1) * HDIM)
        state = (near_ref[cols, :] + far_ref[cols, :].astype(F32)).astype(BF16)
        state_ref[cols, :] = state
        vg_ref[:, cols] = (vp_ref[:, cols] + dot(k_ref[:, cols], state)).astype(BF16)
    half = right_ref.shape[0]

    def use(p):
        right_ref[...] = p[:half]
        left_ref[...] = p[half:]

    chunk_product(dests, vg_ref[...], own_ref, other_ref, 0, 512, use)


def second_kernel(dests, vg_ref, own_ref, other_ref, rb_ref, la_ref, pa_ref, pb_ref):
    half = rb_ref.shape[0]
    step = pl.program_id(0)

    def use(p):
        @pl.when(step == 0)
        def _():
            pa_ref[...] = p[:half]
            rb_ref[...] = p[half:]

        @pl.when(step == 1)
        def _():
            la_ref[...] = p[:half]
            pb_ref[...] = p[half:]

    chunk_product(dests, vg_ref[...], own_ref, other_ref, 1 + step, 512, use)


def rest_kernel(dests, vg_ref, own_ref, other_ref, _, p_ref):
    def use(p):
        p_ref[0] = p

    chunk_product(dests, vg_ref[...], own_ref, other_ref, 3 + pl.program_id(0), 512, use)


def weight_chunk(first):
    return pl.BlockSpec((512, 512), lambda s, dests: (lax.rem(dests[first + s], 4), 0))


def turn_kernel(r_ref, l_ref, pr_ref, pl_ref, _, ro_ref, lo_ref):
    ro_ref[...] = (r_ref[...].astype(F32) + pr_ref[...].reshape(r_ref.shape).astype(F32)).astype(BF16)
    lo_ref[...] = (l_ref[...].astype(F32) + pl_ref[...].reshape(l_ref.shape).astype(F32)).astype(BF16)


def turn(r, l, pr, pr_at, pl_, pl_at, after):
    def part(at):
        if at is None:
            return pl.BlockSpec(r.shape, lambda s: (0, 0))
        return pl.BlockSpec((1,) + r.shape, lambda s: at + (0,))

    msg = pl.BlockSpec(r.shape, lambda s: (0, 0))
    return pl.pallas_call(
        turn_kernel,
        out_shape=(sds(r.shape, BF16),) * 2,
        grid=(1,),
        in_specs=[msg, msg, part(pr_at), part(pl_at), ANY],
        out_specs=(msg, msg),
        compiler_params=params(),
        cost_estimate=cost(0, 12 * r.size),
        name="turn",
    )(r, l, pr, pl_, after)


def last_kernel(p_ref, ra_ref, la_ref, rb_ref, lb_ref, _, o_ref):
    half = ra_ref.shape[0]
    p = p_ref[0].astype(F32)
    o_ref[:half] = (p[:half] + ra_ref[...].astype(F32) + la_ref[...].astype(F32)).astype(BF16)
    o_ref[half:] = (p[half:] + rb_ref[...].astype(F32) + lb_ref[...].astype(F32)).astype(BF16)


def last_turn(p, ra, la, rb, lb, after):
    _, tok, cols = p.shape
    msg = pl.BlockSpec(ra.shape, lambda s: (0, 0))
    return pl.pallas_call(
        last_kernel,
        out_shape=sds((tok, cols), BF16),
        grid=(1,),
        in_specs=[pl.BlockSpec((1, tok, cols), lambda s: (4, 0, 0)), msg, msg, msg, msg, ANY],
        out_specs=pl.BlockSpec((tok, cols), lambda s: (0, 0)),
        compiler_params=params(),
        cost_estimate=cost(0, 8 * tok * cols),
        name="last_turn",
    )(p, ra, la, rb, lb, after)


def key_grad_kernel(v_ref, kp_ref, state_ref, _, kg_ref):
    kg_ref[...] = (kp_ref[...] + dot(v_ref[...], state_ref[...], NT)).astype(BF16)


def key_grad_step(v, kp, state, after):
    tok, cols = v.shape
    return pl.pallas_call(
        key_grad_kernel,
        out_shape=sds((tok, cols), BF16),
        grid=(cols // HDIM,),
        in_specs=[head_spec(tok), head_spec(tok), state_spec(), ANY],
        out_specs=head_spec(tok),
        compiler_params=params(),
        cost_estimate=cost(2 * tok * cols * HDIM, 8 * tok * cols),
        name="key_grad",
    )(v, kp, state, after)


def weight_grad_kernel(scale, side, core, vg_ref, x_ref, _, o_ref, turned):
    @pl.when(pl.program_id(0) == 0)
    def _():
        turned[...] = vg_ref[...].T

    first = (core[0] == 0) if side == 0 else (core[0] == 1)
    x = x_ref[...]
    both = []
    for p in range(x.shape[1] // 256):
        a = x[:, p * 256 : p * 256 + 128]
        b = x[:, p * 256 + 128 : p * 256 + 256]
        both.append(jnp.where(first, a, b))
    res = dot(turned[...], jnp.concatenate(both, axis=1)) * scale
    for p in range(len(both)):
        o_ref[p] = res[:, p * 128 : p * 128 + 128].astype(BF16)


def weight_grad_step(core, vg, x, scale, side, after):
    tok, cols = vg.shape
    width = x.shape[1]
    pieces = width // 256

    def body(*refs):
        weight_grad_kernel(scale, side, *refs)

    return single(
        body,
        core,
        [vg, x, after],
        [whole((tok, cols)), pl.BlockSpec((tok, 1024), lambda s, core: (0, s)), ANY],
        [sds((pieces, cols, 128), BF16)],
        flops=tok * width * cols,
        scratch=[pltpu.VMEM((cols, tok), BF16)],
        name="weight_grad",
        grid=width // 1024,
        out_specs=(pl.BlockSpec((4, cols, 128), lambda s, core: (s, 0, 0)),),
    )[0]


def chip_kernel(where, a_ref, b_ref, _, ru2, lv2, rv1, lu1, cu1, cv1, own):
    s = (a_ref[0].astype(F32) + b_ref[0].astype(F32)).astype(BF16)
    half = s.shape[1] // 2
    step = pl.program_id(0)

    @pl.when(step == 0)
    def _():
        ru2[...] = s[:, :half]
        lv2[...] = s[:, half:]

    @pl.when(step == 1)
    def _():
        cu1[...] = s[:, :half]
        rv1[...] = s[:, half:]

    @pl.when(step == 2)
    def _():
        lu1[...] = s[:, :half]
        cv1[...] = s[:, half:]

    @pl.when(step == 3)
    def _():
        own[...] = s


def chip_step(where, mine, other, after):
    _, _, cols, width = mine.shape
    block = pl.BlockSpec((1, SIDE, cols, width), lambda s, where: (where[s], 0, 0, 0))
    piece = sds((SIDE, cols // 2, width), BF16)
    return single(
        chip_kernel,
        where,
        [mine, other, after],
        [block, block, ANY],
        [piece] * 6 + [sds((SIDE, cols, width), BF16)],
        name="chip",
        grid=4,
    )


def pair_kernel(_, a_ref, b_ref, c_ref, d_ref, _2, o_ref, p_ref):
    o_ref[...] = (a_ref[...].astype(F32) + b_ref[...].astype(F32)).astype(BF16)
    p_ref[...] = (c_ref[...].astype(F32) + d_ref[...].astype(F32)).astype(BF16)


def line_kernel(where, own_ref, ru_ref, lu_ref, rv_ref, lv_ref, _, m1, m2, m3, keep):
    own = own_ref[0].astype(F32)
    half = own.shape[0] // 2
    u = own[:half] + ru_ref[0].astype(F32) + lu_ref[0].astype(F32)
    v = own[half:] + rv_ref[0].astype(F32) + lv_ref[0].astype(F32)
    step = pl.program_id(0)
    for i, ref in enumerate((m1, m2, m3)):

        @pl.when(step == i)
        def _():
            ref[:half] = u.astype(BF16)
            ref[half:] = v.astype(BF16)

    @pl.when(step == 3)
    def _():
        keep[:half] = u
        keep[half:] = v


def line_step(where, own, ru, lu, rv, lv, after):
    _, cols, width = own.shape
    big = pl.BlockSpec((1, cols, width), lambda s, where: (where[4 + s], 0, 0))
    small = pl.BlockSpec((1, cols // 2, width), lambda s, where: (where[4 + s], 0, 0))
    return single(
        line_kernel,
        where,
        [own, ru, lu, rv, lv, after],
        [big] + [small] * 4 + [ANY],
        [sds((cols, width), BF16)] * 3 + [sds((cols, width), F32)],
        name="line",
        grid=4,
    )


def owner_kernel(_, keep_ref, a_ref, b_ref, c_ref, o_ref):
    t = keep_ref[...] + a_ref[...].astype(F32) + b_ref[...].astype(F32) + c_ref[...].astype(F32)
    o_ref[...] = t.T


def local(layer_input, query_act, key_act, out_grad, value_weight):
    tok, width = layer_input.shape
    cols = query_act.shape[1]
    core = lax.axis_index("fsdp")
    place = lax.axis_index("ctx")
    group = lax.axis_index("head")
    x, y = place // SIDE, lax.rem(place, SIDE)
    core_arr = core.reshape(1).astype(jnp.int32)
    hops = jnp.arange(1, 4, dtype=jnp.int32)
    onward = (y + hops < SIDE).astype(jnp.int32)
    back = (y - hops >= 0).astype(jnp.int32)
    dests = jnp.concatenate(
        [lax.rem(group + jnp.array([4, 3, 5, 2, 6, 1, 7, 0], jnp.int32), 8), core_arr]
    )
    where = jnp.concatenate(
        [
            lax.rem(x + jnp.array([2, 1, 3, 0], jnp.int32), SIDE),
            lax.rem(y + jnp.array([1, 2, 3, 0], jnp.int32), SIDE),
        ]
    )

    weight_other = swap(value_weight)
    part = value_own(core_arr, layer_input, value_weight)
    value, pair = value_rest(core_arr, layer_input, weight_other, part, key_act)
    near, far, attended = exclusive(
        pair, onward, 1 - core_arr, 1, lambda: inside(query_act, key_act, value)
    )
    low, state, own_grad = norm_step(query_act, out_grad, attended, near, far)
    near, far, (query_grad, key_part, value_part) = exclusive(
        own_grad, back, core_arr, -1, lambda: cross_step(query_act, key_act, value, low, state)
    )

    both_w = [value_weight, weight_other]
    msg = sds((tok // 2, 512), BF16)
    value_grad, state_grad, ra4, lb4 = single(
        first_kernel,
        dests,
        [key_act, value_part, near, far, *both_w],
        [whole((tok, cols))] * 2 + [whole((cols, HDIM))] * 2 + [weight_chunk(0)] * 2,
        [sds((tok, cols), BF16), sds((cols, HDIM), BF16), msg, msg],
        flops=4 * tok * cols * 512,
        name="value_grad",
    )
    ra4, lb4 = along_z(ra4, 1), along_z(lb4, -1)
    rb3, la3, pa3, pb3 = single(
        second_kernel,
        dests,
        [value_grad, *both_w],
        [whole((tok, cols))] + [weight_chunk(1)] * 2,
        [msg] * 4,
        flops=4 * tok * cols * 512,
        name="second",
        grid=2,
    )
    rb3, la3 = along_z(rb3, 1), along_z(la3, -1)

    seq_devices = lax.axis_size(("ctx", "fsdp"))
    scale = 1.0 / math.sqrt(tok * seq_devices)
    other = weight_grad_step(core_arr, value_grad, layer_input, scale, 1, pa3)
    got = swap(other)

    r, l = turn(ra4, lb4, pa3, None, pb3, None, other)
    ra3, lb3 = along_z(r, 1), along_z(l, -1)
    (rest,) = single(
        rest_kernel,
        dests,
        [value_grad, *both_w, r],
        [whole((tok, cols))] + [weight_chunk(3)] * 2 + [ANY],
        [sds((5, tok, 512), BF16)],
        flops=10 * tok * cols * 512,
        name="rest",
        grid=5,
        out_specs=(pl.BlockSpec((1, tok, 512), lambda s, dests: (s, 0, 0)),),
    )
    r, l = turn(rb3, la3, rest, (0, 1), rest, (1, 0), rest)
    rb2, la2 = along_z(r, 1), along_z(l, -1)
    mine = weight_grad_step(core_arr, value_grad, layer_input, scale, 0, r)
    r, l = turn(ra3, lb3, rest, (0, 0), rest, (1, 1), mine)
    ra2, lb2 = along_z(r, 1), along_z(l, -1)

    grid4 = (SIDE, SIDE) + mine.shape[1:]
    ru2, lv2, rv1, lu1, cu1, cv1, own = chip_step(
        where, mine.reshape(grid4), got.reshape(grid4), r
    )
    ru2, lv2 = along_x_ring(ru2, 1), along_x_ring(lv2, -1)
    rv1, lu1 = along_x_ring(rv1, 1), along_x_ring(lu1, -1)
    r, l = turn(rb2, la2, rest, (2, 1), rest, (3, 0), own)
    rb1, la1 = along_z(r, 1), along_z(l, -1)
    key_grad = key_grad_step(value, key_part, state_grad, r)
    r, l = turn(ra2, lb2, rest, (2, 0), rest, (3, 1), key_grad)
    ra1, lb1 = along_z(r, 1), along_z(l, -1)

    ru1, lv1 = single(
        pair_kernel,
        core_arr,
        [cu1, ru2, cv1, lv2, r],
        [whole(cu1.shape)] * 4 + [ANY],
        [sds(cu1.shape, BF16)] * 2,
        name="pair",
    )
    ru1, lv1 = along_x_ring(ru1, 1), along_x_ring(lv1, -1)
    m1, m2, m3, keep = line_step(where, own, ru1, lu1, rv1, lv1, lv1)
    got = [along_y_ring(m, k) for m, k in zip((m1, m2, m3), (1, 2, 3))]
    input_grad = last_turn(rest, ra1, la1, rb1, lb1, keep)
    (weight_grad,) = single(
        owner_kernel,
        core_arr,
        [keep, *got],
        [whole((cols, 128))] * 4,
        [sds((128, cols), F32)],
        name="owner",
    )
    return (query_grad, key_grad, input_grad, weight_grad)


def solution(mesh):
    in_specs = (
        P(("ctx", "fsdp"), None),
        P(("ctx", "fsdp"), "head"),
        P(("ctx", "fsdp"), "head"),
        P(("ctx", "fsdp"), "head"),
        P("fsdp", "head"),
    )
    out_specs = (
        P(("ctx", "fsdp"), "head"),
        P(("ctx", "fsdp"), "head"),
        P(("ctx", "fsdp"), "head"),
        P(("ctx", "fsdp"), "head"),
    )
    return jax.shard_map(local, mesh=mesh, in_specs=in_specs, out_specs=out_specs, check_vma=False)
```

```python
import math

import jax
import jax.numpy as jnp
from jax import lax
from jax.experimental import pallas as pl
from jax.experimental.pallas import tpu as pltpu
from jax.sharding import PartitionSpec as P

HDIM = 128
SIDE = 4
RING = 8
F32 = jnp.float32
BF16 = jnp.bfloat16
NT = (((1,), (1,)), ((), ()))
TN = (((0,), (0,)), ((), ()))
NN = (((1,), (0,)), ((), ()))

VMEM = pl.BlockSpec(memory_space=pltpu.VMEM)
SMEM = pl.BlockSpec(memory_space=pltpu.SMEM)
ANY = pl.BlockSpec(memory_space=pl.ANY)
HBM = pl.BlockSpec(memory_space=pltpu.HBM)


def dot(a, b, dims=NN):
    return lax.dot_general(a, b, dims, preferred_element_type=F32)


def sds(shape, dtype=BF16):
    return jax.ShapeDtypeStruct(shape, dtype)


def wide(ref):
    return ref[...].astype(F32)


def call(body, specs, ins, outs, name, scratch=(), limit=16):
    return pl.pallas_call(
        body,
        out_shape=tuple(outs),
        in_specs=specs,
        out_specs=tuple([VMEM] * len(outs)),
        scratch_shapes=list(scratch),
        compiler_params=pltpu.CompilerParams(vmem_limit_bytes=limit * 2**20),
        cost_estimate=pl.CostEstimate(flops=1000, bytes_accessed=1000, transcendentals=0),
        name=name,
    )(*ins)


def heads_of(ref):
    return [slice(h, h + HDIM) for h in range(0, ref.shape[1], HDIM)]


def tril(scores):
    rows = lax.broadcasted_iota(jnp.int32, scores.shape, 0)
    cols = lax.broadcasted_iota(jnp.int32, scores.shape, 1)
    return jnp.where(rows >= cols, scores, 0.0).astype(BF16)


def value_own_kernel(core, x_hbm, w_hbm, x_ref, w_ref, part_ref, sems):
    step = 512
    n = x_hbm.shape[1] // step
    half = n // 2

    def x_cols(j):
        return pl.ds(pl.multiple_of(lax.rem(core[0] * half + j, n) * step, step), step)

    xs = [
        pltpu.make_async_copy(x_hbm.at[:, x_cols(j)], x_ref.at[:, x_cols(j)], sems.at[j])
        for j in range(n)
    ]
    ws = [
        pltpu.make_async_copy(
            w_hbm.at[pl.ds(j * step, step), :], w_ref.at[pl.ds(j * step, step), :], sems.at[n + j]
        )
        for j in range(half)
    ]
    for j in range(half):
        ws[j].start()
        xs[j].start()
    for j in range(half, n):
        xs[j].start()
    for j in range(half):
        ws[j].wait()
        xs[j].wait()
        prod = dot(x_ref[:, x_cols(j)], w_ref[j * step : (j + 1) * step, :])
        if j == 0:
            part_ref[...] = prod
        else:
            part_ref[...] += prod
    for j in range(half, n):
        xs[j].wait()


def value_rest_kernel(core, x_ref, w_ref, part_ref, k_ref, v_ref, pair_ref):
    rows = w_ref.shape[0]
    cols = pl.ds(pl.multiple_of((1 - core[0]) * rows, rows), rows)
    v = (part_ref[...] + dot(x_ref[:, cols], w_ref[...])).astype(BF16)
    v_ref[...] = v
    for c in heads_of(v_ref):
        pair_ref[c, :] = dot(k_ref[:, c], v[:, c], TN).astype(BF16)


def inside_kernel(q_ref, k_ref, v_ref, a_ref):
    for c in heads_of(q_ref):
        a_ref[:, c] = dot(tril(dot(q_ref[:, c], k_ref[:, c], NT)), v_ref[:, c])


def norm_kernel(q_ref, g_ref, a_ref, near_ref, far_ref, low_ref, state_ref, local_ref):
    for c in heads_of(q_ref):
        state = (near_ref[c, :] + far_ref[c, :].astype(F32)).astype(BF16)
        state_ref[c, :] = state
        att = a_ref[:, c] + dot(q_ref[:, c], state)
        inv = lax.rsqrt(jnp.mean(att * att, axis=-1, keepdims=True) + 1e-05)
        normed = att * inv
        g = g_ref[:, c].astype(F32)
        low = (inv * (g - normed * jnp.mean(g * normed, axis=-1, keepdims=True))).astype(BF16)
        low_ref[:, c] = low
        local_ref[c, :] = dot(q_ref[:, c], low, TN).astype(BF16)


def cross_kernel(q_ref, k_ref, v_ref, low_ref, state_ref, qg_ref, kp_ref, vp_ref):
    for c in heads_of(q_ref):
        q, k, low = q_ref[:, c], k_ref[:, c], low_ref[:, c]
        cross = tril(dot(low, v_ref[:, c], NT))
        qg_ref[:, c] = (dot(cross, k) + dot(low, state_ref[c, :], NT)).astype(BF16)
        kp_ref[:, c] = dot(cross, q, TN)
        vp_ref[:, c] = dot(tril(dot(q, k, NT)), low, TN)


def fold_x_kernel(keep, mine_ref, a_ref, b_ref, c_ref, _, before_ref, *msgs):
    before = wide(a_ref) + wide(b_ref) + wide(c_ref)
    before_ref[...] = before
    both = (before + wide(mine_ref)).astype(BF16)
    alone = before.astype(BF16)
    for i, ref in enumerate(msgs):
        ref[...] = jnp.where(keep[i] > 0, both, alone)


def fold_y_kernel(ahead, mine_ref, before_ref, a_ref, b_ref, c_ref, near_ref, far_ref):
    near = before_ref[...] + (wide(a_ref) + wide(b_ref) + wide(c_ref))
    near_ref[...] = near
    far_ref[...] = jnp.where(ahead[0] > 0, near + wide(mine_ref), near).astype(BF16)


def along_x(a, k):
    return lax.ppermute(
        a, "ctx", [(i, i + SIDE * k) for i in range(16) if 0 <= i + SIDE * k < 16]
    )


def along_x_ring(a, k):
    return lax.ppermute(a, "ctx", [(i, (i + SIDE * k) % 16) for i in range(16)])


def along_y_ring(a, k):
    return lax.ppermute(
        a, "ctx", [(i, i // SIDE * SIDE + (i + k) % SIDE) for i in range(16)]
    )


def along_z(a, k):
    return lax.ppermute(a, "head", [(i, (i + k) % RING) for i in range(RING)])


def swap(a):
    return lax.ppermute(a, "fsdp", [(0, 1), (1, 0)])


def exclusive(mine, keep, ahead, sign, work):
    shape = mine.shape
    got = [along_x(mine, sign * k) for k in (1, 2, 3)]
    done = work()
    before, *msgs = call(
        fold_x_kernel,
        [SMEM] + [VMEM] * 4 + [ANY],
        [keep, mine, *got, done[0]],
        [sds(shape, F32)] + [sds(shape)] * 3,
        "fold_x",
    )
    got = [along_y_ring(m, sign * k) for m, k in zip(msgs, (1, 2, 3))]
    near, far = call(
        fold_y_kernel,
        [SMEM] + [VMEM] * 5,
        [ahead, mine, before, *got],
        [sds(shape, F32), sds(shape)],
        "fold_y",
    )
    return near, swap(far), done


def chunk_product(dests, which, vg, own_ref, other_ref, use):
    dest = dests[which]
    rows = pl.ds(pl.multiple_of(lax.rem(dest, RING // 2) * 512, 512), 512)
    mine = dest // (RING // 2) == dests[RING]

    @pl.when(mine)
    def _():
        use(dot(vg, own_ref[rows, :], NT).astype(BF16))

    @pl.when(jnp.logical_not(mine))
    def _():
        use(dot(vg, other_ref[rows, :], NT).astype(BF16))


def first_kernel(dests, k_ref, vp_ref, near_ref, far_ref, own_ref, other_ref, vg_ref, state_ref, right_ref, left_ref):
    for c in heads_of(k_ref):
        state = (near_ref[c, :] + far_ref[c, :].astype(F32)).astype(BF16)
        state_ref[c, :] = state
        vg_ref[:, c] = (vp_ref[:, c] + dot(k_ref[:, c], state)).astype(BF16)
    half = right_ref.shape[0]

    def use(p):
        right_ref[...] = p[:half]
        left_ref[...] = p[half:]

    chunk_product(dests, 0, vg_ref[...], own_ref, other_ref, use)


def chunks_kernel(first, dests, vg_ref, own_ref, other_ref, _, p_ref):
    for i in range(p_ref.shape[0]):

        def use(p):
            p_ref[i] = p

        chunk_product(dests, first + i, vg_ref[...], own_ref, other_ref, use)


def open_turn_kernel(r_ref, l_ref, p_ref, _, ro_ref, lo_ref):
    half = r_ref.shape[0]
    ro_ref[:half] = (wide(r_ref) + p_ref[0, :half].astype(F32)).astype(BF16)
    ro_ref[half:] = p_ref[0, half:]
    lo_ref[:half] = p_ref[1, :half]
    lo_ref[half:] = (wide(l_ref) + p_ref[1, half:].astype(F32)).astype(BF16)


def turn_kernel(first, r_ref, l_ref, p_ref, _, ro_ref, lo_ref):
    ro_ref[...] = (wide(r_ref) + p_ref[first].astype(F32)).astype(BF16)
    lo_ref[...] = (wide(l_ref) + p_ref[first + 1].astype(F32)).astype(BF16)


def last_turn_kernel(r_ref, l_ref, p_ref, _, o_ref):
    o_ref[...] = (p_ref[p_ref.shape[0] - 1].astype(F32) + wide(r_ref) + wide(l_ref)).astype(BF16)


def key_grad_kernel(v_ref, kp_ref, state_ref, _, kg_ref):
    for c in heads_of(v_ref):
        kg_ref[:, c] = (kp_ref[:, c] + dot(v_ref[:, c], state_ref[c, :], NT)).astype(BF16)


def weight_grad_kernel(scale, side, core, vg_ref, x_ref, _, o_ref):
    turned = vg_ref[...].T
    shift = core[0] * 128 if side == 0 else (1 - core[0]) * 128
    for first in range(0, o_ref.shape[0], 4):
        x = jnp.concatenate(
            [
                x_ref[:, pl.ds(pl.multiple_of(p * 256 + shift, 128), 128)]
                for p in range(first, first + 4)
            ],
            axis=1,
        )
        res = (dot(turned, x) * scale).astype(BF16)
        for p in range(4):
            o_ref[first + p] = res[:, p * 128 : p * 128 + 128]


def chip_kernel(where, a_ref, b_ref, _, ru2, lv2, rv1, lu1, cu1, cv1, own):
    half = own.shape[1] // 2

    def s(i):
        return (a_ref[where[i]].astype(F32) + b_ref[where[i]].astype(F32)).astype(BF16)

    t = s(0)
    ru2[...] = t[:, :half]
    lv2[...] = t[:, half:]
    t = s(1)
    cu1[...] = t[:, :half]
    rv1[...] = t[:, half:]
    t = s(2)
    lu1[...] = t[:, :half]
    cv1[...] = t[:, half:]
    own[...] = s(3)


def pair_kernel(a_ref, b_ref, c_ref, d_ref, _, o_ref, p_ref):
    o_ref[...] = (wide(a_ref) + wide(b_ref)).astype(BF16)
    p_ref[...] = (wide(c_ref) + wide(d_ref)).astype(BF16)


def line_kernel(where, own_ref, ru_ref, lu_ref, rv_ref, lv_ref, _, m1, m2, m3, keep):
    half = ru_ref.shape[1]
    for s, ref in enumerate((m1, m2, m3, keep)):
        i = where[4 + s]
        own = own_ref[i].astype(F32)
        u = own[:half] + ru_ref[i].astype(F32) + lu_ref[i].astype(F32)
        v = own[half:] + rv_ref[i].astype(F32) + lv_ref[i].astype(F32)
        ref[:half] = u.astype(ref.dtype)
        ref[half:] = v.astype(ref.dtype)


def owner_kernel(keep_ref, a_ref, b_ref, c_ref, o_ref):
    o_ref[...] = (keep_ref[...] + wide(a_ref) + wide(b_ref) + wide(c_ref)).T


def local(layer_input, query_act, key_act, out_grad, value_weight):
    tok, width = layer_input.shape
    rows, cols = value_weight.shape
    core = lax.axis_index("fsdp")
    place = lax.axis_index("ctx")
    group = lax.axis_index("head")
    x, y = place // SIDE, lax.rem(place, SIDE)
    core_arr = core.reshape(1).astype(jnp.int32)
    hops = jnp.arange(1, 4, dtype=jnp.int32)
    onward = (y + hops < SIDE).astype(jnp.int32)
    back = (y - hops >= 0).astype(jnp.int32)
    dests = jnp.concatenate(
        [lax.rem(group + jnp.array([4, 3, 5, 2, 6, 1, 7, 0], jnp.int32), RING), core_arr]
    )
    where = jnp.concatenate(
        [
            lax.rem(x + jnp.array([2, 1, 3, 0], jnp.int32), SIDE),
            lax.rem(y + jnp.array([1, 2, 3, 0], jnp.int32), SIDE),
        ]
    )
    square = sds((tok, cols))
    square_f32 = sds((tok, cols), F32)
    states = sds((cols, HDIM))

    w_other = swap(value_weight)
    x_near, w_own, part = call(
        value_own_kernel,
        [SMEM, HBM, HBM],
        [core_arr, layer_input, value_weight],
        [sds((tok, width)), sds((rows, cols)), square_f32],
        "value_own",
        scratch=[pltpu.SemaphoreType.DMA((width // 512 + rows // 512,))],
    )
    value, pair = call(
        value_rest_kernel,
        [SMEM] + [VMEM] * 4,
        [core_arr, x_near, w_other, part, key_act],
        [square, states],
        "value_rest",
    )
    near, far, (attended,) = exclusive(
        pair,
        onward,
        1 - core_arr,
        1,
        lambda: call(
            inside_kernel, [VMEM] * 3, [query_act, key_act, value], [square_f32], "inside"
        ),
    )
    low, state, own_grad = call(
        norm_kernel,
        [VMEM] * 5,
        [query_act, out_grad, attended, near, far],
        [square, states, states],
        "norm_grad",
    )
    near, far, (query_grad, key_part, value_part) = exclusive(
        own_grad,
        back,
        core_arr,
        -1,
        lambda: call(
            cross_kernel,
            [VMEM] * 5,
            [query_act, key_act, value, low, state],
            [square, square_f32, square_f32],
            "cross",
        ),
    )

    half = sds((tok // 2, 512))
    full = sds((tok, 512))
    value_grad, state_grad, r, l = call(
        first_kernel,
        [SMEM] + [VMEM] * 6,
        [dests, key_act, value_part, near, far, w_own, w_other],
        [square, states, half, half],
        "value_grad",
    )
    r, l = along_z(r, 1), along_z(l, -1)

    def chunks(first, count, after):
        return call(
            lambda *refs: chunks_kernel(first, *refs),
            [SMEM] + [VMEM] * 3 + [ANY],
            [dests, value_grad, w_own, w_other, after],
            [sds((count, tok, 512))],
            "chunks",
        )[0]

    def weight_part(side, after):
        return call(
            lambda *refs: weight_grad_kernel(scale, side, *refs),
            [SMEM] + [VMEM] * 2 + [ANY],
            [core_arr, value_grad, x_near, after],
            [sds((width // 256, cols, 128))],
            "weight_grad",
        )[0]

    scale = 1.0 / math.sqrt(tok * lax.axis_size(("ctx", "fsdp")))
    threes = chunks(1, 2, state_grad)
    other = weight_part(1, threes)
    got = swap(other)
    mine = weight_part(0, other)
    r, l = call(open_turn_kernel, [VMEM] * 3 + [ANY], [r, l, threes, mine], [full] * 2, "turn")
    r, l = along_z(r, 1), along_z(l, -1)

    square4 = (SIDE, SIDE) + mine.shape[1:]
    piece = sds((SIDE, cols // 2, 128))
    ru2, lv2, rv1, lu1, cu1, cv1, own = call(
        chip_kernel,
        [SMEM] + [VMEM] * 2 + [ANY],
        [where, mine.reshape(square4), got.reshape(square4), r],
        [piece] * 6 + [sds((SIDE, cols, 128))],
        "chip",
    )
    ru2, lv2 = along_x_ring(ru2, 1), along_x_ring(lv2, -1)
    rv1, lu1 = along_x_ring(rv1, 1), along_x_ring(lu1, -1)
    rest = chunks(3, 5, own)

    def turn(first, r, l, after):
        r, l = call(
            lambda *refs: turn_kernel(first, *refs),
            [VMEM] * 3 + [ANY],
            [r, l, rest, after],
            [full] * 2,
            "turn",
        )
        return r, along_z(r, 1), along_z(l, -1)

    sent, r, l = turn(0, r, l, own)
    (key_grad,) = call(
        key_grad_kernel,
        [VMEM] * 3 + [ANY],
        [value, key_part, state_grad, sent],
        [square],
        "key_grad",
    )
    ru1, lv1 = call(
        pair_kernel,
        [VMEM] * 4 + [ANY],
        [cu1, ru2, cv1, lv2, key_grad],
        [piece] * 2,
        "pair",
    )
    after = ru1
    ru1, lv1 = along_x_ring(ru1, 1), along_x_ring(lv1, -1)
    sent, r, l = turn(2, r, l, after)
    m1, m2, m3, keep = call(
        line_kernel,
        [SMEM] + [VMEM] * 5 + [ANY],
        [where, own, ru1, lu1, rv1, lv1, sent],
        [sds((cols, 128))] * 3 + [sds((cols, 128), F32)],
        "line",
    )
    got = [along_y_ring(m, k) for m, k in zip((m1, m2, m3), (1, 2, 3))]
    (input_grad,) = call(
        last_turn_kernel, [VMEM] * 3 + [ANY], [r, l, rest, keep], [full], "last_turn"
    )
    (weight_grad,) = call(
        owner_kernel, [VMEM] * 4, [keep, *got], [sds((128, cols), F32)], "owner"
    )
    return (query_grad, key_grad, input_grad, weight_grad)


def solution(mesh):
    in_specs = (
        P(("ctx", "fsdp"), None),
        P(("ctx", "fsdp"), "head"),
        P(("ctx", "fsdp"), "head"),
        P(("ctx", "fsdp"), "head"),
        P("fsdp", "head"),
    )
    out_specs = (
        P(("ctx", "fsdp"), "head"),
        P(("ctx", "fsdp"), "head"),
        P(("ctx", "fsdp"), "head"),
        P(("ctx", "fsdp"), "head"),
    )
    return jax.shard_map(local, mesh=mesh, in_specs=in_specs, out_specs=out_specs, check_vma=False)
```

```python
import math

import jax
import jax.numpy as jnp
from jax import lax
from jax.experimental import pallas as pl
from jax.experimental.pallas import tpu as pltpu
from jax.sharding import PartitionSpec as P

HDIM = 128
SIDE = 4
RING = 8
F32 = jnp.float32
BF16 = jnp.bfloat16
NT = (((1,), (1,)), ((), ()))
TN = (((0,), (0,)), ((), ()))
NN = (((1,), (0,)), ((), ()))

VMEM = pl.BlockSpec(memory_space=pltpu.VMEM)
SMEM = pl.BlockSpec(memory_space=pltpu.SMEM)
ANY = pl.BlockSpec(memory_space=pl.ANY)
HBM = pl.BlockSpec(memory_space=pltpu.HBM)


def dot(a, b, dims=NN):
    return lax.dot_general(a, b, dims, preferred_element_type=F32)


def sds(shape, dtype=BF16):
    return jax.ShapeDtypeStruct(shape, dtype)


def hbm_like(a):
    return pltpu.HBM(a.shape, a.dtype)


def wide(ref):
    return ref[...].astype(F32)


def call(body, specs, ins, outs, name, scratch=(), limit=16):
    return pl.pallas_call(
        body,
        out_shape=tuple(outs),
        in_specs=specs,
        out_specs=tuple(VMEM if isinstance(o, jax.ShapeDtypeStruct) else HBM for o in outs),
        scratch_shapes=list(scratch),
        compiler_params=pltpu.CompilerParams(vmem_limit_bytes=limit * 2**20),
        cost_estimate=pl.CostEstimate(
            flops=1000,
            bytes_accessed=sum(a.size * a.dtype.itemsize for a in ins)
            + sum(math.prod(o.shape) * o.dtype.itemsize for o in outs),
            transcendentals=0,
        ),
        name=name,
    )(*ins)


def in_hbm(a):
    return pltpu.with_memory_space_constraint(a, pltpu.HBM)


def heads_of(ref):
    return [slice(h, h + HDIM) for h in range(0, ref.shape[1], HDIM)]


def tril(scores):
    rows = lax.broadcasted_iota(jnp.int32, scores.shape, 0)
    cols = lax.broadcasted_iota(jnp.int32, scores.shape, 1)
    return jnp.where(rows >= cols, scores, 0.0).astype(BF16)


def value_own_kernel(core, x_hbm, w_hbm, x_ref, part_ref, w_ref, sems):
    step = 512
    n = x_hbm.shape[1] // step
    half = n // 2

    def x_cols(j):
        return pl.ds(pl.multiple_of(lax.rem(core[0] * half + j, n) * step, step), step)

    xs = [
        pltpu.make_async_copy(x_hbm.at[:, x_cols(j)], x_ref.at[:, x_cols(j)], sems.at[j])
        for j in range(n)
    ]
    ws = [
        pltpu.make_async_copy(
            w_hbm.at[pl.ds(j * step, step), :], w_ref.at[pl.ds(j * step, step), :], sems.at[n + j]
        )
        for j in range(half)
    ]
    for j in range(half):
        ws[j].start()
        xs[j].start()
    for j in range(half, n):
        xs[j].start()
    for j in range(half):
        ws[j].wait()
        xs[j].wait()
        prod = dot(x_ref[:, x_cols(j)], w_ref[j * step : (j + 1) * step, :])
        if j == 0:
            part_ref[...] = prod
        else:
            part_ref[...] += prod
    for j in range(half, n):
        xs[j].wait()


def value_rest_kernel(core, x_ref, w_ref, part_ref, k_ref, v_ref, pair_ref, w_out, sem):
    copy = pltpu.make_async_copy(w_ref, w_out, sem)
    copy.start()
    rows = w_ref.shape[0]
    cols = pl.ds(pl.multiple_of((1 - core[0]) * rows, rows), rows)
    v = (part_ref[...] + dot(x_ref[:, cols], w_ref[...])).astype(BF16)
    v_ref[...] = v
    for c in heads_of(v_ref):
        pair_ref[c, :] = dot(k_ref[:, c], v[:, c], TN).astype(BF16)
    copy.wait()


def inside_kernel(q_ref, k_ref, v_ref, a_ref, v_out, sem):
    copy = pltpu.make_async_copy(v_ref, v_out, sem)
    copy.start()
    for c in heads_of(q_ref):
        a_ref[:, c] = dot(tril(dot(q_ref[:, c], k_ref[:, c], NT)), v_ref[:, c])
    copy.wait()


def norm_kernel(q_ref, g_ref, a_ref, near_ref, far_ref, low_ref, state_ref, local_ref):
    for c in heads_of(q_ref):
        state = (near_ref[c, :] + far_ref[c, :].astype(F32)).astype(BF16)
        state_ref[c, :] = state
        att = a_ref[:, c] + dot(q_ref[:, c], state)
        inv = lax.rsqrt(jnp.mean(att * att, axis=-1, keepdims=True) + 1e-05)
        normed = att * inv
        g = g_ref[:, c].astype(F32)
        low = (inv * (g - normed * jnp.mean(g * normed, axis=-1, keepdims=True))).astype(BF16)
        low_ref[:, c] = low
        local_ref[c, :] = dot(q_ref[:, c], low, TN).astype(BF16)


def cross_kernel(q_ref, k_ref, v_ref, low_ref, state_ref, vp_ref, kp_ref, qg_ref):
    for c in heads_of(q_ref):
        q, k, low = q_ref[:, c], k_ref[:, c], low_ref[:, c]
        cross = tril(dot(low, v_ref[:, c], NT))
        qg_ref[:, c] = (dot(cross, k) + dot(low, state_ref[c, :], NT)).astype(BF16)
        kp_ref[:, c] = dot(cross, q, TN)
        vp_ref[:, c] = dot(tril(dot(q, k, NT)), low, TN)


def fold_x_kernel(keep, mine_ref, a_ref, b_ref, c_ref, _, before_ref, *msgs):
    before = wide(a_ref) + wide(b_ref) + wide(c_ref)
    before_ref[...] = before
    both = (before + wide(mine_ref)).astype(BF16)
    alone = before.astype(BF16)
    for i, ref in enumerate(msgs):
        ref[...] = jnp.where(keep[i] > 0, both, alone)


def fold_y_kernel(ahead, mine_ref, before_ref, a_ref, b_ref, c_ref, _, near_ref, far_ref):
    near = before_ref[...] + (wide(a_ref) + wide(b_ref) + wide(c_ref))
    near_ref[...] = near
    far_ref[...] = jnp.where(ahead[0] > 0, near + wide(mine_ref), near).astype(BF16)


def along_x(a, k):
    return lax.ppermute(
        a, "ctx", [(i, i + SIDE * k) for i in range(16) if 0 <= i + SIDE * k < 16]
    )


def along_x_ring(a, k):
    return lax.ppermute(a, "ctx", [(i, (i + SIDE * k) % 16) for i in range(16)])


def along_y_ring(a, k):
    return lax.ppermute(
        a, "ctx", [(i, i // SIDE * SIDE + (i + k) % SIDE) for i in range(16)]
    )


def along_z(a, k):
    return lax.ppermute(a, "head", [(i, (i + k) % RING) for i in range(RING)])


def swap(a):
    return lax.ppermute(a, "fsdp", [(0, 1), (1, 0)])


def exclusive(mine, keep, ahead, sign, work):
    shape = mine.shape
    got = [along_x(mine, sign * k) for k in (1, 2, 3)]
    done = work()
    before, *msgs = call(
        fold_x_kernel,
        [SMEM] + [VMEM] * 5,
        [keep, mine, *got, done[0]],
        [sds(shape, F32)] + [sds(shape)] * 3,
        "fold_x",
    )
    got = [along_y_ring(m, sign * k) for m, k in zip(msgs, (1, 2, 3))]
    near, far = call(
        fold_y_kernel,
        [SMEM] + [VMEM] * 6,
        [ahead, mine, before, *got, done[0]],
        [sds(shape, F32), sds(shape)],
        "fold_y",
    )
    return near, swap(far), done


def chunk_product(dests, which, vg, own_ref, other_ref, use):
    dest = dests[which]
    rows = pl.ds(pl.multiple_of(lax.rem(dest, RING // 2) * 512, 512), 512)
    mine = dest // (RING // 2) == dests[RING]

    @pl.when(mine)
    def _():
        use(dot(vg, own_ref[rows, :], NT).astype(BF16))

    @pl.when(jnp.logical_not(mine))
    def _():
        use(dot(vg, other_ref[rows, :], NT).astype(BF16))


def first_kernel(scale, dests, k_ref, vp_ref, near_ref, far_ref, own_ref, other_ref, x_ref, vg_ref, state_ref, right_ref, left_ref, piece_ref):
    for c in heads_of(k_ref):
        state = (near_ref[c, :] + far_ref[c, :].astype(F32)).astype(BF16)
        state_ref[c, :] = state
        vg_ref[:, c] = (vp_ref[:, c] + dot(k_ref[:, c], state)).astype(BF16)
    half = right_ref.shape[0]

    def use(p):
        right_ref[...] = p[:half]
        left_ref[...] = p[half:]

    chunk_product(dests, 0, vg_ref[...], own_ref, other_ref, use)
    weight_pieces(scale, 1 - dests[RING], vg_ref, x_ref, piece_ref)


def work_kernel(scale, dests, vg_ref, own_ref, other_ref, x_ref, p_ref, piece_ref):
    for i in range(p_ref.shape[0]):

        def use(p):
            p_ref[i] = p

        chunk_product(dests, 1 + i, vg_ref[...], own_ref, other_ref, use)
    weight_pieces(scale, dests[RING], vg_ref, x_ref, piece_ref)


def open_turn_kernel(r_ref, l_ref, p_ref, ro_ref, lo_ref):
    half = r_ref.shape[0]
    ro_ref[:half] = (wide(r_ref) + p_ref[0, :half].astype(F32)).astype(BF16)
    ro_ref[half:] = p_ref[0, half:]
    lo_ref[:half] = p_ref[1, :half]
    lo_ref[half:] = (wide(l_ref) + p_ref[1, half:].astype(F32)).astype(BF16)


def turn(first, r_ref, l_ref, p_ref, ro_ref, lo_ref):
    ro_ref[...] = (wide(r_ref) + p_ref[first].astype(F32)).astype(BF16)
    lo_ref[...] = (wide(l_ref) + p_ref[first + 1].astype(F32)).astype(BF16)


def last_turn_kernel(r_ref, l_ref, p_ref, o_ref):
    o_ref[...] = (p_ref[p_ref.shape[0] - 1].astype(F32) + wide(r_ref) + wide(l_ref)).astype(BF16)


def key_grad_kernel(v_ref, kp_ref, state_ref, _, kg_ref):
    for c in heads_of(v_ref):
        kg_ref[:, c] = (kp_ref[:, c] + dot(v_ref[:, c], state_ref[c, :], NT)).astype(BF16)


def weight_pieces(scale, side, vg_ref, x_ref, o_ref):
    turned = vg_ref[...].T
    shift = side * 128
    for first in range(0, o_ref.shape[0], 4):
        x = jnp.concatenate(
            [
                x_ref[:, pl.ds(pl.multiple_of(p * 256 + shift, 128), 128)]
                for p in range(first, first + 4)
            ],
            axis=1,
        )
        res = (dot(turned, x) * scale).astype(BF16)
        for p in range(4):
            o_ref[first + p] = res[:, p * 128 : p * 128 + 128]


def chip_kernel(where, a_ref, b_ref, _, ru2, lv2, rv1, lu1, cu1, cv1, own):
    half = own.shape[1] // 2

    def s(i):
        return (a_ref[where[i]].astype(F32) + b_ref[where[i]].astype(F32)).astype(BF16)

    t = s(0)
    ru2[...] = t[:, :half]
    lv2[...] = t[:, half:]
    t = s(1)
    cu1[...] = t[:, :half]
    rv1[...] = t[:, half:]
    t = s(2)
    lu1[...] = t[:, :half]
    cv1[...] = t[:, half:]
    own[...] = s(3)


def pair_kernel(r_ref, l_ref, p_ref, a_ref, b_ref, c_ref, d_ref, _, ro_ref, lo_ref, o_ref, q_ref):
    turn(2, r_ref, l_ref, p_ref, ro_ref, lo_ref)
    o_ref[...] = (wide(a_ref) + wide(b_ref)).astype(BF16)
    q_ref[...] = (wide(c_ref) + wide(d_ref)).astype(BF16)


def line_kernel(where, r_ref, l_ref, p_ref, own_ref, ru_ref, lu_ref, rv_ref, lv_ref, ro_ref, lo_ref, m1, m2, m3, keep):
    turn(4, r_ref, l_ref, p_ref, ro_ref, lo_ref)
    half = ru_ref.shape[1]
    for s, ref in enumerate((m1, m2, m3, keep)):
        i = where[4 + s]
        own = own_ref[i].astype(F32)
        u = own[:half] + ru_ref[i].astype(F32) + lu_ref[i].astype(F32)
        v = own[half:] + rv_ref[i].astype(F32) + lv_ref[i].astype(F32)
        ref[:half] = u.astype(ref.dtype)
        ref[half:] = v.astype(ref.dtype)


def owner_kernel(keep_ref, a_ref, b_ref, c_ref, o_ref):
    o_ref[...] = (keep_ref[...] + wide(a_ref) + wide(b_ref) + wide(c_ref)).T


def local(layer_input, query_act, key_act, out_grad, value_weight):
    tok, width = layer_input.shape
    rows, cols = value_weight.shape
    core = lax.axis_index("fsdp")
    place = lax.axis_index("ctx")
    group = lax.axis_index("head")
    x, y = place // SIDE, lax.rem(place, SIDE)
    core_arr = core.reshape(1).astype(jnp.int32)
    hops = jnp.arange(1, 4, dtype=jnp.int32)
    onward = (y + hops < SIDE).astype(jnp.int32)
    back = (y - hops >= 0).astype(jnp.int32)
    dests = jnp.concatenate(
        [lax.rem(group + jnp.array([4, 3, 5, 2, 6, 1, 7, 0], jnp.int32), RING), core_arr]
    )
    where = jnp.concatenate(
        [
            lax.rem(x + jnp.array([2, 1, 3, 0], jnp.int32), SIDE),
            lax.rem(y + jnp.array([1, 2, 3, 0], jnp.int32), SIDE),
        ]
    )
    square = sds((tok, cols))
    square_f32 = sds((tok, cols), F32)
    states = sds((cols, HDIM))

    w_other = swap(value_weight)
    x_near, part = call(
        value_own_kernel,
        [SMEM, HBM, HBM],
        [core_arr, in_hbm(layer_input), in_hbm(value_weight)],
        [sds((tok, width)), square_f32],
        "value_own",
        scratch=[pltpu.VMEM((rows, cols), BF16), pltpu.SemaphoreType.DMA((width // 512 + rows // 512,))],
    )
    value, pair, w_other = call(
        value_rest_kernel,
        [SMEM] + [VMEM] * 4,
        [core_arr, x_near, w_other, part, key_act],
        [square, states, hbm_like(w_other)],
        "value_rest",
        scratch=[pltpu.SemaphoreType.DMA],
    )
    near, far, (attended, value) = exclusive(
        pair,
        onward,
        1 - core_arr,
        1,
        lambda: call(
            inside_kernel,
            [VMEM] * 3,
            [query_act, key_act, value],
            [square_f32, hbm_like(value)],
            "inside",
            scratch=[pltpu.SemaphoreType.DMA],
        ),
    )
    low, state, own_grad = call(
        norm_kernel,
        [VMEM] * 5,
        [query_act, out_grad, attended, near, far],
        [square, states, states],
        "norm_grad",
    )
    near, far, (value_part, key_part, query_grad) = exclusive(
        own_grad,
        back,
        core_arr,
        -1,
        lambda: call(
            cross_kernel,
            [VMEM] * 5,
            [query_act, key_act, value, low, state],
            [square_f32, square_f32, square],
            "cross",
        ),
    )

    scale = 1.0 / math.sqrt(tok * lax.axis_size(("ctx", "fsdp")))
    half = sds((tok // 2, 512))
    full = sds((tok, 512))
    pieces = sds((width // 256, cols, 128))
    value_grad, state_grad, r, l, other = call(
        lambda *refs: first_kernel(scale, *refs),
        [SMEM] + [VMEM] * 7,
        [dests, key_act, value_part, near, far, value_weight, w_other, layer_input],
        [square, states, half, half, pieces],
        "value_grad",
    )
    r, l = along_z(r, 1), along_z(l, -1)
    got = swap(other)
    parts, mine = call(
        lambda *refs: work_kernel(scale, *refs),
        [SMEM] + [VMEM] * 4,
        [dests, value_grad, value_weight, w_other, layer_input],
        [sds((RING - 1, tok, 512)), pieces],
        "work",
    )
    r, l = call(open_turn_kernel, [VMEM] * 3, [r, l, parts], [full] * 2, "turn")
    after = r
    r, l = along_z(r, 1), along_z(l, -1)

    square4 = (SIDE, SIDE) + mine.shape[1:]
    piece = sds((SIDE, cols // 2, 128))
    ru2, lv2, rv1, lu1, cu1, cv1, own = call(
        chip_kernel,
        [SMEM] + [VMEM] * 2 + [ANY],
        [where, mine.reshape(square4), got.reshape(square4), after],
        [piece] * 6 + [sds((SIDE, cols, 128))],
        "chip",
    )
    ru2, lv2 = along_x_ring(ru2, 1), along_x_ring(lv2, -1)
    rv1, lu1 = along_x_ring(rv1, 1), along_x_ring(lu1, -1)
    (key_grad,) = call(
        key_grad_kernel,
        [VMEM] * 3 + [ANY],
        [value, key_part, state_grad, own],
        [square],
        "key_grad",
    )
    r, l, ru1, lv1 = call(
        pair_kernel,
        [VMEM] * 7 + [HBM],
        [r, l, parts, cu1, ru2, cv1, lv2, in_hbm(key_grad)],
        [full] * 2 + [piece] * 2,
        "pair",
    )
    r, l = along_z(r, 1), along_z(l, -1)
    ru1, lv1 = along_x_ring(ru1, 1), along_x_ring(lv1, -1)
    r, l, m1, m2, m3, keep = call(
        line_kernel,
        [SMEM] + [VMEM] * 8,
        [where, r, l, parts, own, ru1, lu1, rv1, lv1],
        [full] * 2 + [sds((cols, 128))] * 3 + [sds((cols, 128), F32)],
        "line",
    )
    r, l = along_z(r, 1), along_z(l, -1)
    got = [along_y_ring(m, k) for m, k in zip((m1, m2, m3), (1, 2, 3))]
    (weight_grad,) = call(
        owner_kernel, [VMEM] * 4, [keep, *got], [sds((128, cols), F32)], "owner"
    )
    (input_grad,) = call(last_turn_kernel, [VMEM] * 3, [r, l, parts], [full], "last_turn")
    return (query_grad, key_grad, input_grad, weight_grad)


def solution(mesh):
    in_specs = (
        P(("ctx", "fsdp"), None),
        P(("ctx", "fsdp"), "head"),
        P(("ctx", "fsdp"), "head"),
        P(("ctx", "fsdp"), "head"),
        P("fsdp", "head"),
    )
    out_specs = (
        P(("ctx", "fsdp"), "head"),
        P(("ctx", "fsdp"), "head"),
        P(("ctx", "fsdp"), "head"),
        P(("ctx", "fsdp"), "head"),
    )
    return jax.shard_map(local, mesh=mesh, in_specs=in_specs, out_specs=out_specs, check_vma=False)
```

```python
import math

import jax
import jax.numpy as jnp
from jax import lax
from jax.experimental import pallas as pl
from jax.experimental.pallas import tpu as pltpu
from jax.sharding import PartitionSpec as P

HDIM = 128
SIDE = 4
RING = 8
F32 = jnp.float32
BF16 = jnp.bfloat16
NT = (((1,), (1,)), ((), ()))
TN = (((0,), (0,)), ((), ()))
NN = (((1,), (0,)), ((), ()))

VMEM = pl.BlockSpec(memory_space=pltpu.VMEM)
ANY = pl.BlockSpec(memory_space=pl.ANY)
HBM = pl.BlockSpec(memory_space=pltpu.HBM)


def dot(a, b, dims=NN):
    return lax.dot_general(a, b, dims, preferred_element_type=F32)


def sds(shape, dtype=BF16):
    return jax.ShapeDtypeStruct(shape, dtype)


def core():
    return lax.axis_index("fsdp")


def place():
    at = lax.axis_index("ctx")
    return at // SIDE, lax.rem(at, SIDE)


def dest(which):
    hop = (4, 3, 5, 2, 6, 1, 7, 0)[which]
    return lax.rem(lax.axis_index("head") + hop, RING)


def wide(ref):
    return ref[...].astype(F32)


def call(body, specs, ins, outs, name, scratch=(), limit=16):
    return pl.pallas_call(
        body,
        out_shape=tuple(outs),
        in_specs=specs,
        out_specs=tuple([VMEM] * len(outs)),
        scratch_shapes=list(scratch),
        compiler_params=pltpu.CompilerParams(vmem_limit_bytes=limit * 2**20),
        cost_estimate=pl.CostEstimate(
            flops=1000,
            bytes_accessed=sum(a.size * a.dtype.itemsize for a in ins)
            + sum(math.prod(o.shape) * o.dtype.itemsize for o in outs),
            transcendentals=0,
        ),
        name=name,
    )(*ins)


def in_hbm(a):
    return pltpu.with_memory_space_constraint(a, pltpu.HBM)


def heads_of(ref):
    return [slice(h, h + HDIM) for h in range(0, ref.shape[1], HDIM)]


def tril(scores):
    rows = lax.broadcasted_iota(jnp.int32, scores.shape, 0)
    cols = lax.broadcasted_iota(jnp.int32, scores.shape, 1)
    return jnp.where(rows >= cols, scores, 0.0).astype(BF16)


def value_own_kernel(x_hbm, w_hbm, x_ref, part_ref, w_ref, sems):
    step = 512
    n = x_hbm.shape[1] // step
    half = n // 2

    def x_cols(j):
        return pl.ds(pl.multiple_of(lax.rem(core() * half + j, n) * step, step), step)

    xs = [
        pltpu.make_async_copy(x_hbm.at[:, x_cols(j)], x_ref.at[:, x_cols(j)], sems.at[j])
        for j in range(n)
    ]
    ws = [
        pltpu.make_async_copy(
            w_hbm.at[pl.ds(j * step, step), :], w_ref.at[pl.ds(j * step, step), :], sems.at[n + j]
        )
        for j in range(half)
    ]
    for j in range(half):
        ws[j].start()
        xs[j].start()
    for j in range(half, n):
        xs[j].start()
    for j in range(half):
        ws[j].wait()
        xs[j].wait()
        prod = dot(x_ref[:, x_cols(j)], w_ref[j * step : (j + 1) * step, :])
        if j == 0:
            part_ref[...] = prod
        else:
            part_ref[...] += prod
    for j in range(half, n):
        xs[j].wait()


def value_rest_kernel(x_ref, w_ref, part_ref, k_ref, v_ref, pair_ref):
    rows = w_ref.shape[0]
    cols = pl.ds(pl.multiple_of((1 - core()) * rows, rows), rows)
    v = (part_ref[...] + dot(x_ref[:, cols], w_ref[...])).astype(BF16)
    v_ref[...] = v
    for c in heads_of(v_ref):
        pair_ref[c, :] = dot(k_ref[:, c], v[:, c], TN).astype(BF16)


def inside_kernel(q_ref, k_ref, v_ref, a_ref):
    for c in heads_of(q_ref):
        a_ref[:, c] = dot(tril(dot(q_ref[:, c], k_ref[:, c], NT)), v_ref[:, c])


def norm_kernel(q_ref, g_ref, a_ref, near_ref, far_ref, low_ref, state_ref, local_ref):
    for c in heads_of(q_ref):
        state = (near_ref[c, :] + far_ref[c, :].astype(F32)).astype(BF16)
        state_ref[c, :] = state
        att = a_ref[:, c] + dot(q_ref[:, c], state)
        inv = lax.rsqrt(jnp.mean(att * att, axis=-1, keepdims=True) + 1e-05)
        normed = att * inv
        g = g_ref[:, c].astype(F32)
        low = (inv * (g - normed * jnp.mean(g * normed, axis=-1, keepdims=True))).astype(BF16)
        low_ref[:, c] = low
        local_ref[c, :] = dot(q_ref[:, c], low, TN).astype(BF16)


def cross_kernel(q_ref, k_ref, v_ref, low_ref, state_ref, vp_ref, kp_ref, qg_ref):
    for c in heads_of(q_ref):
        q, k, low = q_ref[:, c], k_ref[:, c], low_ref[:, c]
        cross = tril(dot(low, v_ref[:, c], NT))
        qg_ref[:, c] = (dot(cross, k) + dot(low, state_ref[c, :], NT)).astype(BF16)
        kp_ref[:, c] = dot(cross, q, TN)
        vp_ref[:, c] = dot(tril(dot(q, k, NT)), low, TN)


def fold_x_kernel(sign, mine_ref, a_ref, b_ref, c_ref, _, before_ref, *msgs):
    _, y = place()
    before = wide(a_ref) + wide(b_ref) + wide(c_ref)
    before_ref[...] = before
    both = (before + wide(mine_ref)).astype(BF16)
    alone = before.astype(BF16)
    for k, ref in enumerate(msgs, 1):
        onward = y + k < SIDE if sign == 1 else y - k >= 0
        ref[...] = jnp.where(onward, both, alone)


def fold_y_kernel(sign, mine_ref, before_ref, a_ref, b_ref, c_ref, _, near_ref, far_ref):
    near = before_ref[...] + (wide(a_ref) + wide(b_ref) + wide(c_ref))
    near_ref[...] = near
    ahead = core() == (0 if sign == 1 else 1)
    far_ref[...] = jnp.where(ahead, near + wide(mine_ref), near).astype(BF16)


def along_x(a, k):
    return lax.ppermute(
        a, "ctx", [(i, i + SIDE * k) for i in range(16) if 0 <= i + SIDE * k < 16]
    )


def along_x_ring(a, k):
    return lax.ppermute(a, "ctx", [(i, (i + SIDE * k) % 16) for i in range(16)])


def along_y_ring(a, k):
    return lax.ppermute(
        a, "ctx", [(i, i // SIDE * SIDE + (i + k) % SIDE) for i in range(16)]
    )


def along_z(a, k):
    return lax.ppermute(a, "head", [(i, (i + k) % RING) for i in range(RING)])


def swap(a):
    return lax.ppermute(a, "fsdp", [(0, 1), (1, 0)])


def exclusive(mine, sign, work):
    shape = mine.shape
    got = [along_x(mine, sign * k) for k in (1, 2, 3)]
    done = work()
    before, *msgs = call(
        lambda *refs: fold_x_kernel(sign, *refs),
        [VMEM] * 5,
        [mine, *got, done[0]],
        [sds(shape, F32)] + [sds(shape)] * 3,
        "fold_x",
    )
    got = [along_y_ring(m, sign * k) for m, k in zip(msgs, (1, 2, 3))]
    near, far = call(
        lambda *refs: fold_y_kernel(sign, *refs),
        [VMEM] * 6,
        [mine, before, *got, done[0]],
        [sds(shape, F32), sds(shape)],
        "fold_y",
    )
    return near, swap(far), done


def chunk_product(which, vg, own_ref, other_ref, use):
    rows = pl.ds(pl.multiple_of(lax.rem(dest(which), RING // 2) * 512, 512), 512)
    mine = dest(which) // (RING // 2) == core()

    @pl.when(mine)
    def _():
        use(dot(vg, own_ref[rows, :], NT).astype(BF16))

    @pl.when(jnp.logical_not(mine))
    def _():
        use(dot(vg, other_ref[rows, :], NT).astype(BF16))


def first_kernel(scale, k_ref, vp_ref, near_ref, far_ref, own_ref, other_ref, x_ref, vg_ref, state_ref, right_ref, left_ref, piece_ref):
    for c in heads_of(k_ref):
        state = (near_ref[c, :] + far_ref[c, :].astype(F32)).astype(BF16)
        state_ref[c, :] = state
        vg_ref[:, c] = (vp_ref[:, c] + dot(k_ref[:, c], state)).astype(BF16)
    half = right_ref.shape[0]

    def use(p):
        right_ref[...] = p[:half]
        left_ref[...] = p[half:]

    chunk_product(0, vg_ref[...], own_ref, other_ref, use)
    weight_pieces(scale, 1 - core(), vg_ref, x_ref, piece_ref)


def work_kernel(scale, vg_ref, own_ref, other_ref, x_ref, p_ref, piece_ref):
    for i in range(p_ref.shape[0]):

        def use(p):
            p_ref[i] = p

        chunk_product(1 + i, vg_ref[...], own_ref, other_ref, use)
    weight_pieces(scale, core(), vg_ref, x_ref, piece_ref)


def open_turn_kernel(r_ref, l_ref, p_ref, ro_ref, lo_ref):
    half = r_ref.shape[0]
    ro_ref[:half] = (wide(r_ref) + p_ref[0, :half].astype(F32)).astype(BF16)
    ro_ref[half:] = p_ref[0, half:]
    lo_ref[:half] = p_ref[1, :half]
    lo_ref[half:] = (wide(l_ref) + p_ref[1, half:].astype(F32)).astype(BF16)


def turn(first, r_ref, l_ref, p_ref, ro_ref, lo_ref):
    ro_ref[...] = (wide(r_ref) + p_ref[first].astype(F32)).astype(BF16)
    lo_ref[...] = (wide(l_ref) + p_ref[first + 1].astype(F32)).astype(BF16)


def last_turn_kernel(r_ref, l_ref, p_ref, o_ref):
    o_ref[...] = (p_ref[p_ref.shape[0] - 1].astype(F32) + wide(r_ref) + wide(l_ref)).astype(BF16)


def key_grad_kernel(v_ref, kp_ref, state_ref, _, kg_ref):
    for c in heads_of(v_ref):
        kg_ref[:, c] = (kp_ref[:, c] + dot(v_ref[:, c], state_ref[c, :], NT)).astype(BF16)


def weight_pieces(scale, side, vg_ref, x_ref, o_ref):
    turned = vg_ref[...].T
    shift = side * 128
    for first in range(0, o_ref.shape[0], 4):
        x = jnp.concatenate(
            [
                x_ref[:, pl.ds(pl.multiple_of(p * 256 + shift, 128), 128)]
                for p in range(first, first + 4)
            ],
            axis=1,
        )
        res = (dot(turned, x) * scale).astype(BF16)
        for p in range(4):
            o_ref[first + p] = res[:, p * 128 : p * 128 + 128]


def chip_kernel(a_ref, b_ref, _, ru2, lv2, rv1, lu1, cu1, cv1, own):
    half = own.shape[1] // 2

    x, _ = place()

    def s(hop):
        i = lax.rem(x + hop, SIDE)
        return (a_ref[i].astype(F32) + b_ref[i].astype(F32)).astype(BF16)

    t = s(2)
    ru2[...] = t[:, :half]
    lv2[...] = t[:, half:]
    t = s(1)
    cu1[...] = t[:, :half]
    rv1[...] = t[:, half:]
    t = s(3)
    lu1[...] = t[:, :half]
    cv1[...] = t[:, half:]
    own[...] = s(0)


def pair_kernel(r_ref, l_ref, p_ref, a_ref, b_ref, c_ref, d_ref, _, ro_ref, lo_ref, o_ref, q_ref):
    turn(2, r_ref, l_ref, p_ref, ro_ref, lo_ref)
    o_ref[...] = (wide(a_ref) + wide(b_ref)).astype(BF16)
    q_ref[...] = (wide(c_ref) + wide(d_ref)).astype(BF16)


def line_kernel(r_ref, l_ref, p_ref, own_ref, ru_ref, lu_ref, rv_ref, lv_ref, ro_ref, lo_ref, m1, m2, m3, keep):
    turn(4, r_ref, l_ref, p_ref, ro_ref, lo_ref)
    half = ru_ref.shape[1]
    _, y = place()
    for hop, ref in ((1, m1), (2, m2), (3, m3), (0, keep)):
        i = lax.rem(y + hop, SIDE)
        own = own_ref[i].astype(F32)
        u = own[:half] + ru_ref[i].astype(F32) + lu_ref[i].astype(F32)
        v = own[half:] + rv_ref[i].astype(F32) + lv_ref[i].astype(F32)
        ref[:half] = u.astype(ref.dtype)
        ref[half:] = v.astype(ref.dtype)


def owner_kernel(keep_ref, a_ref, b_ref, c_ref, o_ref):
    o_ref[...] = (keep_ref[...] + wide(a_ref) + wide(b_ref) + wide(c_ref)).T


def local(layer_input, query_act, key_act, out_grad, value_weight):
    tok, width = layer_input.shape
    rows, cols = value_weight.shape
    square = sds((tok, cols))
    square_f32 = sds((tok, cols), F32)
    states = sds((cols, HDIM))

    w_other = swap(value_weight)
    x_near, part = call(
        value_own_kernel,
        [HBM, HBM],
        [in_hbm(layer_input), in_hbm(value_weight)],
        [sds((tok, width)), square_f32],
        "value_own",
        scratch=[pltpu.VMEM((rows, cols), BF16), pltpu.SemaphoreType.DMA((width // 512 + rows // 512,))],
    )
    value, pair = call(
        value_rest_kernel,
        [VMEM] * 4,
        [x_near, w_other, part, key_act],
        [square, states],
        "value_rest",
    )
    near, far, (attended,) = exclusive(
        pair,
        1,
        lambda: call(
            inside_kernel,
            [VMEM] * 3,
            [query_act, key_act, value],
            [square_f32],
            "inside",
        ),
    )
    low, state, own_grad = call(
        norm_kernel,
        [VMEM] * 5,
        [query_act, out_grad, attended, near, far],
        [square, states, states],
        "norm_grad",
    )
    near, far, (value_part, key_part, query_grad) = exclusive(
        own_grad,
        -1,
        lambda: call(
            cross_kernel,
            [VMEM] * 5,
            [query_act, key_act, value, low, state],
            [square_f32, square_f32, square],
            "cross",
        ),
    )

    scale = 1.0 / math.sqrt(tok * lax.axis_size(("ctx", "fsdp")))
    half = sds((tok // 2, 512))
    full = sds((tok, 512))
    pieces = sds((width // 256, cols, 128))
    value_grad, state_grad, r, l, other = call(
        lambda *refs: first_kernel(scale, *refs),
        [VMEM] * 7,
        [key_act, value_part, near, far, value_weight, w_other, x_near],
        [square, states, half, half, pieces],
        "value_grad",
    )
    r, l = along_z(r, 1), along_z(l, -1)
    got = swap(other)
    parts, mine = call(
        lambda *refs: work_kernel(scale, *refs),
        [VMEM] * 4,
        [value_grad, value_weight, w_other, x_near],
        [sds((RING - 1, tok, 512)), pieces],
        "work",
    )
    r, l = call(open_turn_kernel, [VMEM] * 3, [r, l, parts], [full] * 2, "turn")
    after = r
    r, l = along_z(r, 1), along_z(l, -1)

    square4 = (SIDE, SIDE) + mine.shape[1:]
    piece = sds((SIDE, cols // 2, 128))
    ru2, lv2, rv1, lu1, cu1, cv1, own = call(
        chip_kernel,
        [VMEM] * 2 + [ANY],
        [mine.reshape(square4), got.reshape(square4), after],
        [piece] * 6 + [sds((SIDE, cols, 128))],
        "chip",
    )
    ru2, lv2 = along_x_ring(ru2, 1), along_x_ring(lv2, -1)
    rv1, lu1 = along_x_ring(rv1, 1), along_x_ring(lu1, -1)
    (key_grad,) = call(
        key_grad_kernel,
        [VMEM] * 3 + [ANY],
        [value, key_part, state_grad, own],
        [square],
        "key_grad",
    )
    r, l, ru1, lv1 = call(
        pair_kernel,
        [VMEM] * 7 + [HBM],
        [r, l, parts, cu1, ru2, cv1, lv2, in_hbm(key_grad)],
        [full] * 2 + [piece] * 2,
        "pair",
    )
    r, l = along_z(r, 1), along_z(l, -1)
    ru1, lv1 = along_x_ring(ru1, 1), along_x_ring(lv1, -1)
    r, l, m1, m2, m3, keep = call(
        line_kernel,
        [VMEM] * 8,
        [r, l, parts, own, ru1, lu1, rv1, lv1],
        [full] * 2 + [sds((cols, 128))] * 3 + [sds((cols, 128), F32)],
        "line",
    )
    r, l = along_z(r, 1), along_z(l, -1)
    got = [along_y_ring(m, k) for m, k in zip((m1, m2, m3), (1, 2, 3))]
    (weight_grad,) = call(
        owner_kernel, [VMEM] * 4, [keep, *got], [sds((128, cols), F32)], "owner"
    )
    (input_grad,) = call(last_turn_kernel, [VMEM] * 3, [r, l, parts], [full], "last_turn")
    return (query_grad, key_grad, input_grad, weight_grad)


def solution(mesh):
    in_specs = (
        P(("ctx", "fsdp"), None),
        P(("ctx", "fsdp"), "head"),
        P(("ctx", "fsdp"), "head"),
        P(("ctx", "fsdp"), "head"),
        P("fsdp", "head"),
    )
    out_specs = (
        P(("ctx", "fsdp"), "head"),
        P(("ctx", "fsdp"), "head"),
        P(("ctx", "fsdp"), "head"),
        P(("ctx", "fsdp"), "head"),
    )
    return jax.shard_map(local, mesh=mesh, in_specs=in_specs, out_specs=out_specs, check_vma=False)
```

```python
import math

import jax
import jax.numpy as jnp
from jax import lax
from jax.experimental import pallas as pl
from jax.experimental.pallas import tpu as pltpu
from jax.sharding import PartitionSpec as P

HDIM = 128
SIDE = 4
RING = 8
F32 = jnp.float32
BF16 = jnp.bfloat16
NT = (((1,), (1,)), ((), ()))
TN = (((0,), (0,)), ((), ()))
NN = (((1,), (0,)), ((), ()))

VMEM = pl.BlockSpec(memory_space=pltpu.VMEM)
ANY = pl.BlockSpec(memory_space=pl.ANY)
HBM = pl.BlockSpec(memory_space=pltpu.HBM)


def dot(a, b, dims=NN):
    return lax.dot_general(a, b, dims, preferred_element_type=F32)


def sds(shape, dtype=BF16):
    return jax.ShapeDtypeStruct(shape, dtype)


def core():
    return lax.axis_index("fsdp")


def place():
    at = lax.axis_index("ctx")
    return at // SIDE, lax.rem(at, SIDE)


def dest(which):
    hop = (4, 3, 5, 2, 6, 1, 7, 0)[which]
    return lax.rem(lax.axis_index("head") + hop, RING)


def wide(ref):
    return ref[...].astype(F32)


def call(body, specs, ins, outs, name, scratch=(), limit=16):
    return pl.pallas_call(
        body,
        out_shape=tuple(outs),
        in_specs=specs,
        out_specs=tuple([VMEM] * len(outs)),
        scratch_shapes=list(scratch),
        compiler_params=pltpu.CompilerParams(vmem_limit_bytes=limit * 2**20),
        cost_estimate=pl.CostEstimate(
            flops=1000,
            bytes_accessed=sum(a.size * a.dtype.itemsize for a in ins)
            + sum(math.prod(o.shape) * o.dtype.itemsize for o in outs),
            transcendentals=0,
        ),
        name=name,
    )(*ins)


def in_hbm(a):
    return pltpu.with_memory_space_constraint(a, pltpu.HBM)


def heads_of(ref):
    return [slice(h, h + HDIM) for h in range(0, ref.shape[1], HDIM)]


def tril(scores):
    rows = lax.broadcasted_iota(jnp.int32, scores.shape, 0)
    cols = lax.broadcasted_iota(jnp.int32, scores.shape, 1)
    return jnp.where(rows >= cols, scores, 0.0).astype(BF16)


def value_own_kernel(x_hbm, w_hbm, x_ref, part_ref, w_ref, sems):
    step = 512
    n = x_hbm.shape[1] // step
    half = n // 2

    def x_cols(j):
        return pl.ds(pl.multiple_of(lax.rem(core() * half + j, n) * step, step), step)

    xs = [
        pltpu.make_async_copy(x_hbm.at[:, x_cols(j)], x_ref.at[:, x_cols(j)], sems.at[j])
        for j in range(n)
    ]
    ws = [
        pltpu.make_async_copy(
            w_hbm.at[pl.ds(j * step, step), :], w_ref.at[pl.ds(j * step, step), :], sems.at[n + j]
        )
        for j in range(half)
    ]
    for j in range(half):
        ws[j].start()
        xs[j].start()
    for j in range(half, n):
        xs[j].start()
    for j in range(half):
        ws[j].wait()
        xs[j].wait()
        prod = dot(x_ref[:, x_cols(j)], w_ref[j * step : (j + 1) * step, :])
        if j == 0:
            part_ref[...] = prod
        else:
            part_ref[...] += prod
    for j in range(half, n):
        xs[j].wait()


def split(rows, keep_ref, give_ref):
    half = keep_ref.shape[0]
    for h, state in enumerate(rows):
        to = (h * HDIM) // half

        @pl.when(core() == to)
        def _():
            keep_ref[h * HDIM - to * half : (h + 1) * HDIM - to * half, :] = state

        @pl.when(core() != to)
        def _():
            give_ref[h * HDIM - to * half : (h + 1) * HDIM - to * half, :] = state


def join(near_ref, far_ref, state_ref):
    half = near_ref.shape[0]
    mine = pl.ds(pl.multiple_of(core() * half, half), half)
    other = pl.ds(pl.multiple_of((1 - core()) * half, half), half)
    state_ref[mine, :] = near_ref[...].astype(BF16)
    state_ref[other, :] = far_ref[...]


def value_rest_kernel(x_ref, w_ref, part_ref, k_ref, v_ref, keep_ref, give_ref):
    rows = w_ref.shape[0]
    cols = pl.ds(pl.multiple_of((1 - core()) * rows, rows), rows)
    v = (part_ref[...] + dot(x_ref[:, cols], w_ref[...])).astype(BF16)
    v_ref[...] = v
    pairs = [dot(k_ref[:, c], v[:, c], TN).astype(BF16) for c in heads_of(v_ref)]
    split(pairs, keep_ref, give_ref)


def inside_kernel(q_ref, k_ref, v_ref, a_ref):
    for c in heads_of(q_ref):
        a_ref[:, c] = dot(tril(dot(q_ref[:, c], k_ref[:, c], NT)), v_ref[:, c])


def norm_kernel(q_ref, g_ref, a_ref, near_ref, far_ref, low_ref, state_ref, keep_ref, give_ref):
    join(near_ref, far_ref, state_ref)
    local = []
    for c in heads_of(q_ref):
        att = a_ref[:, c] + dot(q_ref[:, c], state_ref[c, :])
        inv = lax.rsqrt(jnp.mean(att * att, axis=-1, keepdims=True) + 1e-05)
        normed = att * inv
        g = g_ref[:, c].astype(F32)
        low = (inv * (g - normed * jnp.mean(g * normed, axis=-1, keepdims=True))).astype(BF16)
        low_ref[:, c] = low
        local.append(dot(q_ref[:, c], low, TN).astype(BF16))
    split(local, keep_ref, give_ref)


def cross_kernel(q_ref, k_ref, v_ref, low_ref, state_ref, vp_ref, kp_ref, qg_ref):
    for c in heads_of(q_ref):
        q, k, low = q_ref[:, c], k_ref[:, c], low_ref[:, c]
        cross = tril(dot(low, v_ref[:, c], NT))
        qg_ref[:, c] = (dot(cross, k) + dot(low, state_ref[c, :], NT)).astype(BF16)
        kp_ref[:, c] = dot(cross, q, TN)
        vp_ref[:, c] = dot(tril(dot(q, k, NT)), low, TN)


def chip_sum_kernel(keep_ref, got_ref, _, t_ref):
    t_ref[...] = (wide(keep_ref) + wide(got_ref)).astype(BF16)


def pair_sum_kernel(a_ref, b_ref, _, t_ref):
    t_ref[...] = (wide(a_ref) + wide(b_ref)).astype(BF16)


def part_before(sign, at, beside, across):
    if sign == -1:
        at = SIDE - 1 - at
    return jnp.where(at % 2 == 1, beside, 0.0) + jnp.where(at >= SIDE // 2, across, 0.0)


def last_sum_kernel(sign, keep_ref, got_ref, y1, y2, x1, x2, near_ref, far_ref):
    x, y = place()
    before = part_before(sign, y, wide(y1), wide(y2)) + part_before(sign, x, wide(x1), wide(x2))
    lead = core() == (0 if sign == 1 else 1)
    near_ref[...] = jnp.where(lead, before, before + wide(got_ref))
    far_ref[...] = jnp.where(lead, before + wide(keep_ref), before).astype(BF16)


def along(a, axis, beside):
    def other(i):
        x, y = i // SIDE, i % SIDE
        if axis == "x":
            x = x ^ 1 if beside else SIDE - 1 - x
        else:
            y = y ^ 1 if beside else SIDE - 1 - y
        return x * SIDE + y

    return lax.ppermute(a, "ctx", [(i, other(i)) for i in range(SIDE * SIDE)])


def along_x_ring(a, k):
    return lax.ppermute(a, "ctx", [(i, (i + SIDE * k) % 16) for i in range(16)])


def along_y_ring(a, k):
    return lax.ppermute(
        a, "ctx", [(i, i // SIDE * SIDE + (i + k) % SIDE) for i in range(16)]
    )


def along_z(a, k):
    return lax.ppermute(a, "head", [(i, (i + k) % RING) for i in range(RING)])


def swap(a):
    return lax.ppermute(a, "fsdp", [(0, 1), (1, 0)])


def exclusive(keep, give, sign, work):
    shape = sds(keep.shape)

    def fold(kernel, *arrays):
        (t,) = call(kernel, [VMEM] * len(arrays), arrays, [shape], "fold")
        return t

    got = swap(give)
    t = fold(chip_sum_kernel, keep, got, keep)
    y1 = along(t, "y", True)
    done = work()
    t = fold(pair_sum_kernel, t, y1, done[0])
    y2 = along(t, "y", False)
    t = fold(pair_sum_kernel, t, y2, done[0])
    x1 = along(t, "x", True)
    t = fold(pair_sum_kernel, t, x1, done[0])
    x2 = along(t, "x", False)
    near, far = call(
        lambda *refs: last_sum_kernel(sign, *refs),
        [VMEM] * 6,
        [keep, got, y1, y2, x1, x2],
        [sds(keep.shape, F32), shape],
        "last_sum",
    )
    return near, swap(far), done


def chunk_product(which, vg, own_ref, other_ref, use):
    rows = pl.ds(pl.multiple_of(lax.rem(dest(which), RING // 2) * 512, 512), 512)
    mine = dest(which) // (RING // 2) == core()

    @pl.when(mine)
    def _():
        use(dot(vg, own_ref[rows, :], NT).astype(BF16))

    @pl.when(jnp.logical_not(mine))
    def _():
        use(dot(vg, other_ref[rows, :], NT).astype(BF16))


def first_kernel(scale, k_ref, vp_ref, near_ref, far_ref, own_ref, other_ref, x_ref, vg_ref, state_ref, right_ref, left_ref, piece_ref):
    join(near_ref, far_ref, state_ref)
    for c in heads_of(k_ref):
        vg_ref[:, c] = (vp_ref[:, c] + dot(k_ref[:, c], state_ref[c, :])).astype(BF16)
    half = right_ref.shape[0]

    def use(p):
        right_ref[...] = p[:half]
        left_ref[...] = p[half:]

    chunk_product(0, vg_ref[...], own_ref, other_ref, use)
    weight_pieces(scale, 1 - core(), vg_ref, x_ref, piece_ref)


def work_kernel(scale, vg_ref, own_ref, other_ref, x_ref, p_ref, piece_ref):
    for i in range(p_ref.shape[0]):

        def use(p):
            p_ref[i] = p

        chunk_product(1 + i, vg_ref[...], own_ref, other_ref, use)
    weight_pieces(scale, core(), vg_ref, x_ref, piece_ref)


def open_turn_kernel(r_ref, l_ref, p_ref, ro_ref, lo_ref):
    half = r_ref.shape[0]
    ro_ref[:half] = (wide(r_ref) + p_ref[0, :half].astype(F32)).astype(BF16)
    ro_ref[half:] = p_ref[0, half:]
    lo_ref[:half] = p_ref[1, :half]
    lo_ref[half:] = (wide(l_ref) + p_ref[1, half:].astype(F32)).astype(BF16)


def turn(first, r_ref, l_ref, p_ref, ro_ref, lo_ref):
    ro_ref[...] = (wide(r_ref) + p_ref[first].astype(F32)).astype(BF16)
    lo_ref[...] = (wide(l_ref) + p_ref[first + 1].astype(F32)).astype(BF16)


def last_turn_kernel(r_ref, l_ref, p_ref, o_ref):
    o_ref[...] = (p_ref[p_ref.shape[0] - 1].astype(F32) + wide(r_ref) + wide(l_ref)).astype(BF16)


def key_grad_kernel(v_ref, kp_ref, state_ref, _, kg_ref):
    for c in heads_of(v_ref):
        kg_ref[:, c] = (kp_ref[:, c] + dot(v_ref[:, c], state_ref[c, :], NT)).astype(BF16)


def weight_pieces(scale, side, vg_ref, x_ref, o_ref):
    turned = vg_ref[...].T
    shift = side * 128
    for first in range(0, o_ref.shape[0], 4):
        x = jnp.concatenate(
            [
                x_ref[:, pl.ds(pl.multiple_of(p * 256 + shift, 128), 128)]
                for p in range(first, first + 4)
            ],
            axis=1,
        )
        res = (dot(turned, x) * scale).astype(BF16)
        for p in range(4):
            o_ref[first + p] = res[:, p * 128 : p * 128 + 128]


def chip_kernel(a_ref, b_ref, _, ru2, lv2, rv1, lu1, cu1, cv1, own):
    half = own.shape[1] // 2

    x, _ = place()

    def s(hop):
        i = lax.rem(x + hop, SIDE)
        return (a_ref[i].astype(F32) + b_ref[i].astype(F32)).astype(BF16)

    t = s(2)
    ru2[...] = t[:, :half]
    lv2[...] = t[:, half:]
    t = s(1)
    cu1[...] = t[:, :half]
    rv1[...] = t[:, half:]
    t = s(3)
    lu1[...] = t[:, :half]
    cv1[...] = t[:, half:]
    own[...] = s(0)


def pair_kernel(r_ref, l_ref, p_ref, a_ref, b_ref, c_ref, d_ref, _, ro_ref, lo_ref, o_ref, q_ref):
    turn(2, r_ref, l_ref, p_ref, ro_ref, lo_ref)
    o_ref[...] = (wide(a_ref) + wide(b_ref)).astype(BF16)
    q_ref[...] = (wide(c_ref) + wide(d_ref)).astype(BF16)


def line_kernel(r_ref, l_ref, p_ref, own_ref, ru_ref, lu_ref, rv_ref, lv_ref, ro_ref, lo_ref, m1, m2, m3, keep):
    turn(4, r_ref, l_ref, p_ref, ro_ref, lo_ref)
    half = ru_ref.shape[1]
    _, y = place()
    for hop, ref in ((1, m1), (2, m2), (3, m3), (0, keep)):
        i = lax.rem(y + hop, SIDE)
        own = own_ref[i].astype(F32)
        u = own[:half] + ru_ref[i].astype(F32) + lu_ref[i].astype(F32)
        v = own[half:] + rv_ref[i].astype(F32) + lv_ref[i].astype(F32)
        ref[:half] = u.astype(ref.dtype)
        ref[half:] = v.astype(ref.dtype)


def owner_kernel(keep_ref, a_ref, b_ref, c_ref, o_ref):
    o_ref[...] = (keep_ref[...] + wide(a_ref) + wide(b_ref) + wide(c_ref)).T


def local(layer_input, query_act, key_act, out_grad, value_weight):
    tok, width = layer_input.shape
    rows, cols = value_weight.shape
    square = sds((tok, cols))
    square_f32 = sds((tok, cols), F32)
    states = sds((cols, HDIM))

    w_other = swap(value_weight)
    x_near, part = call(
        value_own_kernel,
        [HBM, HBM],
        [in_hbm(layer_input), in_hbm(value_weight)],
        [sds((tok, width)), square_f32],
        "value_own",
        scratch=[pltpu.VMEM((rows, cols), BF16), pltpu.SemaphoreType.DMA((width // 512 + rows // 512,))],
    )
    halves = sds((cols // 2, HDIM))
    value, keep, give = call(
        value_rest_kernel,
        [VMEM] * 4,
        [x_near, w_other, part, key_act],
        [square, halves, halves],
        "value_rest",
    )
    near, far, (attended,) = exclusive(
        keep,
        give,
        1,
        lambda: call(
            inside_kernel,
            [VMEM] * 3,
            [query_act, key_act, value],
            [square_f32],
            "inside",
        ),
    )
    low, state, keep, give = call(
        norm_kernel,
        [VMEM] * 5,
        [query_act, out_grad, attended, near, far],
        [square, states, halves, halves],
        "norm_grad",
    )
    near, far, (value_part, key_part, query_grad) = exclusive(
        keep,
        give,
        -1,
        lambda: call(
            cross_kernel,
            [VMEM] * 5,
            [query_act, key_act, value, low, state],
            [square_f32, square_f32, square],
            "cross",
        ),
    )

    scale = 1.0 / math.sqrt(tok * lax.axis_size(("ctx", "fsdp")))
    half = sds((tok // 2, 512))
    full = sds((tok, 512))
    pieces = sds((width // 256, cols, 128))
    value_grad, state_grad, r, l, other = call(
        lambda *refs: first_kernel(scale, *refs),
        [VMEM] * 7,
        [key_act, value_part, near, far, value_weight, w_other, x_near],
        [square, states, half, half, pieces],
        "value_grad",
    )
    r, l = along_z(r, 1), along_z(l, -1)
    got = swap(other)
    parts, mine = call(
        lambda *refs: work_kernel(scale, *refs),
        [VMEM] * 4,
        [value_grad, value_weight, w_other, x_near],
        [sds((RING - 1, tok, 512)), pieces],
        "work",
    )
    r, l = call(open_turn_kernel, [VMEM] * 3, [r, l, parts], [full] * 2, "turn")
    after = r
    r, l = along_z(r, 1), along_z(l, -1)

    square4 = (SIDE, SIDE) + mine.shape[1:]
    piece = sds((SIDE, cols // 2, 128))
    ru2, lv2, rv1, lu1, cu1, cv1, own = call(
        chip_kernel,
        [VMEM] * 2 + [ANY],
        [mine.reshape(square4), got.reshape(square4), after],
        [piece] * 6 + [sds((SIDE, cols, 128))],
        "chip",
    )
    ru2, lv2 = along_x_ring(ru2, 1), along_x_ring(lv2, -1)
    rv1, lu1 = along_x_ring(rv1, 1), along_x_ring(lu1, -1)
    (key_grad,) = call(
        key_grad_kernel,
        [VMEM] * 3 + [ANY],
        [value, key_part, state_grad, own],
        [square],
        "key_grad",
    )
    r, l, ru1, lv1 = call(
        pair_kernel,
        [VMEM] * 7 + [HBM],
        [r, l, parts, cu1, ru2, cv1, lv2, in_hbm(key_grad)],
        [full] * 2 + [piece] * 2,
        "pair",
    )
    r, l = along_z(r, 1), along_z(l, -1)
    ru1, lv1 = along_x_ring(ru1, 1), along_x_ring(lv1, -1)
    r, l, m1, m2, m3, keep = call(
        line_kernel,
        [VMEM] * 8,
        [r, l, parts, own, ru1, lu1, rv1, lv1],
        [full] * 2 + [sds((cols, 128))] * 3 + [sds((cols, 128), F32)],
        "line",
    )
    r, l = along_z(r, 1), along_z(l, -1)
    got = [along_y_ring(m, k) for m, k in zip((m1, m2, m3), (1, 2, 3))]
    (weight_grad,) = call(
        owner_kernel, [VMEM] * 4, [keep, *got], [sds((128, cols), F32)], "owner"
    )
    (input_grad,) = call(last_turn_kernel, [VMEM] * 3, [r, l, parts], [full], "last_turn")
    return (query_grad, key_grad, input_grad, weight_grad)


def solution(mesh):
    in_specs = (
        P(("ctx", "fsdp"), None),
        P(("ctx", "fsdp"), "head"),
        P(("ctx", "fsdp"), "head"),
        P(("ctx", "fsdp"), "head"),
        P("fsdp", "head"),
    )
    out_specs = (
        P(("ctx", "fsdp"), "head"),
        P(("ctx", "fsdp"), "head"),
        P(("ctx", "fsdp"), "head"),
        P(("ctx", "fsdp"), "head"),
    )
    return jax.shard_map(local, mesh=mesh, in_specs=in_specs, out_specs=out_specs, check_vma=False)
```

```python
import math

import jax
import jax.numpy as jnp
from jax import lax
from jax.experimental import pallas as pl
from jax.experimental.pallas import tpu as pltpu
from jax.sharding import PartitionSpec as P

HDIM = 128
SIDE = 4
RING = 8
F32 = jnp.float32
BF16 = jnp.bfloat16
NT = (((1,), (1,)), ((), ()))
TN = (((0,), (0,)), ((), ()))
NN = (((1,), (0,)), ((), ()))

VMEM = pl.BlockSpec(memory_space=pltpu.VMEM)
ANY = pl.BlockSpec(memory_space=pl.ANY)
HBM = pl.BlockSpec(memory_space=pltpu.HBM)


def dot(a, b, dims=NN):
    return lax.dot_general(a, b, dims, preferred_element_type=F32)


def sds(shape, dtype=BF16):
    return jax.ShapeDtypeStruct(shape, dtype)


def core():
    return lax.axis_index("fsdp")


def place():
    at = lax.axis_index("ctx")
    return at // SIDE, lax.rem(at, SIDE)


def dest(which):
    i = which - 1
    hop = jnp.where(i % 2 == 0, 3 - i // 2, 5 + i // 2)
    return lax.rem(lax.axis_index("head") + hop, RING)


def wide(ref):
    return ref[...].astype(F32)


def call(body, specs, ins, outs, name, scratch=(), limit=16):
    return pl.pallas_call(
        body,
        out_shape=tuple(outs),
        in_specs=specs,
        out_specs=tuple([VMEM] * len(outs)),
        scratch_shapes=list(scratch),
        compiler_params=pltpu.CompilerParams(vmem_limit_bytes=limit * 2**20),
        cost_estimate=pl.CostEstimate(
            flops=1000,
            bytes_accessed=sum(a.size * a.dtype.itemsize for a in ins)
            + sum(math.prod(o.shape) * o.dtype.itemsize for o in outs),
            transcendentals=0,
        ),
        name=name,
    )(*ins)


def in_hbm(a):
    return pltpu.with_memory_space_constraint(a, pltpu.HBM)


def heads_of(ref):
    return [slice(h, h + HDIM) for h in range(0, ref.shape[1], HDIM)]


def each_head(ref, body):
    @pl.loop(0, ref.shape[1] // HDIM)
    def _(h):
        at = pl.multiple_of(h * HDIM, HDIM)
        body(pl.ds(at, HDIM))


def tril(scores):
    rows = lax.broadcasted_iota(jnp.int32, scores.shape, 0)
    cols = lax.broadcasted_iota(jnp.int32, scores.shape, 1)
    return jnp.where(rows >= cols, scores, 0.0).astype(BF16)


def value_own_kernel(x_hbm, w_hbm, x_ref, part_ref, w_ref, sems):
    step = 512
    n = x_hbm.shape[1] // step
    half = n // 2

    def x_cols(j):
        return pl.ds(pl.multiple_of(lax.rem(core() * half + j, n) * step, step), step)

    xs = [
        pltpu.make_async_copy(x_hbm.at[:, x_cols(j)], x_ref.at[:, x_cols(j)], sems.at[j])
        for j in range(n)
    ]
    ws = [
        pltpu.make_async_copy(
            w_hbm.at[pl.ds(j * step, step), :], w_ref.at[pl.ds(j * step, step), :], sems.at[n + j]
        )
        for j in range(half)
    ]
    for j in range(half):
        ws[j].start()
        xs[j].start()
    for j in range(half, n):
        xs[j].start()
    part_ref[...] = jnp.zeros_like(part_ref)

    @pl.loop(0, half)
    def _(j):
        rows = pl.ds(pl.multiple_of(j * step, step), step)
        pltpu.make_async_copy(w_hbm.at[rows, :], w_ref.at[rows, :], sems.at[n + j]).wait()
        pltpu.make_async_copy(
            x_hbm.at[:, x_cols(j)], x_ref.at[:, x_cols(j)], sems.at[j]
        ).wait()
        part_ref[...] += dot(x_ref[:, x_cols(j)], w_ref[rows, :])

    for j in range(half, n):
        xs[j].wait()


def split(rows, keep_ref, give_ref):
    half = keep_ref.shape[0]
    for h, state in enumerate(rows):
        to = (h * HDIM) // half

        @pl.when(core() == to)
        def _():
            keep_ref[h * HDIM - to * half : (h + 1) * HDIM - to * half, :] = state

        @pl.when(core() != to)
        def _():
            give_ref[h * HDIM - to * half : (h + 1) * HDIM - to * half, :] = state


def join(near_ref, far_ref, state_ref):
    half = near_ref.shape[0]
    mine = pl.ds(pl.multiple_of(core() * half, half), half)
    other = pl.ds(pl.multiple_of((1 - core()) * half, half), half)
    state_ref[mine, :] = near_ref[...].astype(BF16)
    state_ref[other, :] = far_ref[...]


def value_rest_kernel(x_ref, w_ref, part_ref, k_ref, v_ref, keep_ref, give_ref):
    rows = w_ref.shape[0]
    cols = pl.ds(pl.multiple_of((1 - core()) * rows, rows), rows)
    v = (part_ref[...] + dot(x_ref[:, cols], w_ref[...])).astype(BF16)
    v_ref[...] = v
    pairs = [dot(k_ref[:, c], v[:, c], TN).astype(BF16) for c in heads_of(v_ref)]
    split(pairs, keep_ref, give_ref)


def inside_kernel(q_ref, k_ref, v_ref, a_ref):
    def head(c):
        a_ref[:, c] = dot(tril(dot(q_ref[:, c], k_ref[:, c], NT)), v_ref[:, c])

    each_head(q_ref, head)


def norm_kernel(q_ref, g_ref, a_ref, near_ref, far_ref, low_ref, state_ref, keep_ref, give_ref):
    join(near_ref, far_ref, state_ref)
    local = []
    for c in heads_of(q_ref):
        att = a_ref[:, c] + dot(q_ref[:, c], state_ref[c, :])
        inv = lax.rsqrt(jnp.mean(att * att, axis=-1, keepdims=True) + 1e-05)
        normed = att * inv
        g = g_ref[:, c].astype(F32)
        low = (inv * (g - normed * jnp.mean(g * normed, axis=-1, keepdims=True))).astype(BF16)
        low_ref[:, c] = low
        local.append(dot(q_ref[:, c], low, TN).astype(BF16))
    split(local, keep_ref, give_ref)


def cross_kernel(q_ref, k_ref, v_ref, low_ref, state_ref, vp_ref, kp_ref, qg_ref):
    def head(c):
        q, k, low = q_ref[:, c], k_ref[:, c], low_ref[:, c]
        cross = tril(dot(low, v_ref[:, c], NT))
        qg_ref[:, c] = (dot(cross, k) + dot(low, state_ref[c, :], NT)).astype(BF16)
        kp_ref[:, c] = dot(cross, q, TN)
        vp_ref[:, c] = dot(tril(dot(q, k, NT)), low, TN)

    each_head(q_ref, head)


def chip_sum_kernel(keep_ref, got_ref, _, t_ref):
    t_ref[...] = (wide(keep_ref) + wide(got_ref)).astype(BF16)


def pair_sum_kernel(a_ref, b_ref, _, t_ref):
    t_ref[...] = (wide(a_ref) + wide(b_ref)).astype(BF16)


def part_before(sign, at, beside, across):
    if sign == -1:
        at = SIDE - 1 - at
    return jnp.where(at % 2 == 1, beside, 0.0) + jnp.where(at >= SIDE // 2, across, 0.0)


def last_sum_kernel(sign, keep_ref, got_ref, y1, y2, x1, x2, near_ref, far_ref):
    x, y = place()
    before = part_before(sign, y, wide(y1), wide(y2)) + part_before(sign, x, wide(x1), wide(x2))
    lead = core() == (0 if sign == 1 else 1)
    near_ref[...] = jnp.where(lead, before, before + wide(got_ref))
    far_ref[...] = jnp.where(lead, before + wide(keep_ref), before).astype(BF16)


def along(a, axis, beside):
    def other(i):
        x, y = i // SIDE, i % SIDE
        if axis == "x":
            x = x ^ 1 if beside else SIDE - 1 - x
        else:
            y = y ^ 1 if beside else SIDE - 1 - y
        return x * SIDE + y

    return lax.ppermute(a, "ctx", [(i, other(i)) for i in range(SIDE * SIDE)])


def along_x_ring(a, k):
    return lax.ppermute(a, "ctx", [(i, (i + SIDE * k) % 16) for i in range(16)])


def along_y_ring(a, k):
    return lax.ppermute(
        a, "ctx", [(i, i // SIDE * SIDE + (i + k) % SIDE) for i in range(16)]
    )


def along_z(a, k):
    return lax.ppermute(a, "head", [(i, (i + k) % RING) for i in range(RING)])


def swap(a):
    return lax.ppermute(a, "fsdp", [(0, 1), (1, 0)])


def exclusive(keep, give, sign, work):
    shape = sds(keep.shape)

    def fold(kernel, *arrays):
        (t,) = call(kernel, [VMEM] * len(arrays), arrays, [shape], "fold")
        return t

    got = swap(give)
    t = fold(chip_sum_kernel, keep, got, keep)
    y1 = along(t, "y", True)
    done = work()
    t = fold(pair_sum_kernel, t, y1, done[0])
    y2 = along(t, "y", False)
    t = fold(pair_sum_kernel, t, y2, done[0])
    x1 = along(t, "x", True)
    t = fold(pair_sum_kernel, t, x1, done[0])
    x2 = along(t, "x", False)
    near, far = call(
        lambda *refs: last_sum_kernel(sign, *refs),
        [VMEM] * 6,
        [keep, got, y1, y2, x1, x2],
        [sds(keep.shape, F32), shape],
        "last_sum",
    )
    return near, swap(far), done


def chunk_product(which, vg, own_ref, other_ref, use):
    rows = pl.ds(pl.multiple_of(lax.rem(dest(which), RING // 2) * 512, 512), 512)
    mine = dest(which) // (RING // 2) == core()

    @pl.when(mine)
    def _():
        use(dot(vg, own_ref[rows, :], NT).astype(BF16))

    @pl.when(jnp.logical_not(mine))
    def _():
        use(dot(vg, other_ref[rows, :], NT).astype(BF16))


def first_kernel(scale, k_ref, vp_ref, near_ref, far_ref, own_ref, other_ref, x_ref, vg_ref, state_ref, right_ref, left_ref, piece_ref):
    join(near_ref, far_ref, state_ref)
    for c in heads_of(k_ref):
        vg_ref[:, c] = (vp_ref[:, c] + dot(k_ref[:, c], state_ref[c, :])).astype(BF16)
    half = right_ref.shape[0]

    def use(p):
        right_ref[...] = p[:half]
        left_ref[...] = p[half:]

    chunk_product(0, vg_ref[...], own_ref, other_ref, use)
    weight_pieces(scale, 1 - core(), vg_ref, x_ref, piece_ref)


def work_kernel(scale, vg_ref, own_ref, other_ref, x_ref, p_ref, piece_ref):
    @pl.loop(0, p_ref.shape[0])
    def _(i):
        def use(p):
            p_ref[i] = p

        chunk_product(1 + i, vg_ref[...], own_ref, other_ref, use)
    weight_pieces(scale, core(), vg_ref, x_ref, piece_ref)


def open_turn_kernel(r_ref, l_ref, p_ref, ro_ref, lo_ref):
    half = r_ref.shape[0]
    ro_ref[:half] = (wide(r_ref) + p_ref[0, :half].astype(F32)).astype(BF16)
    ro_ref[half:] = p_ref[0, half:]
    lo_ref[:half] = p_ref[1, :half]
    lo_ref[half:] = (wide(l_ref) + p_ref[1, half:].astype(F32)).astype(BF16)


def turn(first, r_ref, l_ref, p_ref, ro_ref, lo_ref):
    ro_ref[...] = (wide(r_ref) + p_ref[first].astype(F32)).astype(BF16)
    lo_ref[...] = (wide(l_ref) + p_ref[first + 1].astype(F32)).astype(BF16)


def last_turn_kernel(r_ref, l_ref, p_ref, o_ref):
    o_ref[...] = (p_ref[p_ref.shape[0] - 1].astype(F32) + wide(r_ref) + wide(l_ref)).astype(BF16)


def key_grad_kernel(v_ref, kp_ref, state_ref, _, kg_ref):
    def head(c):
        kg_ref[:, c] = (kp_ref[:, c] + dot(v_ref[:, c], state_ref[c, :], NT)).astype(BF16)

    each_head(v_ref, head)


def weight_pieces(scale, side, vg_ref, x_ref, o_ref):
    turned = vg_ref[...].T
    shift = side * 128

    @pl.loop(0, o_ref.shape[0] // 4)
    def _(group):
        first = group * 4
        x = jnp.concatenate(
            [
                x_ref[:, pl.ds(pl.multiple_of((first + p) * 256 + shift, 128), 128)]
                for p in range(4)
            ],
            axis=1,
        )
        res = (dot(turned, x) * scale).astype(BF16)
        for p in range(4):
            o_ref[first + p] = res[:, p * 128 : p * 128 + 128]


def chip_kernel(a_ref, b_ref, _, ru2, lv2, rv1, lu1, cu1, cv1, own):
    half = own.shape[1] // 2

    x, _ = place()

    def s(hop):
        i = lax.rem(x + hop, SIDE)
        return (a_ref[i].astype(F32) + b_ref[i].astype(F32)).astype(BF16)

    t = s(2)
    ru2[...] = t[:, :half]
    lv2[...] = t[:, half:]
    t = s(1)
    cu1[...] = t[:, :half]
    rv1[...] = t[:, half:]
    t = s(3)
    lu1[...] = t[:, :half]
    cv1[...] = t[:, half:]
    own[...] = s(0)


def pair_kernel(r_ref, l_ref, p_ref, a_ref, b_ref, c_ref, d_ref, _, ro_ref, lo_ref, o_ref, q_ref):
    turn(2, r_ref, l_ref, p_ref, ro_ref, lo_ref)
    o_ref[...] = (wide(a_ref) + wide(b_ref)).astype(BF16)
    q_ref[...] = (wide(c_ref) + wide(d_ref)).astype(BF16)


def line_kernel(r_ref, l_ref, p_ref, own_ref, ru_ref, lu_ref, rv_ref, lv_ref, ro_ref, lo_ref, m1, m2, m3, keep):
    turn(4, r_ref, l_ref, p_ref, ro_ref, lo_ref)
    half = ru_ref.shape[1]
    _, y = place()
    for hop, ref in ((1, m1), (2, m2), (3, m3), (0, keep)):
        i = lax.rem(y + hop, SIDE)
        own = own_ref[i].astype(F32)
        u = own[:half] + ru_ref[i].astype(F32) + lu_ref[i].astype(F32)
        v = own[half:] + rv_ref[i].astype(F32) + lv_ref[i].astype(F32)
        ref[:half] = u.astype(ref.dtype)
        ref[half:] = v.astype(ref.dtype)


def owner_kernel(keep_ref, a_ref, b_ref, c_ref, o_ref):
    o_ref[...] = (keep_ref[...] + wide(a_ref) + wide(b_ref) + wide(c_ref)).T


def local(layer_input, query_act, key_act, out_grad, value_weight):
    tok, width = layer_input.shape
    rows, cols = value_weight.shape
    square = sds((tok, cols))
    square_f32 = sds((tok, cols), F32)
    states = sds((cols, HDIM))

    w_other = swap(value_weight)
    x_near, part = call(
        value_own_kernel,
        [HBM, HBM],
        [in_hbm(layer_input), in_hbm(value_weight)],
        [sds((tok, width)), square_f32],
        "value_own",
        scratch=[pltpu.VMEM((rows, cols), BF16), pltpu.SemaphoreType.DMA((width // 512 + rows // 512,))],
    )
    halves = sds((cols // 2, HDIM))
    value, keep, give = call(
        value_rest_kernel,
        [VMEM] * 4,
        [x_near, w_other, part, key_act],
        [square, halves, halves],
        "value_rest",
    )
    near, far, (attended,) = exclusive(
        keep,
        give,
        1,
        lambda: call(
            inside_kernel,
            [VMEM] * 3,
            [query_act, key_act, value],
            [square_f32],
            "inside",
        ),
    )
    low, state, keep, give = call(
        norm_kernel,
        [VMEM] * 5,
        [query_act, out_grad, attended, near, far],
        [square, states, halves, halves],
        "norm_grad",
    )
    near, far, (value_part, key_part, query_grad) = exclusive(
        keep,
        give,
        -1,
        lambda: call(
            cross_kernel,
            [VMEM] * 5,
            [query_act, key_act, value, low, state],
            [square_f32, square_f32, square],
            "cross",
        ),
    )

    scale = 1.0 / math.sqrt(tok * lax.axis_size(("ctx", "fsdp")))
    half = sds((tok // 2, 512))
    full = sds((tok, 512))
    pieces = sds((width // 256, cols, 128))
    value_grad, state_grad, r, l, other = call(
        lambda *refs: first_kernel(scale, *refs),
        [VMEM] * 7,
        [key_act, value_part, near, far, value_weight, w_other, x_near],
        [square, states, half, half, pieces],
        "value_grad",
    )
    r, l = along_z(r, 1), along_z(l, -1)
    got = swap(other)
    parts, mine = call(
        lambda *refs: work_kernel(scale, *refs),
        [VMEM] * 4,
        [value_grad, value_weight, w_other, x_near],
        [sds((RING - 1, tok, 512)), pieces],
        "work",
    )
    r, l = call(open_turn_kernel, [VMEM] * 3, [r, l, parts], [full] * 2, "turn")
    after = r
    r, l = along_z(r, 1), along_z(l, -1)

    square4 = (SIDE, SIDE) + mine.shape[1:]
    piece = sds((SIDE, cols // 2, 128))
    ru2, lv2, rv1, lu1, cu1, cv1, own = call(
        chip_kernel,
        [VMEM] * 2 + [ANY],
        [mine.reshape(square4), got.reshape(square4), after],
        [piece] * 6 + [sds((SIDE, cols, 128))],
        "chip",
    )
    ru2, lv2 = along_x_ring(ru2, 1), along_x_ring(lv2, -1)
    rv1, lu1 = along_x_ring(rv1, 1), along_x_ring(lu1, -1)
    (key_grad,) = call(
        key_grad_kernel,
        [VMEM] * 3 + [ANY],
        [value, key_part, state_grad, own],
        [square],
        "key_grad",
    )
    r, l, ru1, lv1 = call(
        pair_kernel,
        [VMEM] * 7 + [HBM],
        [r, l, parts, cu1, ru2, cv1, lv2, in_hbm(key_grad)],
        [full] * 2 + [piece] * 2,
        "pair",
    )
    r, l = along_z(r, 1), along_z(l, -1)
    ru1, lv1 = along_x_ring(ru1, 1), along_x_ring(lv1, -1)
    r, l, m1, m2, m3, keep = call(
        line_kernel,
        [VMEM] * 8,
        [r, l, parts, own, ru1, lu1, rv1, lv1],
        [full] * 2 + [sds((cols, 128))] * 3 + [sds((cols, 128), F32)],
        "line",
    )
    r, l = along_z(r, 1), along_z(l, -1)
    got = [along_y_ring(m, k) for m, k in zip((m1, m2, m3), (1, 2, 3))]
    (weight_grad,) = call(
        owner_kernel, [VMEM] * 4, [keep, *got], [sds((128, cols), F32)], "owner"
    )
    (input_grad,) = call(last_turn_kernel, [VMEM] * 3, [r, l, parts], [full], "last_turn")
    return (query_grad, key_grad, input_grad, weight_grad)


def solution(mesh):
    in_specs = (
        P(("ctx", "fsdp"), None),
        P(("ctx", "fsdp"), "head"),
        P(("ctx", "fsdp"), "head"),
        P(("ctx", "fsdp"), "head"),
        P("fsdp", "head"),
    )
    out_specs = (
        P(("ctx", "fsdp"), "head"),
        P(("ctx", "fsdp"), "head"),
        P(("ctx", "fsdp"), "head"),
        P(("ctx", "fsdp"), "head"),
    )
    return jax.shard_map(local, mesh=mesh, in_specs=in_specs, out_specs=out_specs, check_vma=False)
```

```python
import math

import jax
import jax.numpy as jnp
from jax import lax
from jax.experimental import pallas as pl
from jax.experimental.pallas import tpu as pltpu
from jax.sharding import PartitionSpec as P

HDIM = 128
SIDE = 4
RING = 8
F32 = jnp.float32
BF16 = jnp.bfloat16
NT = (((1,), (1,)), ((), ()))
TN = (((0,), (0,)), ((), ()))
NN = (((1,), (0,)), ((), ()))

VMEM = pl.BlockSpec(memory_space=pltpu.VMEM)
ANY = pl.BlockSpec(memory_space=pl.ANY)
HBM = pl.BlockSpec(memory_space=pltpu.HBM)


def dot(a, b, dims=NN):
    return lax.dot_general(a, b, dims, preferred_element_type=F32)


def sds(shape, dtype=BF16):
    return jax.ShapeDtypeStruct(shape, dtype)


def core():
    return lax.axis_index("fsdp")


def place():
    at = lax.axis_index("ctx")
    return at // SIDE, lax.rem(at, SIDE)


def dest(which):
    i = which - 1
    hop = jnp.where(i % 2 == 0, 3 - i // 2, 5 + i // 2)
    return lax.rem(lax.axis_index("head") + hop, RING)


def wide(ref):
    return ref[...].astype(F32)


def call(body, specs, ins, outs, name, scratch=(), limit=16):
    return pl.pallas_call(
        body,
        out_shape=tuple(outs),
        in_specs=specs,
        out_specs=tuple([VMEM] * len(outs)),
        scratch_shapes=list(scratch),
        compiler_params=pltpu.CompilerParams(vmem_limit_bytes=limit * 2**20),
        cost_estimate=pl.CostEstimate(
            flops=1000,
            bytes_accessed=sum(a.size * a.dtype.itemsize for a in ins)
            + sum(math.prod(o.shape) * o.dtype.itemsize for o in outs),
            transcendentals=0,
        ),
        name=name,
    )(*ins)


def in_hbm(a):
    return pltpu.with_memory_space_constraint(a, pltpu.HBM)


def heads_of(ref):
    return [slice(h, h + HDIM) for h in range(0, ref.shape[1], HDIM)]


def each_head(ref, body):
    @pl.loop(0, ref.shape[1] // HDIM)
    def _(h):
        at = pl.multiple_of(h * HDIM, HDIM)
        body(pl.ds(at, HDIM))


def tril(scores):
    rows = lax.broadcasted_iota(jnp.int32, scores.shape, 0)
    cols = lax.broadcasted_iota(jnp.int32, scores.shape, 1)
    return jnp.where(rows >= cols, scores, 0.0).astype(BF16)


def value_own_kernel(x_hbm, w_hbm, x_ref, part_ref, w_ref, sems):
    step = 512
    n = x_hbm.shape[1] // step
    half = n // 2

    def x_cols(j):
        return pl.ds(pl.multiple_of(lax.rem(core() * half + j, n) * step, step), step)

    xs = [
        pltpu.make_async_copy(x_hbm.at[:, x_cols(j)], x_ref.at[:, x_cols(j)], sems.at[j])
        for j in range(n)
    ]
    ws = [
        pltpu.make_async_copy(
            w_hbm.at[pl.ds(j * step, step), :], w_ref.at[pl.ds(j * step, step), :], sems.at[n + j]
        )
        for j in range(half)
    ]
    for j in range(half):
        ws[j].start()
        xs[j].start()
    for j in range(half, n):
        xs[j].start()
    for j in range(half):
        ws[j].wait()
        xs[j].wait()
        prod = dot(x_ref[:, x_cols(j)], w_ref[j * step : (j + 1) * step, :])
        if j == 0:
            part_ref[...] = prod
        else:
            part_ref[...] += prod
    for j in range(half, n):
        xs[j].wait()


def split(rows, keep_ref, give_ref):
    half = keep_ref.shape[0]
    for h, state in enumerate(rows):
        to = (h * HDIM) // half

        @pl.when(core() == to)
        def _():
            keep_ref[h * HDIM - to * half : (h + 1) * HDIM - to * half, :] = state

        @pl.when(core() != to)
        def _():
            give_ref[h * HDIM - to * half : (h + 1) * HDIM - to * half, :] = state


def join(near_ref, far_ref, state_ref):
    half = near_ref.shape[0]
    mine = pl.ds(pl.multiple_of(core() * half, half), half)
    other = pl.ds(pl.multiple_of((1 - core()) * half, half), half)
    state_ref[mine, :] = near_ref[...].astype(BF16)
    state_ref[other, :] = far_ref[...]


def value_rest_kernel(x_ref, w_ref, part_ref, k_ref, v_ref, keep_ref, give_ref):
    rows = w_ref.shape[0]
    cols = pl.ds(pl.multiple_of((1 - core()) * rows, rows), rows)
    v = (part_ref[...] + dot(x_ref[:, cols], w_ref[...])).astype(BF16)
    v_ref[...] = v
    pairs = [dot(k_ref[:, c], v[:, c], TN).astype(BF16) for c in heads_of(v_ref)]
    split(pairs, keep_ref, give_ref)


def inside_kernel(q_ref, k_ref, v_ref, a_ref):
    def head(c):
        a_ref[:, c] = dot(tril(dot(q_ref[:, c], k_ref[:, c], NT)), v_ref[:, c])

    each_head(q_ref, head)


def norm_kernel(q_ref, g_ref, a_ref, near_ref, far_ref, low_ref, state_ref, keep_ref, give_ref):
    join(near_ref, far_ref, state_ref)
    local = []
    for c in heads_of(q_ref):
        att = a_ref[:, c] + dot(q_ref[:, c], state_ref[c, :])
        inv = lax.rsqrt(jnp.mean(att * att, axis=-1, keepdims=True) + 1e-05)
        normed = att * inv
        g = g_ref[:, c].astype(F32)
        low = (inv * (g - normed * jnp.mean(g * normed, axis=-1, keepdims=True))).astype(BF16)
        low_ref[:, c] = low
        local.append(dot(q_ref[:, c], low, TN).astype(BF16))
    split(local, keep_ref, give_ref)


def masked_kernel(q_ref, k_ref, low_ref, vp_ref):
    def head(c):
        vp_ref[:, c] = dot(tril(dot(q_ref[:, c], k_ref[:, c], NT)), low_ref[:, c], TN)

    each_head(q_ref, head)


def cross_kernel(q_ref, k_ref, v_ref, low_ref, state_ref, qg_ref, kp_ref):
    def head(c):
        low = low_ref[:, c]
        cross = tril(dot(low, v_ref[:, c], NT))
        qg_ref[:, c] = (dot(cross, k_ref[:, c]) + dot(low, state_ref[c, :], NT)).astype(BF16)
        kp_ref[:, c] = dot(cross, q_ref[:, c], TN)

    each_head(q_ref, head)


def chip_sum_kernel(keep_ref, got_ref, _, t_ref):
    t_ref[...] = (wide(keep_ref) + wide(got_ref)).astype(BF16)


def pair_sum_kernel(a_ref, b_ref, _, t_ref):
    t_ref[...] = (wide(a_ref) + wide(b_ref)).astype(BF16)


def part_before(sign, at, beside, across):
    if sign == -1:
        at = SIDE - 1 - at
    return jnp.where(at % 2 == 1, beside, 0.0) + jnp.where(at >= SIDE // 2, across, 0.0)


def last_sum_kernel(sign, keep_ref, got_ref, y1, y2, x1, x2, near_ref, far_ref):
    x, y = place()
    before = part_before(sign, y, wide(y1), wide(y2)) + part_before(sign, x, wide(x1), wide(x2))
    lead = core() == (0 if sign == 1 else 1)
    near_ref[...] = jnp.where(lead, before, before + wide(got_ref))
    far_ref[...] = jnp.where(lead, before + wide(keep_ref), before).astype(BF16)


def along(a, axis, beside):
    def other(i):
        x, y = i // SIDE, i % SIDE
        if axis == "x":
            x = x ^ 1 if beside else SIDE - 1 - x
        else:
            y = y ^ 1 if beside else SIDE - 1 - y
        return x * SIDE + y

    return lax.ppermute(a, "ctx", [(i, other(i)) for i in range(SIDE * SIDE)])


def along_x_ring(a, k):
    return lax.ppermute(a, "ctx", [(i, (i + SIDE * k) % 16) for i in range(16)])


def along_y_ring(a, k):
    return lax.ppermute(
        a, "ctx", [(i, i // SIDE * SIDE + (i + k) % SIDE) for i in range(16)]
    )


def along_z(a, k):
    return lax.ppermute(a, "head", [(i, (i + k) % RING) for i in range(RING)])


def swap(a):
    return lax.ppermute(a, "fsdp", [(0, 1), (1, 0)])


def exclusive(keep, give, sign, first, second=lambda: ()):
    shape = sds(keep.shape)

    def fold(kernel, *arrays):
        (t,) = call(kernel, [VMEM] * len(arrays), arrays, [shape], "fold")
        return t

    got = swap(give)
    t = fold(chip_sum_kernel, keep, got, keep)
    y1 = along(t, "y", True)
    done = list(first())
    t = fold(pair_sum_kernel, t, y1, done[0])
    y2 = along(t, "y", False)
    done += list(second())
    t = fold(pair_sum_kernel, t, y2, done[-1])
    x1 = along(t, "x", True)
    t = fold(pair_sum_kernel, t, x1, done[0])
    x2 = along(t, "x", False)
    near, far = call(
        lambda *refs: last_sum_kernel(sign, *refs),
        [VMEM] * 6,
        [keep, got, y1, y2, x1, x2],
        [sds(keep.shape, F32), shape],
        "last_sum",
    )
    return near, swap(far), done


def chunk_product(which, vg, own_ref, other_ref, use):
    rows = pl.ds(pl.multiple_of(lax.rem(dest(which), RING // 2) * 512, 512), 512)
    mine = dest(which) // (RING // 2) == core()

    @pl.when(mine)
    def _():
        use(dot(vg, own_ref[rows, :], NT).astype(BF16))

    @pl.when(jnp.logical_not(mine))
    def _():
        use(dot(vg, other_ref[rows, :], NT).astype(BF16))


def first_kernel(scale, k_ref, vp_ref, near_ref, far_ref, own_ref, other_ref, x_ref, vg_ref, state_ref, right_ref, left_ref, piece_ref):
    join(near_ref, far_ref, state_ref)
    for c in heads_of(k_ref):
        vg_ref[:, c] = (vp_ref[:, c] + dot(k_ref[:, c], state_ref[c, :])).astype(BF16)
    half = right_ref.shape[0]

    def use(p):
        right_ref[...] = p[:half]
        left_ref[...] = p[half:]

    chunk_product(0, vg_ref[...], own_ref, other_ref, use)
    weight_pieces(scale, 1 - core(), vg_ref, x_ref, piece_ref)


def work_kernel(scale, vg_ref, own_ref, other_ref, x_ref, p_ref, piece_ref):
    @pl.loop(0, p_ref.shape[0])
    def _(i):
        def use(p):
            p_ref[i] = p

        chunk_product(1 + i, vg_ref[...], own_ref, other_ref, use)
    weight_pieces(scale, core(), vg_ref, x_ref, piece_ref)


def open_turn_kernel(r_ref, l_ref, p_ref, ro_ref, lo_ref):
    half = r_ref.shape[0]
    ro_ref[:half] = (wide(r_ref) + p_ref[0, :half].astype(F32)).astype(BF16)
    ro_ref[half:] = p_ref[0, half:]
    lo_ref[:half] = p_ref[1, :half]
    lo_ref[half:] = (wide(l_ref) + p_ref[1, half:].astype(F32)).astype(BF16)


def turn(first, r_ref, l_ref, p_ref, ro_ref, lo_ref):
    ro_ref[...] = (wide(r_ref) + p_ref[first].astype(F32)).astype(BF16)
    lo_ref[...] = (wide(l_ref) + p_ref[first + 1].astype(F32)).astype(BF16)


def last_turn_kernel(r_ref, l_ref, p_ref, o_ref):
    o_ref[...] = (p_ref[p_ref.shape[0] - 1].astype(F32) + wide(r_ref) + wide(l_ref)).astype(BF16)


def key_grad_kernel(v_ref, kp_ref, state_ref, _, kg_ref):
    def head(c):
        kg_ref[:, c] = (kp_ref[:, c] + dot(v_ref[:, c], state_ref[c, :], NT)).astype(BF16)

    each_head(v_ref, head)


def weight_pieces(scale, side, vg_ref, x_ref, o_ref):
    turned = vg_ref[...].T
    shift = side * 128
    for first in range(0, o_ref.shape[0], 4):
        x = jnp.concatenate(
            [
                x_ref[:, pl.ds(pl.multiple_of((first + p) * 256 + shift, 128), 128)]
                for p in range(4)
            ],
            axis=1,
        )
        res = (dot(turned, x) * scale).astype(BF16)
        for p in range(4):
            o_ref[first + p] = res[:, p * 128 : p * 128 + 128]


def chip_kernel(a_ref, b_ref, _, ru2, lv2, rv1, lu1, cu1, cv1, own):
    half = own.shape[1] // 2

    x, _ = place()

    def s(hop):
        i = lax.rem(x + hop, SIDE)
        return (a_ref[i].astype(F32) + b_ref[i].astype(F32)).astype(BF16)

    t = s(2)
    ru2[...] = t[:, :half]
    lv2[...] = t[:, half:]
    t = s(1)
    cu1[...] = t[:, :half]
    rv1[...] = t[:, half:]
    t = s(3)
    lu1[...] = t[:, :half]
    cv1[...] = t[:, half:]
    own[...] = s(0)


def pair_kernel(r_ref, l_ref, p_ref, a_ref, b_ref, c_ref, d_ref, _, ro_ref, lo_ref, o_ref, q_ref):
    turn(2, r_ref, l_ref, p_ref, ro_ref, lo_ref)
    o_ref[...] = (wide(a_ref) + wide(b_ref)).astype(BF16)
    q_ref[...] = (wide(c_ref) + wide(d_ref)).astype(BF16)


def line_kernel(r_ref, l_ref, p_ref, own_ref, ru_ref, lu_ref, rv_ref, lv_ref, ro_ref, lo_ref, m1, m2, m3, keep):
    turn(4, r_ref, l_ref, p_ref, ro_ref, lo_ref)
    half = ru_ref.shape[1]
    _, y = place()
    for hop, ref in ((1, m1), (2, m2), (3, m3), (0, keep)):
        i = lax.rem(y + hop, SIDE)
        own = own_ref[i].astype(F32)
        u = own[:half] + ru_ref[i].astype(F32) + lu_ref[i].astype(F32)
        v = own[half:] + rv_ref[i].astype(F32) + lv_ref[i].astype(F32)
        ref[:half] = u.astype(ref.dtype)
        ref[half:] = v.astype(ref.dtype)


def owner_kernel(keep_ref, a_ref, b_ref, c_ref, o_ref):
    o_ref[...] = (keep_ref[...] + wide(a_ref) + wide(b_ref) + wide(c_ref)).T


def local(layer_input, query_act, key_act, out_grad, value_weight):
    tok, width = layer_input.shape
    rows, cols = value_weight.shape
    square = sds((tok, cols))
    square_f32 = sds((tok, cols), F32)
    states = sds((cols, HDIM))

    w_other = swap(value_weight)
    x_near, part = call(
        value_own_kernel,
        [HBM, HBM],
        [in_hbm(layer_input), in_hbm(value_weight)],
        [sds((tok, width)), square_f32],
        "value_own",
        scratch=[pltpu.VMEM((rows, cols), BF16), pltpu.SemaphoreType.DMA((width // 512 + rows // 512,))],
    )
    halves = sds((cols // 2, HDIM))
    value, keep, give = call(
        value_rest_kernel,
        [VMEM] * 4,
        [x_near, w_other, part, key_act],
        [square, halves, halves],
        "value_rest",
    )
    near, far, (attended,) = exclusive(
        keep,
        give,
        1,
        lambda: call(
            inside_kernel,
            [VMEM] * 3,
            [query_act, key_act, value],
            [square_f32],
            "inside",
        ),
    )
    low, state, keep, give = call(
        norm_kernel,
        [VMEM] * 5,
        [query_act, out_grad, attended, near, far],
        [square, states, halves, halves],
        "norm_grad",
    )
    near, far, (value_part, query_grad, key_part) = exclusive(
        keep,
        give,
        -1,
        lambda: call(
            masked_kernel, [VMEM] * 3, [query_act, key_act, low], [square_f32], "masked"
        ),
        lambda: call(
            cross_kernel,
            [VMEM] * 5,
            [query_act, key_act, value, low, state],
            [square, square_f32],
            "cross",
        ),
    )

    scale = 1.0 / math.sqrt(tok * lax.axis_size(("ctx", "fsdp")))
    half = sds((tok // 2, 512))
    full = sds((tok, 512))
    pieces = sds((width // 256, cols, 128))
    value_grad, state_grad, r, l, other = call(
        lambda *refs: first_kernel(scale, *refs),
        [VMEM] * 7,
        [key_act, value_part, near, far, value_weight, w_other, x_near],
        [square, states, half, half, pieces],
        "value_grad",
    )
    r, l = along_z(r, 1), along_z(l, -1)
    got = swap(other)
    parts, mine = call(
        lambda *refs: work_kernel(scale, *refs),
        [VMEM] * 4,
        [value_grad, value_weight, w_other, x_near],
        [sds((RING - 1, tok, 512)), pieces],
        "work",
    )
    r, l = call(open_turn_kernel, [VMEM] * 3, [r, l, parts], [full] * 2, "turn")
    after = r
    r, l = along_z(r, 1), along_z(l, -1)

    square4 = (SIDE, SIDE) + mine.shape[1:]
    piece = sds((SIDE, cols // 2, 128))
    ru2, lv2, rv1, lu1, cu1, cv1, own = call(
        chip_kernel,
        [VMEM] * 2 + [ANY],
        [mine.reshape(square4), got.reshape(square4), after],
        [piece] * 6 + [sds((SIDE, cols, 128))],
        "chip",
    )
    ru2, lv2 = along_x_ring(ru2, 1), along_x_ring(lv2, -1)
    rv1, lu1 = along_x_ring(rv1, 1), along_x_ring(lu1, -1)
    (key_grad,) = call(
        key_grad_kernel,
        [VMEM] * 3 + [ANY],
        [value, key_part, state_grad, own],
        [square],
        "key_grad",
    )
    r, l, ru1, lv1 = call(
        pair_kernel,
        [VMEM] * 7 + [HBM],
        [r, l, parts, cu1, ru2, cv1, lv2, in_hbm(key_grad)],
        [full] * 2 + [piece] * 2,
        "pair",
    )
    r, l = along_z(r, 1), along_z(l, -1)
    ru1, lv1 = along_x_ring(ru1, 1), along_x_ring(lv1, -1)
    r, l, m1, m2, m3, keep = call(
        line_kernel,
        [VMEM] * 8,
        [r, l, parts, own, ru1, lu1, rv1, lv1],
        [full] * 2 + [sds((cols, 128))] * 3 + [sds((cols, 128), F32)],
        "line",
    )
    r, l = along_z(r, 1), along_z(l, -1)
    got = [along_y_ring(m, k) for m, k in zip((m1, m2, m3), (1, 2, 3))]
    (weight_grad,) = call(
        owner_kernel, [VMEM] * 4, [keep, *got], [sds((128, cols), F32)], "owner"
    )
    (input_grad,) = call(last_turn_kernel, [VMEM] * 3, [r, l, parts], [full], "last_turn")
    return (query_grad, key_grad, input_grad, weight_grad)


def solution(mesh):
    in_specs = (
        P(("ctx", "fsdp"), None),
        P(("ctx", "fsdp"), "head"),
        P(("ctx", "fsdp"), "head"),
        P(("ctx", "fsdp"), "head"),
        P("fsdp", "head"),
    )
    out_specs = (
        P(("ctx", "fsdp"), "head"),
        P(("ctx", "fsdp"), "head"),
        P(("ctx", "fsdp"), "head"),
        P(("ctx", "fsdp"), "head"),
    )
    return jax.shard_map(local, mesh=mesh, in_specs=in_specs, out_specs=out_specs, check_vma=False)
```

```python
import math

import jax
import jax.numpy as jnp
from jax import lax
from jax.experimental import pallas as pl
from jax.experimental.pallas import tpu as pltpu
from jax.sharding import PartitionSpec as P

HDIM = 128
SIDE = 4
RING = 8
F32 = jnp.float32
BF16 = jnp.bfloat16
NT = (((1,), (1,)), ((), ()))
TN = (((0,), (0,)), ((), ()))
NN = (((1,), (0,)), ((), ()))

VMEM = pl.BlockSpec(memory_space=pltpu.VMEM)
ANY = pl.BlockSpec(memory_space=pl.ANY)
HBM = pl.BlockSpec(memory_space=pltpu.HBM)


def dot(a, b, dims=NN):
    return lax.dot_general(a, b, dims, preferred_element_type=F32)


def sds(shape, dtype=BF16):
    return jax.ShapeDtypeStruct(shape, dtype)


def core():
    return lax.axis_index("fsdp")


def place():
    at = lax.axis_index("ctx")
    return at // SIDE, lax.rem(at, SIDE)


def dest(which):
    i = which - 1
    hop = jnp.where(i % 2 == 0, 3 - i // 2, 5 + i // 2)
    return lax.rem(lax.axis_index("head") + hop, RING)


def wide(ref):
    return ref[...].astype(F32)


def call(body, specs, ins, outs, name, scratch=(), limit=16):
    return pl.pallas_call(
        body,
        out_shape=tuple(outs),
        in_specs=specs,
        out_specs=tuple([VMEM] * len(outs)),
        scratch_shapes=list(scratch),
        compiler_params=pltpu.CompilerParams(vmem_limit_bytes=limit * 2**20),
        cost_estimate=pl.CostEstimate(
            flops=1000,
            bytes_accessed=sum(a.size * a.dtype.itemsize for a in ins)
            + sum(math.prod(o.shape) * o.dtype.itemsize for o in outs),
            transcendentals=0,
        ),
        name=name,
    )(*ins)


def in_hbm(a):
    return pltpu.with_memory_space_constraint(a, pltpu.HBM)


def heads_of(ref):
    return [slice(h, h + HDIM) for h in range(0, ref.shape[1], HDIM)]


def each_head(ref, body):
    @pl.loop(0, ref.shape[1] // (2 * HDIM))
    def _(pair):
        for h in range(2):
            body(pl.ds(pl.multiple_of((2 * pair + h) * HDIM, HDIM), HDIM))


def tril(scores):
    rows = lax.broadcasted_iota(jnp.int32, scores.shape, 0)
    cols = lax.broadcasted_iota(jnp.int32, scores.shape, 1)
    return jnp.where(rows >= cols, scores, 0.0).astype(BF16)


def value_own_kernel(x_hbm, w_hbm, x_ref, part_ref, w_ref, sems):
    step = 512
    n = x_hbm.shape[1] // step
    half = n // 2

    def x_cols(j):
        return pl.ds(pl.multiple_of(lax.rem(core() * half + j, n) * step, step), step)

    xs = [
        pltpu.make_async_copy(x_hbm.at[:, x_cols(j)], x_ref.at[:, x_cols(j)], sems.at[j])
        for j in range(n)
    ]
    ws = [
        pltpu.make_async_copy(
            w_hbm.at[pl.ds(j * step, step), :], w_ref.at[pl.ds(j * step, step), :], sems.at[n + j]
        )
        for j in range(half)
    ]
    for j in range(half):
        ws[j].start()
        xs[j].start()
    for j in range(half, n):
        xs[j].start()
    for j in range(half):
        ws[j].wait()
        xs[j].wait()
        prod = dot(x_ref[:, x_cols(j)], w_ref[j * step : (j + 1) * step, :])
        if j == 0:
            part_ref[...] = prod
        else:
            part_ref[...] += prod
    for j in range(half, n):
        xs[j].wait()


def split(rows, keep_ref, give_ref):
    half = keep_ref.shape[0]
    for h, state in enumerate(rows):
        to = (h * HDIM) // half

        @pl.when(core() == to)
        def _():
            keep_ref[h * HDIM - to * half : (h + 1) * HDIM - to * half, :] = state

        @pl.when(core() != to)
        def _():
            give_ref[h * HDIM - to * half : (h + 1) * HDIM - to * half, :] = state


def join(near_ref, far_ref, state_ref):
    half = near_ref.shape[0]
    mine = pl.ds(pl.multiple_of(core() * half, half), half)
    other = pl.ds(pl.multiple_of((1 - core()) * half, half), half)
    state_ref[mine, :] = near_ref[...].astype(BF16)
    state_ref[other, :] = far_ref[...]


def value_rest_kernel(x_ref, w_ref, part_ref, k_ref, v_ref, keep_ref, give_ref):
    rows = w_ref.shape[0]
    cols = pl.ds(pl.multiple_of((1 - core()) * rows, rows), rows)
    v = (part_ref[...] + dot(x_ref[:, cols], w_ref[...])).astype(BF16)
    v_ref[...] = v
    pairs = [dot(k_ref[:, c], v[:, c], TN).astype(BF16) for c in heads_of(v_ref)]
    split(pairs, keep_ref, give_ref)


def inside_kernel(q_ref, k_ref, v_ref, a_ref):
    def head(c):
        a_ref[:, c] = dot(tril(dot(q_ref[:, c], k_ref[:, c], NT)), v_ref[:, c])

    each_head(q_ref, head)


def norm_kernel(q_ref, g_ref, a_ref, near_ref, far_ref, low_ref, state_ref, keep_ref, give_ref):
    join(near_ref, far_ref, state_ref)
    local = []
    for c in heads_of(q_ref):
        att = a_ref[:, c] + dot(q_ref[:, c], state_ref[c, :])
        inv = lax.rsqrt(jnp.mean(att * att, axis=-1, keepdims=True) + 1e-05)
        normed = att * inv
        g = g_ref[:, c].astype(F32)
        low = (inv * (g - normed * jnp.mean(g * normed, axis=-1, keepdims=True))).astype(BF16)
        low_ref[:, c] = low
        local.append(dot(q_ref[:, c], low, TN).astype(BF16))
    split(local, keep_ref, give_ref)


def masked_kernel(q_ref, k_ref, low_ref, vp_ref):
    def head(c):
        vp_ref[:, c] = dot(tril(dot(q_ref[:, c], k_ref[:, c], NT)), low_ref[:, c], TN)

    each_head(q_ref, head)


def cross_kernel(q_ref, k_ref, v_ref, low_ref, state_ref, qg_ref, kp_ref):
    def head(c):
        low = low_ref[:, c]
        cross = tril(dot(low, v_ref[:, c], NT))
        qg_ref[:, c] = (dot(cross, k_ref[:, c]) + dot(low, state_ref[c, :], NT)).astype(BF16)
        kp_ref[:, c] = dot(cross, q_ref[:, c], TN)

    each_head(q_ref, head)


def chip_sum_kernel(keep_ref, got_ref, _, t_ref):
    t_ref[...] = (wide(keep_ref) + wide(got_ref)).astype(BF16)


def pair_sum_kernel(a_ref, b_ref, _, t_ref):
    t_ref[...] = (wide(a_ref) + wide(b_ref)).astype(BF16)


def part_before(sign, at, beside, across):
    if sign == -1:
        at = SIDE - 1 - at
    return jnp.where(at % 2 == 1, beside, 0.0) + jnp.where(at >= SIDE // 2, across, 0.0)


def last_sum_kernel(sign, keep_ref, got_ref, y1, y2, x1, x2, near_ref, far_ref):
    x, y = place()
    before = part_before(sign, y, wide(y1), wide(y2)) + part_before(sign, x, wide(x1), wide(x2))
    lead = core() == (0 if sign == 1 else 1)
    near_ref[...] = jnp.where(lead, before, before + wide(got_ref))
    far_ref[...] = jnp.where(lead, before + wide(keep_ref), before).astype(BF16)


def along(a, axis, beside):
    def other(i):
        x, y = i // SIDE, i % SIDE
        if axis == "x":
            x = x ^ 1 if beside else SIDE - 1 - x
        else:
            y = y ^ 1 if beside else SIDE - 1 - y
        return x * SIDE + y

    return lax.ppermute(a, "ctx", [(i, other(i)) for i in range(SIDE * SIDE)])


def along_x_ring(a, k):
    return lax.ppermute(a, "ctx", [(i, (i + SIDE * k) % 16) for i in range(16)])


def along_y_ring(a, k):
    return lax.ppermute(
        a, "ctx", [(i, i // SIDE * SIDE + (i + k) % SIDE) for i in range(16)]
    )


def along_z(a, k):
    return lax.ppermute(a, "head", [(i, (i + k) % RING) for i in range(RING)])


def swap(a):
    return lax.ppermute(a, "fsdp", [(0, 1), (1, 0)])


def exclusive(keep, give, sign, first, second=lambda: ()):
    shape = sds(keep.shape)

    def fold(kernel, *arrays):
        (t,) = call(kernel, [VMEM] * len(arrays), arrays, [shape], "fold")
        return t

    got = swap(give)
    t = fold(chip_sum_kernel, keep, got, keep)
    y1 = along(t, "y", True)
    done = list(first())
    t = fold(pair_sum_kernel, t, y1, done[0])
    y2 = along(t, "y", False)
    done += list(second())
    t = fold(pair_sum_kernel, t, y2, done[-1])
    x1 = along(t, "x", True)
    t = fold(pair_sum_kernel, t, x1, done[0])
    x2 = along(t, "x", False)
    near, far = call(
        lambda *refs: last_sum_kernel(sign, *refs),
        [VMEM] * 6,
        [keep, got, y1, y2, x1, x2],
        [sds(keep.shape, F32), shape],
        "last_sum",
    )
    return near, swap(far), done


def chunk_product(which, vg, own_ref, other_ref, use):
    rows = pl.ds(pl.multiple_of(lax.rem(dest(which), RING // 2) * 512, 512), 512)
    mine = dest(which) // (RING // 2) == core()

    @pl.when(mine)
    def _():
        use(dot(vg, own_ref[rows, :], NT).astype(BF16))

    @pl.when(jnp.logical_not(mine))
    def _():
        use(dot(vg, other_ref[rows, :], NT).astype(BF16))


def first_kernel(scale, k_ref, vp_ref, near_ref, far_ref, own_ref, other_ref, x_ref, vg_ref, state_ref, right_ref, left_ref, piece_ref):
    join(near_ref, far_ref, state_ref)
    for c in heads_of(k_ref):
        vg_ref[:, c] = (vp_ref[:, c] + dot(k_ref[:, c], state_ref[c, :])).astype(BF16)
    half = right_ref.shape[0]

    def use(p):
        right_ref[...] = p[:half]
        left_ref[...] = p[half:]

    chunk_product(0, vg_ref[...], own_ref, other_ref, use)
    weight_pieces(scale, 1 - core(), vg_ref, x_ref, piece_ref)


def chunks(first, vg_ref, own_ref, other_ref, p_ref):
    @pl.loop(0, p_ref.shape[0])
    def _(i):
        def use(p):
            p_ref[i] = p

        chunk_product(first + i, vg_ref[...], own_ref, other_ref, use)


def work_kernel(scale, vg_ref, own_ref, other_ref, x_ref, p_ref, piece_ref):
    chunks(1, vg_ref, own_ref, other_ref, p_ref)
    weight_pieces(scale, core(), vg_ref, x_ref, piece_ref)


def open_turn_kernel(r_ref, l_ref, p_ref, ro_ref, lo_ref):
    half = r_ref.shape[0]
    ro_ref[:half] = (wide(r_ref) + p_ref[0, :half].astype(F32)).astype(BF16)
    ro_ref[half:] = p_ref[0, half:]
    lo_ref[:half] = p_ref[1, :half]
    lo_ref[half:] = (wide(l_ref) + p_ref[1, half:].astype(F32)).astype(BF16)


def turn(first, r_ref, l_ref, p_ref, ro_ref, lo_ref):
    ro_ref[...] = (wide(r_ref) + p_ref[first].astype(F32)).astype(BF16)
    lo_ref[...] = (wide(l_ref) + p_ref[first + 1].astype(F32)).astype(BF16)


def key_grad_kernel(v_ref, kp_ref, state_ref, vg_ref, own_ref, other_ref, _, kg_ref, p_ref):
    def head(c):
        kg_ref[:, c] = (kp_ref[:, c] + dot(v_ref[:, c], state_ref[c, :], NT)).astype(BF16)

    each_head(v_ref, head)
    chunks(3, vg_ref, own_ref, other_ref, p_ref)


def weight_pieces(scale, side, vg_ref, x_ref, o_ref):
    turned = vg_ref[...].T
    shift = side * 128
    for first in range(0, o_ref.shape[0], 4):
        x = jnp.concatenate(
            [
                x_ref[:, pl.ds(pl.multiple_of((first + p) * 256 + shift, 128), 128)]
                for p in range(4)
            ],
            axis=1,
        )
        res = (dot(turned, x) * scale).astype(BF16)
        for p in range(4):
            o_ref[first + p] = res[:, p * 128 : p * 128 + 128]


def chip_kernel(a_ref, b_ref, _, ru2, lv2, rv1, lu1, cu1, cv1, own):
    half = own.shape[1] // 2

    x, _ = place()

    def s(hop):
        i = lax.rem(x + hop, SIDE)
        return (a_ref[i].astype(F32) + b_ref[i].astype(F32)).astype(BF16)

    t = s(2)
    ru2[...] = t[:, :half]
    lv2[...] = t[:, half:]
    t = s(1)
    cu1[...] = t[:, :half]
    rv1[...] = t[:, half:]
    t = s(3)
    lu1[...] = t[:, :half]
    cv1[...] = t[:, half:]
    own[...] = s(0)


def pair_kernel(r_ref, l_ref, p_ref, a_ref, b_ref, c_ref, d_ref, ro_ref, lo_ref, o_ref, q_ref):
    turn(0, r_ref, l_ref, p_ref, ro_ref, lo_ref)
    o_ref[...] = (wide(a_ref) + wide(b_ref)).astype(BF16)
    q_ref[...] = (wide(c_ref) + wide(d_ref)).astype(BF16)


def line_kernel(r_ref, l_ref, p_ref, own_ref, ru_ref, lu_ref, rv_ref, lv_ref, ro_ref, lo_ref, m1, m2, m3, keep):
    turn(2, r_ref, l_ref, p_ref, ro_ref, lo_ref)
    half = ru_ref.shape[1]
    _, y = place()
    for hop, ref in ((1, m1), (2, m2), (3, m3), (0, keep)):
        i = lax.rem(y + hop, SIDE)
        own = own_ref[i].astype(F32)
        u = own[:half] + ru_ref[i].astype(F32) + lu_ref[i].astype(F32)
        v = own[half:] + rv_ref[i].astype(F32) + lv_ref[i].astype(F32)
        ref[:half] = u.astype(ref.dtype)
        ref[half:] = v.astype(ref.dtype)


def last_kernel(keep_ref, a_ref, b_ref, c_ref, r_ref, l_ref, p_ref, o_ref, i_ref):
    i_ref[...] = (p_ref[p_ref.shape[0] - 1].astype(F32) + wide(r_ref) + wide(l_ref)).astype(BF16)
    o_ref[...] = (keep_ref[...] + wide(a_ref) + wide(b_ref) + wide(c_ref)).T


def local(layer_input, query_act, key_act, out_grad, value_weight):
    tok, width = layer_input.shape
    rows, cols = value_weight.shape
    square = sds((tok, cols))
    square_f32 = sds((tok, cols), F32)
    states = sds((cols, HDIM))

    w_other = swap(value_weight)
    x_near, part = call(
        value_own_kernel,
        [HBM, HBM],
        [in_hbm(layer_input), in_hbm(value_weight)],
        [sds((tok, width)), square_f32],
        "value_own",
        scratch=[pltpu.VMEM((rows, cols), BF16), pltpu.SemaphoreType.DMA((width // 512 + rows // 512,))],
    )
    halves = sds((cols // 2, HDIM))
    value, keep, give = call(
        value_rest_kernel,
        [VMEM] * 4,
        [x_near, w_other, part, key_act],
        [square, halves, halves],
        "value_rest",
    )
    near, far, (attended,) = exclusive(
        keep,
        give,
        1,
        lambda: call(
            inside_kernel,
            [VMEM] * 3,
            [query_act, key_act, value],
            [square_f32],
            "inside",
        ),
    )
    low, state, keep, give = call(
        norm_kernel,
        [VMEM] * 5,
        [query_act, out_grad, attended, near, far],
        [square, states, halves, halves],
        "norm_grad",
    )
    near, far, (value_part, query_grad, key_part) = exclusive(
        keep,
        give,
        -1,
        lambda: call(
            masked_kernel, [VMEM] * 3, [query_act, key_act, low], [square_f32], "masked"
        ),
        lambda: call(
            cross_kernel,
            [VMEM] * 5,
            [query_act, key_act, value, low, state],
            [square, square_f32],
            "cross",
        ),
    )

    scale = 1.0 / math.sqrt(tok * lax.axis_size(("ctx", "fsdp")))
    half = sds((tok // 2, 512))
    full = sds((tok, 512))
    pieces = sds((width // 256, cols, 128))
    value_grad, state_grad, r, l, other = call(
        lambda *refs: first_kernel(scale, *refs),
        [VMEM] * 7,
        [key_act, value_part, near, far, value_weight, w_other, x_near],
        [square, states, half, half, pieces],
        "value_grad",
    )
    r, l = along_z(r, 1), along_z(l, -1)
    got = swap(other)
    threes, mine = call(
        lambda *refs: work_kernel(scale, *refs),
        [VMEM] * 4,
        [value_grad, value_weight, w_other, x_near],
        [sds((2, tok, 512)), pieces],
        "work",
    )
    r, l = call(open_turn_kernel, [VMEM] * 3, [r, l, threes], [full] * 2, "turn")
    after = r
    r, l = along_z(r, 1), along_z(l, -1)

    square4 = (SIDE, SIDE) + mine.shape[1:]
    piece = sds((SIDE, cols // 2, 128))
    ru2, lv2, rv1, lu1, cu1, cv1, own = call(
        chip_kernel,
        [VMEM] * 2 + [ANY],
        [mine.reshape(square4), got.reshape(square4), after],
        [piece] * 6 + [sds((SIDE, cols, 128))],
        "chip",
    )
    ru2, lv2 = along_x_ring(ru2, 1), along_x_ring(lv2, -1)
    rv1, lu1 = along_x_ring(rv1, 1), along_x_ring(lu1, -1)
    key_grad, parts = call(
        key_grad_kernel,
        [VMEM] * 6 + [ANY],
        [value, key_part, state_grad, value_grad, value_weight, w_other, own],
        [square, sds((5, tok, 512))],
        "key_grad",
    )
    r, l, ru1, lv1 = call(
        pair_kernel,
        [VMEM] * 7,
        [r, l, parts, cu1, ru2, cv1, lv2],
        [full] * 2 + [piece] * 2,
        "pair",
    )
    r, l = along_z(r, 1), along_z(l, -1)
    ru1, lv1 = along_x_ring(ru1, 1), along_x_ring(lv1, -1)
    r, l, m1, m2, m3, keep = call(
        line_kernel,
        [VMEM] * 8,
        [r, l, parts, own, ru1, lu1, rv1, lv1],
        [full] * 2 + [sds((cols, 128))] * 3 + [sds((cols, 128), F32)],
        "line",
    )
    r, l = along_z(r, 1), along_z(l, -1)
    got = [along_y_ring(m, k) for m, k in zip((m1, m2, m3), (1, 2, 3))]
    weight_grad, input_grad = call(
        last_kernel,
        [VMEM] * 7,
        [keep, *got, r, l, parts],
        [sds((128, cols), F32), full],
        "last",
    )
    return (query_grad, key_grad, input_grad, weight_grad)


def solution(mesh):
    in_specs = (
        P(("ctx", "fsdp"), None),
        P(("ctx", "fsdp"), "head"),
        P(("ctx", "fsdp"), "head"),
        P(("ctx", "fsdp"), "head"),
        P("fsdp", "head"),
    )
    out_specs = (
        P(("ctx", "fsdp"), "head"),
        P(("ctx", "fsdp"), "head"),
        P(("ctx", "fsdp"), "head"),
        P(("ctx", "fsdp"), "head"),
    )
    return jax.shard_map(local, mesh=mesh, in_specs=in_specs, out_specs=out_specs, check_vma=False)
```

```python
import math

import jax
import jax.numpy as jnp
from jax import lax
from jax.experimental import pallas as pl
from jax.experimental.pallas import tpu as pltpu
from jax.sharding import PartitionSpec as P

HDIM = 128
SIDE = 4
RING = 8
F32 = jnp.float32
BF16 = jnp.bfloat16
NT = (((1,), (1,)), ((), ()))
TN = (((0,), (0,)), ((), ()))
NN = (((1,), (0,)), ((), ()))

VMEM = pl.BlockSpec(memory_space=pltpu.VMEM)
ANY = pl.BlockSpec(memory_space=pl.ANY)
HBM = pl.BlockSpec(memory_space=pltpu.HBM)


def dot(a, b, dims=NN):
    return lax.dot_general(a, b, dims, preferred_element_type=F32)


def sds(shape, dtype=BF16):
    return jax.ShapeDtypeStruct(shape, dtype)


def core():
    return lax.axis_index("fsdp")


def place():
    at = lax.axis_index("ctx")
    return at // SIDE, lax.rem(at, SIDE)


def dest(which):
    i = which - 1
    hop = jnp.where(i % 2 == 0, 3 - i // 2, 5 + i // 2)
    return lax.rem(lax.axis_index("head") + hop, RING)


def wide(ref):
    return ref[...].astype(F32)


def call(body, specs, ins, outs, name, scratch=(), limit=16):
    return pl.pallas_call(
        body,
        out_shape=tuple(outs),
        in_specs=specs,
        out_specs=tuple([VMEM] * len(outs)),
        scratch_shapes=list(scratch),
        compiler_params=pltpu.CompilerParams(vmem_limit_bytes=limit * 2**20),
        cost_estimate=pl.CostEstimate(
            flops=1000,
            bytes_accessed=sum(a.size * a.dtype.itemsize for a in ins)
            + sum(math.prod(o.shape) * o.dtype.itemsize for o in outs),
            transcendentals=0,
        ),
        name=name,
    )(*ins)


def in_hbm(a):
    return pltpu.with_memory_space_constraint(a, pltpu.HBM)


def heads_of(ref):
    return [slice(h, h + HDIM) for h in range(0, ref.shape[1], HDIM)]


def each_head(ref, body):
    @pl.loop(0, ref.shape[1] // (2 * HDIM))
    def _(pair):
        for h in range(2):
            body(pl.ds(pl.multiple_of((2 * pair + h) * HDIM, HDIM), HDIM))


def tril(scores):
    rows = lax.broadcasted_iota(jnp.int32, scores.shape, 0)
    cols = lax.broadcasted_iota(jnp.int32, scores.shape, 1)
    return jnp.where(rows >= cols, scores, 0.0).astype(BF16)


def value_own_kernel(x_hbm, w_hbm, x_ref, part_ref, w_ref, sems):
    step = 512
    n = x_hbm.shape[1] // step
    half = n // 2

    def x_cols(j):
        return pl.ds(pl.multiple_of(lax.rem(core() * half + j, n) * step, step), step)

    xs = [
        pltpu.make_async_copy(x_hbm.at[:, x_cols(j)], x_ref.at[:, x_cols(j)], sems.at[j])
        for j in range(n)
    ]
    ws = [
        pltpu.make_async_copy(
            w_hbm.at[pl.ds(j * step, step), :], w_ref.at[pl.ds(j * step, step), :], sems.at[n + j]
        )
        for j in range(half)
    ]
    for j in range(half):
        ws[j].start()
        xs[j].start()
    for j in range(half, n):
        xs[j].start()
    for j in range(half):
        ws[j].wait()
        xs[j].wait()
        prod = dot(x_ref[:, x_cols(j)], w_ref[j * step : (j + 1) * step, :])
        if j == 0:
            part_ref[...] = prod
        else:
            part_ref[...] += prod
    for j in range(half, n):
        xs[j].wait()


def split(rows, keep_ref, give_ref):
    half = keep_ref.shape[0]
    for h, state in enumerate(rows):
        to = (h * HDIM) // half

        @pl.when(core() == to)
        def _():
            keep_ref[h * HDIM - to * half : (h + 1) * HDIM - to * half, :] = state

        @pl.when(core() != to)
        def _():
            give_ref[h * HDIM - to * half : (h + 1) * HDIM - to * half, :] = state


def join(near_ref, far_ref, state_ref):
    half = near_ref.shape[0]
    mine = pl.ds(pl.multiple_of(core() * half, half), half)
    other = pl.ds(pl.multiple_of((1 - core()) * half, half), half)
    state_ref[mine, :] = near_ref[...].astype(BF16)
    state_ref[other, :] = far_ref[...]


def value_rest_kernel(x_ref, w_ref, part_ref, k_ref, v_ref, keep_ref, give_ref):
    rows = w_ref.shape[0]
    cols = pl.ds(pl.multiple_of((1 - core()) * rows, rows), rows)
    v = (part_ref[...] + dot(x_ref[:, cols], w_ref[...])).astype(BF16)
    v_ref[...] = v
    pairs = [dot(k_ref[:, c], v[:, c], TN).astype(BF16) for c in heads_of(v_ref)]
    split(pairs, keep_ref, give_ref)


def inside_kernel(q_ref, k_ref, v_ref, a_ref):
    def head(c):
        a_ref[:, c] = dot(tril(dot(q_ref[:, c], k_ref[:, c], NT)), v_ref[:, c])

    each_head(q_ref, head)


def norm_kernel(q_ref, g_ref, a_ref, near_ref, far_ref, low_ref, state_ref, keep_ref, give_ref):
    join(near_ref, far_ref, state_ref)
    local = []
    for c in heads_of(q_ref):
        att = a_ref[:, c] + dot(q_ref[:, c], state_ref[c, :])
        inv = lax.rsqrt(jnp.mean(att * att, axis=-1, keepdims=True) + 1e-05)
        normed = att * inv
        g = g_ref[:, c].astype(F32)
        low = (inv * (g - normed * jnp.mean(g * normed, axis=-1, keepdims=True))).astype(BF16)
        low_ref[:, c] = low
        local.append(dot(q_ref[:, c], low, TN).astype(BF16))
    split(local, keep_ref, give_ref)


def masked_kernel(q_ref, k_ref, low_ref, vp_ref):
    def head(c):
        vp_ref[:, c] = dot(tril(dot(q_ref[:, c], k_ref[:, c], NT)), low_ref[:, c], TN)

    each_head(q_ref, head)


def cross_kernel(q_ref, k_ref, v_ref, low_ref, state_ref, qg_ref, kp_ref):
    def head(c):
        low = low_ref[:, c]
        cross = tril(dot(low, v_ref[:, c], NT))
        qg_ref[:, c] = (dot(cross, k_ref[:, c]) + dot(low, state_ref[c, :], NT)).astype(BF16)
        kp_ref[:, c] = dot(cross, q_ref[:, c], TN)

    each_head(q_ref, head)


def chip_sum_kernel(keep_ref, got_ref, _, t_ref):
    t_ref[...] = (wide(keep_ref) + wide(got_ref)).astype(BF16)


def pair_sum_kernel(a_ref, b_ref, _, t_ref):
    t_ref[...] = (wide(a_ref) + wide(b_ref)).astype(BF16)


def part_before(sign, at, beside, across):
    if sign == -1:
        at = SIDE - 1 - at
    return jnp.where(at % 2 == 1, beside, 0.0) + jnp.where(at >= SIDE // 2, across, 0.0)


def last_sum_kernel(sign, keep_ref, got_ref, y1, y2, x1, x2, near_ref, far_ref):
    x, y = place()
    before = part_before(sign, y, wide(y1), wide(y2)) + part_before(sign, x, wide(x1), wide(x2))
    lead = core() == (0 if sign == 1 else 1)
    near_ref[...] = jnp.where(lead, before, before + wide(got_ref))
    far_ref[...] = jnp.where(lead, before + wide(keep_ref), before).astype(BF16)


def along(a, axis, beside):
    def other(i):
        x, y = i // SIDE, i % SIDE
        if axis == "x":
            x = x ^ 1 if beside else SIDE - 1 - x
        else:
            y = y ^ 1 if beside else SIDE - 1 - y
        return x * SIDE + y

    return lax.ppermute(a, "ctx", [(i, other(i)) for i in range(SIDE * SIDE)])


def along_x_ring(a, k):
    return lax.ppermute(a, "ctx", [(i, (i + SIDE * k) % 16) for i in range(16)])


def along_y_ring(a, k):
    return lax.ppermute(
        a, "ctx", [(i, i // SIDE * SIDE + (i + k) % SIDE) for i in range(16)]
    )


def along_z(a, k):
    return lax.ppermute(a, "head", [(i, (i + k) % RING) for i in range(RING)])


def swap(a):
    return lax.ppermute(a, "fsdp", [(0, 1), (1, 0)])


def exclusive(keep, give, sign, first, second=lambda: ()):
    shape = sds(keep.shape)

    def fold(kernel, *arrays):
        (t,) = call(kernel, [VMEM] * len(arrays), arrays, [shape], "fold")
        return t

    got = swap(give)
    t = fold(chip_sum_kernel, keep, got, keep)
    y1 = along(t, "y", True)
    done = list(first())
    t = fold(pair_sum_kernel, t, y1, done[0])
    y2 = along(t, "y", False)
    done += list(second())
    t = fold(pair_sum_kernel, t, y2, done[-1])
    x1 = along(t, "x", True)
    t = fold(pair_sum_kernel, t, x1, done[0])
    x2 = along(t, "x", False)
    near, far = call(
        lambda *refs: last_sum_kernel(sign, *refs),
        [VMEM] * 6,
        [keep, got, y1, y2, x1, x2],
        [sds(keep.shape, F32), shape],
        "last_sum",
    )
    return near, swap(far), done


def chunk_product(which, vg, own_ref, other_ref, use):
    rows = pl.ds(pl.multiple_of(lax.rem(dest(which), RING // 2) * 512, 512), 512)
    mine = dest(which) // (RING // 2) == core()

    @pl.when(mine)
    def _():
        use(dot(vg, own_ref[rows, :], NT).astype(BF16))

    @pl.when(jnp.logical_not(mine))
    def _():
        use(dot(vg, other_ref[rows, :], NT).astype(BF16))


def first_kernel(scale, k_ref, vp_ref, near_ref, far_ref, own_ref, other_ref, x_ref, vg_ref, state_ref, right_ref, left_ref, piece_ref):
    join(near_ref, far_ref, state_ref)
    for c in heads_of(k_ref):
        vg_ref[:, c] = (vp_ref[:, c] + dot(k_ref[:, c], state_ref[c, :])).astype(BF16)
    half = right_ref.shape[0]

    def use(p):
        right_ref[...] = p[:half]
        left_ref[...] = p[half:]

    chunk_product(0, vg_ref[...], own_ref, other_ref, use)
    weight_pieces(scale, 1 - core(), vg_ref, x_ref, piece_ref)


def chunks(first, vg_ref, own_ref, other_ref, p_ref):
    @pl.loop(0, p_ref.shape[0])
    def _(i):
        def use(p):
            p_ref[i] = p

        chunk_product(first + i, vg_ref[...], own_ref, other_ref, use)


def work_kernel(scale, vg_ref, own_ref, other_ref, x_ref, p_ref, piece_ref):
    chunks(1, vg_ref, own_ref, other_ref, p_ref)
    weight_pieces(scale, core(), vg_ref, x_ref, piece_ref)


def open_turn_kernel(r_ref, l_ref, p_ref, ro_ref, lo_ref):
    half = r_ref.shape[0]
    ro_ref[:half] = (wide(r_ref) + p_ref[0, :half].astype(F32)).astype(BF16)
    ro_ref[half:] = p_ref[0, half:]
    lo_ref[:half] = p_ref[1, :half]
    lo_ref[half:] = (wide(l_ref) + p_ref[1, half:].astype(F32)).astype(BF16)


def turn(first, r_ref, l_ref, p_ref, ro_ref, lo_ref):
    ro_ref[...] = (wide(r_ref) + p_ref[first].astype(F32)).astype(BF16)
    lo_ref[...] = (wide(l_ref) + p_ref[first + 1].astype(F32)).astype(BF16)


def key_grad_kernel(v_ref, kp_ref, state_ref, vg_ref, own_ref, other_ref, _, kg_ref, p_ref):
    def head(c):
        kg_ref[:, c] = (kp_ref[:, c] + dot(v_ref[:, c], state_ref[c, :], NT)).astype(BF16)

    each_head(v_ref, head)
    chunks(3, vg_ref, own_ref, other_ref, p_ref)


def weight_pieces(scale, side, vg_ref, x_ref, o_ref):
    turned = vg_ref[...].T
    shift = side * 128
    for first in range(0, o_ref.shape[0], 4):
        x = jnp.concatenate(
            [
                x_ref[:, pl.ds(pl.multiple_of((first + p) * 256 + shift, 128), 128)]
                for p in range(4)
            ],
            axis=1,
        )
        res = (dot(turned, x) * scale).astype(BF16)
        for p in range(4):
            o_ref[first + p] = res[:, p * 128 : p * 128 + 128]


def chip_kernel(a_ref, b_ref, _, right, left, cu1, cv1, own):
    half = own.shape[1] // 2

    x, _ = place()

    def s(hop):
        i = lax.rem(x + hop, SIDE)
        return (a_ref[i].astype(F32) + b_ref[i].astype(F32)).astype(BF16)

    t = s(2)
    right[0] = t[:, :half]
    left[0] = t[:, half:]
    t = s(1)
    cu1[...] = t[:, :half]
    right[1] = t[:, half:]
    t = s(3)
    left[1] = t[:, :half]
    cv1[...] = t[:, half:]
    own[...] = s(0)


def pair_kernel(r_ref, l_ref, p_ref, a_ref, b_ref, c_ref, d_ref, ro_ref, lo_ref, o_ref, q_ref):
    turn(0, r_ref, l_ref, p_ref, ro_ref, lo_ref)
    o_ref[...] = (wide(a_ref) + b_ref[0].astype(F32)).astype(BF16)
    q_ref[...] = (wide(c_ref) + d_ref[0].astype(F32)).astype(BF16)


def line_kernel(r_ref, l_ref, p_ref, own_ref, ru_ref, left_ref, right_ref, lv_ref, ro_ref, lo_ref, m1, m2, m3, keep):
    turn(2, r_ref, l_ref, p_ref, ro_ref, lo_ref)
    half = ru_ref.shape[1]
    _, y = place()
    for hop, ref in ((1, m1), (2, m2), (3, m3), (0, keep)):
        i = lax.rem(y + hop, SIDE)
        own = own_ref[i].astype(F32)
        u = own[:half] + ru_ref[i].astype(F32) + left_ref[1, i].astype(F32)
        v = own[half:] + right_ref[1, i].astype(F32) + lv_ref[i].astype(F32)
        ref[:half] = u.astype(ref.dtype)
        ref[half:] = v.astype(ref.dtype)


def last_kernel(keep_ref, a_ref, b_ref, c_ref, r_ref, l_ref, p_ref, o_ref, i_ref):
    i_ref[...] = (p_ref[p_ref.shape[0] - 1].astype(F32) + wide(r_ref) + wide(l_ref)).astype(BF16)
    o_ref[...] = (keep_ref[...] + wide(a_ref) + wide(b_ref) + wide(c_ref)).T


def local(layer_input, query_act, key_act, out_grad, value_weight):
    tok, width = layer_input.shape
    rows, cols = value_weight.shape
    square = sds((tok, cols))
    square_f32 = sds((tok, cols), F32)
    states = sds((cols, HDIM))

    w_other = swap(value_weight)
    x_near, part = call(
        value_own_kernel,
        [HBM, HBM],
        [in_hbm(layer_input), in_hbm(value_weight)],
        [sds((tok, width)), square_f32],
        "value_own",
        scratch=[pltpu.VMEM((rows, cols), BF16), pltpu.SemaphoreType.DMA((width // 512 + rows // 512,))],
    )
    halves = sds((cols // 2, HDIM))
    value, keep, give = call(
        value_rest_kernel,
        [VMEM] * 4,
        [x_near, w_other, part, key_act],
        [square, halves, halves],
        "value_rest",
    )
    near, far, (attended,) = exclusive(
        keep,
        give,
        1,
        lambda: call(
            inside_kernel,
            [VMEM] * 3,
            [query_act, key_act, value],
            [square_f32],
            "inside",
        ),
    )
    low, state, keep, give = call(
        norm_kernel,
        [VMEM] * 5,
        [query_act, out_grad, attended, near, far],
        [square, states, halves, halves],
        "norm_grad",
    )
    near, far, (value_part, query_grad, key_part) = exclusive(
        keep,
        give,
        -1,
        lambda: call(
            masked_kernel, [VMEM] * 3, [query_act, key_act, low], [square_f32], "masked"
        ),
        lambda: call(
            cross_kernel,
            [VMEM] * 5,
            [query_act, key_act, value, low, state],
            [square, square_f32],
            "cross",
        ),
    )

    scale = 1.0 / math.sqrt(tok * lax.axis_size(("ctx", "fsdp")))
    half = sds((tok // 2, 512))
    full = sds((tok, 512))
    pieces = sds((width // 256, cols, 128))
    value_grad, state_grad, r, l, other = call(
        lambda *refs: first_kernel(scale, *refs),
        [VMEM] * 7,
        [key_act, value_part, near, far, value_weight, w_other, x_near],
        [square, states, half, half, pieces],
        "value_grad",
    )
    r, l = along_z(r, 1), along_z(l, -1)
    got = swap(other)
    threes, mine = call(
        lambda *refs: work_kernel(scale, *refs),
        [VMEM] * 4,
        [value_grad, value_weight, w_other, x_near],
        [sds((2, tok, 512)), pieces],
        "work",
    )
    r, l = call(open_turn_kernel, [VMEM] * 3, [r, l, threes], [full] * 2, "turn")
    after = r
    r, l = along_z(r, 1), along_z(l, -1)

    square4 = (SIDE, SIDE) + mine.shape[1:]
    piece = sds((SIDE, cols // 2, 128))
    two_pieces = sds((2,) + piece.shape)
    right, left, cu1, cv1, own = call(
        chip_kernel,
        [VMEM] * 2 + [ANY],
        [mine.reshape(square4), got.reshape(square4), after],
        [two_pieces] * 2 + [piece] * 2 + [sds((SIDE, cols, 128))],
        "chip",
    )
    right, left = along_x_ring(right, 1), along_x_ring(left, -1)
    key_grad, parts = call(
        key_grad_kernel,
        [VMEM] * 6 + [ANY],
        [value, key_part, state_grad, value_grad, value_weight, w_other, own],
        [square, sds((5, tok, 512))],
        "key_grad",
    )
    r, l, ru1, lv1 = call(
        pair_kernel,
        [VMEM] * 7,
        [r, l, parts, cu1, right, cv1, left],
        [full] * 2 + [piece] * 2,
        "pair",
    )
    r, l = along_z(r, 1), along_z(l, -1)
    ru1, lv1 = along_x_ring(ru1, 1), along_x_ring(lv1, -1)
    r, l, m1, m2, m3, keep = call(
        line_kernel,
        [VMEM] * 8,
        [r, l, parts, own, ru1, left, right, lv1],
        [full] * 2 + [sds((cols, 128))] * 3 + [sds((cols, 128), F32)],
        "line",
    )
    r, l = along_z(r, 1), along_z(l, -1)
    got = [along_y_ring(m, k) for m, k in zip((m1, m2, m3), (1, 2, 3))]
    weight_grad, input_grad = call(
        last_kernel,
        [VMEM] * 7,
        [keep, *got, r, l, parts],
        [sds((128, cols), F32), full],
        "last",
    )
    return (query_grad, key_grad, input_grad, weight_grad)


def solution(mesh):
    in_specs = (
        P(("ctx", "fsdp"), None),
        P(("ctx", "fsdp"), "head"),
        P(("ctx", "fsdp"), "head"),
        P(("ctx", "fsdp"), "head"),
        P("fsdp", "head"),
    )
    out_specs = (
        P(("ctx", "fsdp"), "head"),
        P(("ctx", "fsdp"), "head"),
        P(("ctx", "fsdp"), "head"),
        P(("ctx", "fsdp"), "head"),
    )
    return jax.shard_map(local, mesh=mesh, in_specs=in_specs, out_specs=out_specs, check_vma=False)
```

```python
import math

import jax
import jax.numpy as jnp
from jax import lax
from jax.experimental import pallas as pl
from jax.experimental.pallas import tpu as pltpu
from jax.sharding import PartitionSpec as P

HDIM = 128
SIDE = 4
RING = 8
F32 = jnp.float32
BF16 = jnp.bfloat16
NT = (((1,), (1,)), ((), ()))
TN = (((0,), (0,)), ((), ()))
NN = (((1,), (0,)), ((), ()))

VMEM = pl.BlockSpec(memory_space=pltpu.VMEM)
ANY = pl.BlockSpec(memory_space=pl.ANY)
HBM = pl.BlockSpec(memory_space=pltpu.HBM)


def dot(a, b, dims=NN):
    return lax.dot_general(a, b, dims, preferred_element_type=F32)


def sds(shape, dtype=BF16):
    return jax.ShapeDtypeStruct(shape, dtype)


def core():
    return lax.axis_index("fsdp")


def place():
    at = lax.axis_index("ctx")
    return at // SIDE, lax.rem(at, SIDE)


def dest(which):
    i = which - 1
    hop = jnp.where(i % 2 == 0, 3 - i // 2, 5 + i // 2)
    return lax.rem(lax.axis_index("head") + hop, RING)


def wide(ref):
    return ref[...].astype(F32)


def call(body, specs, ins, outs, name, scratch=(), limit=16):
    return pl.pallas_call(
        body,
        out_shape=tuple(outs),
        in_specs=specs,
        out_specs=tuple([VMEM] * len(outs)),
        scratch_shapes=list(scratch),
        compiler_params=pltpu.CompilerParams(vmem_limit_bytes=limit * 2**20),
        cost_estimate=pl.CostEstimate(
            flops=1000,
            bytes_accessed=sum(a.size * a.dtype.itemsize for a in ins)
            + sum(math.prod(o.shape) * o.dtype.itemsize for o in outs),
            transcendentals=0,
        ),
        name=name,
    )(*ins)


def in_hbm(a):
    return pltpu.with_memory_space_constraint(a, pltpu.HBM)


def heads_of(ref):
    return [slice(h, h + HDIM) for h in range(0, ref.shape[1], HDIM)]


def each_head(ref, body):
    @pl.loop(0, ref.shape[1] // (2 * HDIM))
    def _(pair):
        for h in range(2):
            body(pl.ds(pl.multiple_of((2 * pair + h) * HDIM, HDIM), HDIM))


def tril(scores):
    rows = lax.broadcasted_iota(jnp.int32, scores.shape, 0)
    cols = lax.broadcasted_iota(jnp.int32, scores.shape, 1)
    return jnp.where(rows >= cols, scores, 0.0).astype(BF16)


def value_own_kernel(x_hbm, w_hbm, x_ref, part_ref, w_ref, sems):
    step = 512
    n = x_hbm.shape[1] // step
    half = n // 2

    def x_cols(j):
        return pl.ds(pl.multiple_of(lax.rem(core() * half + j, n) * step, step), step)

    xs = [
        pltpu.make_async_copy(x_hbm.at[:, x_cols(j)], x_ref.at[:, x_cols(j)], sems.at[j])
        for j in range(n)
    ]
    ws = [
        pltpu.make_async_copy(
            w_hbm.at[pl.ds(j * step, step), :], w_ref.at[pl.ds(j * step, step), :], sems.at[n + j]
        )
        for j in range(half)
    ]
    for j in range(half):
        ws[j].start()
        xs[j].start()
    for j in range(half, n):
        xs[j].start()
    for j in range(half):
        ws[j].wait()
        xs[j].wait()
        prod = dot(x_ref[:, x_cols(j)], w_ref[j * step : (j + 1) * step, :])
        if j == 0:
            part_ref[...] = prod
        else:
            part_ref[...] += prod
    for j in range(half, n):
        xs[j].wait()


def split(rows, keep_ref, give_ref):
    half = keep_ref.shape[0]
    for h, state in enumerate(rows):
        to = (h * HDIM) // half

        @pl.when(core() == to)
        def _():
            keep_ref[h * HDIM - to * half : (h + 1) * HDIM - to * half, :] = state

        @pl.when(core() != to)
        def _():
            give_ref[h * HDIM - to * half : (h + 1) * HDIM - to * half, :] = state


def join(near_ref, far_ref, state_ref):
    half = near_ref.shape[0]
    mine = pl.ds(pl.multiple_of(core() * half, half), half)
    other = pl.ds(pl.multiple_of((1 - core()) * half, half), half)
    state_ref[mine, :] = near_ref[...].astype(BF16)
    state_ref[other, :] = far_ref[...]


def value_rest_kernel(x_ref, w_ref, part_ref, k_ref, v_ref, keep_ref, give_ref):
    rows = w_ref.shape[0]
    cols = pl.ds(pl.multiple_of((1 - core()) * rows, rows), rows)
    v = (part_ref[...] + dot(x_ref[:, cols], w_ref[...])).astype(BF16)
    v_ref[...] = v
    pairs = [dot(k_ref[:, c], v[:, c], TN).astype(BF16) for c in heads_of(v_ref)]
    split(pairs, keep_ref, give_ref)


def inside_kernel(q_ref, k_ref, v_ref, a_ref):
    def head(c):
        a_ref[:, c] = dot(tril(dot(q_ref[:, c], k_ref[:, c], NT)), v_ref[:, c])

    each_head(q_ref, head)


def norm_kernel(q_ref, g_ref, a_ref, near_ref, far_ref, low_ref, state_ref, keep_ref, give_ref):
    join(near_ref, far_ref, state_ref)
    local = []
    for c in heads_of(q_ref):
        att = a_ref[:, c] + dot(q_ref[:, c], state_ref[c, :])
        inv = lax.rsqrt(jnp.mean(att * att, axis=-1, keepdims=True) + 1e-05)
        normed = att * inv
        g = g_ref[:, c].astype(F32)
        low = (inv * (g - normed * jnp.mean(g * normed, axis=-1, keepdims=True))).astype(BF16)
        low_ref[:, c] = low
        local.append(dot(q_ref[:, c], low, TN).astype(BF16))
    split(local, keep_ref, give_ref)


def masked_kernel(q_ref, k_ref, low_ref, vp_ref):
    def head(c):
        vp_ref[:, c] = dot(tril(dot(q_ref[:, c], k_ref[:, c], NT)), low_ref[:, c], TN)

    each_head(q_ref, head)


def cross_kernel(q_ref, k_ref, v_ref, low_ref, state_ref, qg_ref, kp_ref):
    def head(c):
        low = low_ref[:, c]
        cross = tril(dot(low, v_ref[:, c], NT))
        qg_ref[:, c] = (dot(cross, k_ref[:, c]) + dot(low, state_ref[c, :], NT)).astype(BF16)
        kp_ref[:, c] = dot(cross, q_ref[:, c], TN)

    each_head(q_ref, head)


def chip_sum_kernel(keep_ref, got_ref, _, t_ref):
    t_ref[...] = (wide(keep_ref) + wide(got_ref)).astype(BF16)


def pair_sum_kernel(a_ref, b_ref, _, t_ref):
    t_ref[...] = (wide(a_ref) + wide(b_ref)).astype(BF16)


def part_before(sign, at, beside, across):
    if sign == -1:
        at = SIDE - 1 - at
    return jnp.where(at % 2 == 1, beside, 0.0) + jnp.where(at >= SIDE // 2, across, 0.0)


def last_sum_kernel(sign, keep_ref, got_ref, y1, y2, x1, x2, near_ref, far_ref):
    x, y = place()
    before = part_before(sign, y, wide(y1), wide(y2)) + part_before(sign, x, wide(x1), wide(x2))
    lead = core() == (0 if sign == 1 else 1)
    near_ref[...] = jnp.where(lead, before, before + wide(got_ref))
    far_ref[...] = jnp.where(lead, before + wide(keep_ref), before).astype(BF16)


def along(a, axis, beside):
    def other(i):
        x, y = i // SIDE, i % SIDE
        if axis == "x":
            x = x ^ 1 if beside else SIDE - 1 - x
        else:
            y = y ^ 1 if beside else SIDE - 1 - y
        return x * SIDE + y

    return lax.ppermute(a, "ctx", [(i, other(i)) for i in range(SIDE * SIDE)])


def along_x_ring(a, k):
    return lax.ppermute(a, "ctx", [(i, (i + SIDE * k) % 16) for i in range(16)])


def along_y_ring(a, k):
    return lax.ppermute(
        a, "ctx", [(i, i // SIDE * SIDE + (i + k) % SIDE) for i in range(16)]
    )


def along_z(a, k):
    return lax.ppermute(a, "head", [(i, (i + k) % RING) for i in range(RING)])


def swap(a):
    return lax.ppermute(a, "fsdp", [(0, 1), (1, 0)])


def exclusive(keep, give, sign, first, second=lambda: ()):
    shape = sds(keep.shape)

    def fold(kernel, *arrays):
        (t,) = call(kernel, [VMEM] * len(arrays), arrays, [shape], "fold")
        return t

    got = swap(give)
    t = fold(chip_sum_kernel, keep, got, keep)
    y1 = along(t, "y", True)
    done = list(first())
    t = fold(pair_sum_kernel, t, y1, done[0])
    y2 = along(t, "y", False)
    done += list(second())
    t = fold(pair_sum_kernel, t, y2, done[-1])
    x1 = along(t, "x", True)
    t = fold(pair_sum_kernel, t, x1, done[0])
    x2 = along(t, "x", False)
    near, far = call(
        lambda *refs: last_sum_kernel(sign, *refs),
        [VMEM] * 6,
        [keep, got, y1, y2, x1, x2],
        [sds(keep.shape, F32), shape],
        "last_sum",
    )
    return near, swap(far), done


def chunk_product(which, vg, own_ref, other_ref, use):
    rows = pl.ds(pl.multiple_of(lax.rem(dest(which), RING // 2) * 512, 512), 512)
    mine = dest(which) // (RING // 2) == core()

    @pl.when(mine)
    def _():
        use(dot(vg, own_ref[rows, :], NT).astype(BF16))

    @pl.when(jnp.logical_not(mine))
    def _():
        use(dot(vg, other_ref[rows, :], NT).astype(BF16))


def first_kernel(scale, k_ref, vp_ref, near_ref, far_ref, own_ref, other_ref, x_ref, vg_ref, state_ref, right_ref, left_ref, piece_ref):
    join(near_ref, far_ref, state_ref)
    for c in heads_of(k_ref):
        vg_ref[:, c] = (vp_ref[:, c] + dot(k_ref[:, c], state_ref[c, :])).astype(BF16)
    half = right_ref.shape[0]

    def use(p):
        right_ref[...] = p[:half]
        left_ref[...] = p[half:]

    chunk_product(0, vg_ref[...], own_ref, other_ref, use)
    weight_pieces(scale, 1 - core(), vg_ref, x_ref, piece_ref)


def chunks(first, vg_ref, own_ref, other_ref, p_ref):
    @pl.loop(0, p_ref.shape[0])
    def _(i):
        def use(p):
            p_ref[i] = p

        chunk_product(first + i, vg_ref[...], own_ref, other_ref, use)


def work_kernel(scale, vg_ref, own_ref, other_ref, x_ref, p_ref, piece_ref):
    chunks(1, vg_ref, own_ref, other_ref, p_ref)
    weight_pieces(scale, core(), vg_ref, x_ref, piece_ref)


def open_turn_kernel(r_ref, l_ref, p_ref, _, ro_ref, lo_ref):
    half = r_ref.shape[0]
    ro_ref[:half] = (wide(r_ref) + p_ref[0, :half].astype(F32)).astype(BF16)
    ro_ref[half:] = p_ref[0, half:]
    lo_ref[:half] = p_ref[1, :half]
    lo_ref[half:] = (wide(l_ref) + p_ref[1, half:].astype(F32)).astype(BF16)


def turn(first, r_ref, l_ref, p_ref, ro_ref, lo_ref):
    ro_ref[...] = (wide(r_ref) + p_ref[first].astype(F32)).astype(BF16)
    lo_ref[...] = (wide(l_ref) + p_ref[first + 1].astype(F32)).astype(BF16)


def key_grad_kernel(v_ref, kp_ref, state_ref, vg_ref, own_ref, other_ref, _, kg_ref, p_ref):
    def head(c):
        kg_ref[:, c] = (kp_ref[:, c] + dot(v_ref[:, c], state_ref[c, :], NT)).astype(BF16)

    each_head(v_ref, head)
    chunks(3, vg_ref, own_ref, other_ref, p_ref)


def weight_pieces(scale, side, vg_ref, x_ref, o_ref):
    turned = vg_ref[...].T
    shift = side * 128
    for first in range(0, o_ref.shape[0], 4):
        x = jnp.concatenate(
            [
                x_ref[:, pl.ds(pl.multiple_of((first + p) * 256 + shift, 128), 128)]
                for p in range(4)
            ],
            axis=1,
        )
        res = (dot(turned, x) * scale).astype(BF16)
        for p in range(4):
            o_ref[first + p] = res[:, p * 128 : p * 128 + 128]


def chip_kernel(a_ref, b_ref, right, left, cu1, cv1, own):
    half = own.shape[1] // 2

    x, _ = place()

    def s(hop):
        i = lax.rem(x + hop, SIDE)
        return (a_ref[i].astype(F32) + b_ref[i].astype(F32)).astype(BF16)

    t = s(2)
    right[0] = t[:, :half]
    left[0] = t[:, half:]
    t = s(1)
    cu1[...] = t[:, :half]
    right[1] = t[:, half:]
    t = s(3)
    left[1] = t[:, :half]
    cv1[...] = t[:, half:]
    own[...] = s(0)


def pair_kernel(r_ref, l_ref, p_ref, a_ref, b_ref, c_ref, d_ref, ro_ref, lo_ref, o_ref, q_ref):
    turn(0, r_ref, l_ref, p_ref, ro_ref, lo_ref)
    o_ref[...] = (wide(a_ref) + b_ref[0].astype(F32)).astype(BF16)
    q_ref[...] = (wide(c_ref) + d_ref[0].astype(F32)).astype(BF16)


def line_kernel(r_ref, l_ref, p_ref, own_ref, ru_ref, left_ref, right_ref, lv_ref, ro_ref, lo_ref, m1, m2, m3, keep):
    turn(2, r_ref, l_ref, p_ref, ro_ref, lo_ref)
    half = ru_ref.shape[1]
    _, y = place()
    for hop, ref in ((1, m1), (2, m2), (3, m3), (0, keep)):
        i = lax.rem(y + hop, SIDE)
        own = own_ref[i].astype(F32)
        u = own[:half] + ru_ref[i].astype(F32) + left_ref[1, i].astype(F32)
        v = own[half:] + right_ref[1, i].astype(F32) + lv_ref[i].astype(F32)
        ref[:half] = u.astype(ref.dtype)
        ref[half:] = v.astype(ref.dtype)


def last_kernel(keep_ref, a_ref, b_ref, c_ref, r_ref, l_ref, p_ref, o_ref, i_ref):
    i_ref[...] = (p_ref[p_ref.shape[0] - 1].astype(F32) + wide(r_ref) + wide(l_ref)).astype(BF16)
    o_ref[...] = (keep_ref[...] + wide(a_ref) + wide(b_ref) + wide(c_ref)).T


def local(layer_input, query_act, key_act, out_grad, value_weight):
    tok, width = layer_input.shape
    rows, cols = value_weight.shape
    square = sds((tok, cols))
    square_f32 = sds((tok, cols), F32)
    states = sds((cols, HDIM))

    w_other = swap(value_weight)
    x_near, part = call(
        value_own_kernel,
        [HBM, HBM],
        [in_hbm(layer_input), in_hbm(value_weight)],
        [sds((tok, width)), square_f32],
        "value_own",
        scratch=[pltpu.VMEM((rows, cols), BF16), pltpu.SemaphoreType.DMA((width // 512 + rows // 512,))],
    )
    halves = sds((cols // 2, HDIM))
    value, keep, give = call(
        value_rest_kernel,
        [VMEM] * 4,
        [x_near, w_other, part, key_act],
        [square, halves, halves],
        "value_rest",
    )
    near, far, (attended,) = exclusive(
        keep,
        give,
        1,
        lambda: call(
            inside_kernel,
            [VMEM] * 3,
            [query_act, key_act, value],
            [square_f32],
            "inside",
        ),
    )
    low, state, keep, give = call(
        norm_kernel,
        [VMEM] * 5,
        [query_act, out_grad, attended, near, far],
        [square, states, halves, halves],
        "norm_grad",
    )
    near, far, (value_part, query_grad, key_part) = exclusive(
        keep,
        give,
        -1,
        lambda: call(
            masked_kernel, [VMEM] * 3, [query_act, key_act, low], [square_f32], "masked"
        ),
        lambda: call(
            cross_kernel,
            [VMEM] * 5,
            [query_act, key_act, value, low, state],
            [square, square_f32],
            "cross",
        ),
    )

    scale = 1.0 / math.sqrt(tok * lax.axis_size(("ctx", "fsdp")))
    half = sds((tok // 2, 512))
    full = sds((tok, 512))
    pieces = sds((width // 256, cols, 128))
    value_grad, state_grad, r, l, other = call(
        lambda *refs: first_kernel(scale, *refs),
        [VMEM] * 7,
        [key_act, value_part, near, far, value_weight, w_other, x_near],
        [square, states, half, half, pieces],
        "value_grad",
    )
    r, l = along_z(r, 1), along_z(l, -1)
    got = swap(other)
    threes, mine = call(
        lambda *refs: work_kernel(scale, *refs),
        [VMEM] * 4,
        [value_grad, value_weight, w_other, x_near],
        [sds((2, tok, 512)), pieces],
        "work",
    )
    square4 = (SIDE, SIDE) + mine.shape[1:]
    piece = sds((SIDE, cols // 2, 128))
    two_pieces = sds((2,) + piece.shape)
    right, left, cu1, cv1, own = call(
        chip_kernel,
        [VMEM] * 2,
        [mine.reshape(square4), got.reshape(square4)],
        [two_pieces] * 2 + [piece] * 2 + [sds((SIDE, cols, 128))],
        "chip",
    )
    right, left = along_x_ring(right, 1), along_x_ring(left, -1)
    r, l = call(open_turn_kernel, [VMEM] * 3 + [ANY], [r, l, threes, own], [full] * 2, "turn")
    after = r
    r, l = along_z(r, 1), along_z(l, -1)
    key_grad, parts = call(
        key_grad_kernel,
        [VMEM] * 6 + [ANY],
        [value, key_part, state_grad, value_grad, value_weight, w_other, after],
        [square, sds((5, tok, 512))],
        "key_grad",
    )
    r, l, ru1, lv1 = call(
        pair_kernel,
        [VMEM] * 7,
        [r, l, parts, cu1, right, cv1, left],
        [full] * 2 + [piece] * 2,
        "pair",
    )
    r, l = along_z(r, 1), along_z(l, -1)
    ru1, lv1 = along_x_ring(ru1, 1), along_x_ring(lv1, -1)
    r, l, m1, m2, m3, keep = call(
        line_kernel,
        [VMEM] * 8,
        [r, l, parts, own, ru1, left, right, lv1],
        [full] * 2 + [sds((cols, 128))] * 3 + [sds((cols, 128), F32)],
        "line",
    )
    r, l = along_z(r, 1), along_z(l, -1)
    got = [along_y_ring(m, k) for m, k in zip((m1, m2, m3), (1, 2, 3))]
    weight_grad, input_grad = call(
        last_kernel,
        [VMEM] * 7,
        [keep, *got, r, l, parts],
        [sds((128, cols), F32), full],
        "last",
    )
    return (query_grad, key_grad, input_grad, weight_grad)


def solution(mesh):
    in_specs = (
        P(("ctx", "fsdp"), None),
        P(("ctx", "fsdp"), "head"),
        P(("ctx", "fsdp"), "head"),
        P(("ctx", "fsdp"), "head"),
        P("fsdp", "head"),
    )
    out_specs = (
        P(("ctx", "fsdp"), "head"),
        P(("ctx", "fsdp"), "head"),
        P(("ctx", "fsdp"), "head"),
        P(("ctx", "fsdp"), "head"),
    )
    return jax.shard_map(local, mesh=mesh, in_specs=in_specs, out_specs=out_specs, check_vma=False)
```

```python
import math

import jax
import jax.numpy as jnp
from jax import lax
from jax.experimental import pallas as pl
from jax.experimental.pallas import tpu as pltpu
from jax.sharding import PartitionSpec as P

HDIM = 128
SIDE = 4
RING = 8
F32 = jnp.float32
BF16 = jnp.bfloat16
NT = (((1,), (1,)), ((), ()))
TN = (((0,), (0,)), ((), ()))
NN = (((1,), (0,)), ((), ()))

VMEM = pl.BlockSpec(memory_space=pltpu.VMEM)
ANY = pl.BlockSpec(memory_space=pl.ANY)
HBM = pl.BlockSpec(memory_space=pltpu.HBM)


def dot(a, b, dims=NN):
    return lax.dot_general(a, b, dims, preferred_element_type=F32)


def sds(shape, dtype=BF16):
    return jax.ShapeDtypeStruct(shape, dtype)


def core():
    return lax.axis_index("fsdp")


def place():
    at = lax.axis_index("ctx")
    return at // SIDE, lax.rem(at, SIDE)


def dest(which):
    i = which - 1
    hop = jnp.where(i % 2 == 0, 3 - i // 2, 5 + i // 2)
    return lax.rem(lax.axis_index("head") + hop, RING)


def wide(ref):
    return ref[...].astype(F32)


def call(body, specs, ins, outs, name, scratch=(), limit=16):
    return pl.pallas_call(
        body,
        out_shape=tuple(outs),
        in_specs=specs,
        out_specs=tuple([VMEM] * len(outs)),
        scratch_shapes=list(scratch),
        compiler_params=pltpu.CompilerParams(vmem_limit_bytes=limit * 2**20),
        cost_estimate=pl.CostEstimate(
            flops=1000,
            bytes_accessed=sum(a.size * a.dtype.itemsize for a in ins)
            + sum(math.prod(o.shape) * o.dtype.itemsize for o in outs),
            transcendentals=0,
        ),
        name=name,
    )(*ins)


def in_hbm(a):
    return pltpu.with_memory_space_constraint(a, pltpu.HBM)


def heads_of(ref):
    return [slice(h, h + HDIM) for h in range(0, ref.shape[1], HDIM)]


def each_head(ref, body):
    @pl.loop(0, ref.shape[1] // (2 * HDIM))
    def _(pair):
        for h in range(2):
            body(pl.ds(pl.multiple_of((2 * pair + h) * HDIM, HDIM), HDIM))


def tril(scores):
    rows = lax.broadcasted_iota(jnp.int32, scores.shape, 0)
    cols = lax.broadcasted_iota(jnp.int32, scores.shape, 1)
    return jnp.where(rows >= cols, scores, 0.0).astype(BF16)


def value_own_kernel(x_hbm, w_hbm, x_ref, part_ref, w_ref, sems):
    step = 512
    n = x_hbm.shape[1] // step
    half = n // 2

    def x_cols(j):
        return pl.ds(pl.multiple_of(lax.rem(core() * half + j, n) * step, step), step)

    xs = [
        pltpu.make_async_copy(x_hbm.at[:, x_cols(j)], x_ref.at[:, x_cols(j)], sems.at[j])
        for j in range(n)
    ]
    ws = [
        pltpu.make_async_copy(
            w_hbm.at[pl.ds(j * step, step), :], w_ref.at[pl.ds(j * step, step), :], sems.at[n + j]
        )
        for j in range(half)
    ]
    for j in range(half):
        ws[j].start()
        xs[j].start()
    for j in range(half, n):
        xs[j].start()
    for j in range(half):
        ws[j].wait()
        xs[j].wait()
        prod = dot(x_ref[:, x_cols(j)], w_ref[j * step : (j + 1) * step, :])
        if j == 0:
            part_ref[...] = prod
        else:
            part_ref[...] += prod
    for j in range(half, n):
        xs[j].wait()


def split(rows, keep_ref, give_ref):
    half = keep_ref.shape[0]
    for h, state in enumerate(rows):
        to = (h * HDIM) // half

        @pl.when(core() == to)
        def _():
            keep_ref[h * HDIM - to * half : (h + 1) * HDIM - to * half, :] = state

        @pl.when(core() != to)
        def _():
            give_ref[h * HDIM - to * half : (h + 1) * HDIM - to * half, :] = state


def join(near_ref, far_ref, state_ref):
    half = near_ref.shape[0]
    mine = pl.ds(pl.multiple_of(core() * half, half), half)
    other = pl.ds(pl.multiple_of((1 - core()) * half, half), half)
    state_ref[mine, :] = near_ref[...].astype(BF16)
    state_ref[other, :] = far_ref[...]


def value_rest_kernel(x_ref, w_ref, part_ref, k_ref, v_ref, keep_ref, give_ref):
    rows = w_ref.shape[0]
    cols = pl.ds(pl.multiple_of((1 - core()) * rows, rows), rows)
    v = (part_ref[...] + dot(x_ref[:, cols], w_ref[...])).astype(BF16)
    v_ref[...] = v
    pairs = [dot(k_ref[:, c], v[:, c], TN).astype(BF16) for c in heads_of(v_ref)]
    split(pairs, keep_ref, give_ref)


def inside_kernel(q_ref, k_ref, v_ref, a_ref):
    def head(c):
        a_ref[:, c] = dot(tril(dot(q_ref[:, c], k_ref[:, c], NT)), v_ref[:, c])

    each_head(q_ref, head)


def norm_kernel(q_ref, g_ref, a_ref, near_ref, far_ref, low_ref, state_ref, keep_ref, give_ref):
    join(near_ref, far_ref, state_ref)
    local = []
    for c in heads_of(q_ref):
        att = a_ref[:, c] + dot(q_ref[:, c], state_ref[c, :])
        inv = lax.rsqrt(jnp.mean(att * att, axis=-1, keepdims=True) + 1e-05)
        normed = att * inv
        g = g_ref[:, c].astype(F32)
        low = (inv * (g - normed * jnp.mean(g * normed, axis=-1, keepdims=True))).astype(BF16)
        low_ref[:, c] = low
        local.append(dot(q_ref[:, c], low, TN).astype(BF16))
    split(local, keep_ref, give_ref)


def masked_kernel(q_ref, k_ref, low_ref, vp_ref):
    def head(c):
        vp_ref[:, c] = dot(tril(dot(q_ref[:, c], k_ref[:, c], NT)), low_ref[:, c], TN)

    each_head(q_ref, head)


def cross_kernel(q_ref, k_ref, v_ref, low_ref, state_ref, qg_ref, kp_ref):
    def head(c):
        low = low_ref[:, c]
        cross = tril(dot(low, v_ref[:, c], NT))
        qg_ref[:, c] = (dot(cross, k_ref[:, c]) + dot(low, state_ref[c, :], NT)).astype(BF16)
        kp_ref[:, c] = dot(cross, q_ref[:, c], TN)

    for c in heads_of(q_ref):
        head(c)


def chip_sum_kernel(keep_ref, got_ref, _, t_ref):
    t_ref[...] = (wide(keep_ref) + wide(got_ref)).astype(BF16)


def pair_sum_kernel(a_ref, b_ref, _, t_ref):
    t_ref[...] = (wide(a_ref) + wide(b_ref)).astype(BF16)


def part_before(sign, at, beside, across):
    if sign == -1:
        at = SIDE - 1 - at
    return jnp.where(at % 2 == 1, beside, 0.0) + jnp.where(at >= SIDE // 2, across, 0.0)


def last_sum_kernel(sign, keep_ref, got_ref, y1, y2, x1, x2, near_ref, far_ref):
    x, y = place()
    before = part_before(sign, y, wide(y1), wide(y2)) + part_before(sign, x, wide(x1), wide(x2))
    lead = core() == (0 if sign == 1 else 1)
    near_ref[...] = jnp.where(lead, before, before + wide(got_ref))
    far_ref[...] = jnp.where(lead, before + wide(keep_ref), before).astype(BF16)


def along(a, axis, beside):
    def other(i):
        x, y = i // SIDE, i % SIDE
        if axis == "x":
            x = x ^ 1 if beside else SIDE - 1 - x
        else:
            y = y ^ 1 if beside else SIDE - 1 - y
        return x * SIDE + y

    return lax.ppermute(a, "ctx", [(i, other(i)) for i in range(SIDE * SIDE)])


def along_x_ring(a, k):
    return lax.ppermute(a, "ctx", [(i, (i + SIDE * k) % 16) for i in range(16)])


def along_y_ring(a, k):
    return lax.ppermute(
        a, "ctx", [(i, i // SIDE * SIDE + (i + k) % SIDE) for i in range(16)]
    )


def along_z(a, k):
    return lax.ppermute(a, "head", [(i, (i + k) % RING) for i in range(RING)])


def swap(a):
    return lax.ppermute(a, "fsdp", [(0, 1), (1, 0)])


def exclusive(keep, give, sign, first, second=lambda: ()):
    shape = sds(keep.shape)

    def fold(kernel, *arrays):
        (t,) = call(kernel, [VMEM] * len(arrays), arrays, [shape], "fold")
        return t

    got = swap(give)
    t = fold(chip_sum_kernel, keep, got, keep)
    y1 = along(t, "y", True)
    done = list(first())
    t = fold(pair_sum_kernel, t, y1, done[0])
    y2 = along(t, "y", False)
    done += list(second())
    t = fold(pair_sum_kernel, t, y2, done[-1])
    x1 = along(t, "x", True)
    t = fold(pair_sum_kernel, t, x1, done[0])
    x2 = along(t, "x", False)
    near, far = call(
        lambda *refs: last_sum_kernel(sign, *refs),
        [VMEM] * 6,
        [keep, got, y1, y2, x1, x2],
        [sds(keep.shape, F32), shape],
        "last_sum",
    )
    return near, swap(far), done


def chunk_product(which, vg, own_ref, other_ref, use):
    rows = pl.ds(pl.multiple_of(lax.rem(dest(which), RING // 2) * 512, 512), 512)
    mine = dest(which) // (RING // 2) == core()

    @pl.when(mine)
    def _():
        use(dot(vg, own_ref[rows, :], NT).astype(BF16))

    @pl.when(jnp.logical_not(mine))
    def _():
        use(dot(vg, other_ref[rows, :], NT).astype(BF16))


def first_kernel(scale, k_ref, vp_ref, near_ref, far_ref, own_ref, other_ref, x_ref, vg_ref, state_ref, right_ref, left_ref, piece_ref):
    join(near_ref, far_ref, state_ref)
    for c in heads_of(k_ref):
        vg_ref[:, c] = (vp_ref[:, c] + dot(k_ref[:, c], state_ref[c, :])).astype(BF16)
    half = right_ref.shape[0]

    def use(p):
        right_ref[...] = p[:half]
        left_ref[...] = p[half:]

    chunk_product(0, vg_ref[...], own_ref, other_ref, use)
    weight_pieces(scale, 1 - core(), vg_ref, x_ref, piece_ref)


def chunks(first, vg_ref, own_ref, other_ref, p_ref):
    @pl.loop(0, p_ref.shape[0])
    def _(i):
        def use(p):
            p_ref[i] = p

        chunk_product(first + i, vg_ref[...], own_ref, other_ref, use)


def work_kernel(scale, vg_ref, own_ref, other_ref, x_ref, p_ref, piece_ref):
    chunks(1, vg_ref, own_ref, other_ref, p_ref)
    weight_pieces(scale, core(), vg_ref, x_ref, piece_ref)


def open_turn_kernel(r_ref, l_ref, p_ref, _, ro_ref, lo_ref):
    half = r_ref.shape[0]
    ro_ref[:half] = (wide(r_ref) + p_ref[0, :half].astype(F32)).astype(BF16)
    ro_ref[half:] = p_ref[0, half:]
    lo_ref[:half] = p_ref[1, :half]
    lo_ref[half:] = (wide(l_ref) + p_ref[1, half:].astype(F32)).astype(BF16)


def turn(first, r_ref, l_ref, p_ref, ro_ref, lo_ref):
    ro_ref[...] = (wide(r_ref) + p_ref[first].astype(F32)).astype(BF16)
    lo_ref[...] = (wide(l_ref) + p_ref[first + 1].astype(F32)).astype(BF16)


def key_grad_kernel(v_ref, kp_ref, state_ref, vg_ref, own_ref, other_ref, _, kg_ref, p_ref):
    def head(c):
        kg_ref[:, c] = (kp_ref[:, c] + dot(v_ref[:, c], state_ref[c, :], NT)).astype(BF16)

    each_head(v_ref, head)
    chunks(3, vg_ref, own_ref, other_ref, p_ref)


def weight_pieces(scale, side, vg_ref, x_ref, o_ref):
    turned = vg_ref[...].T
    shift = side * 128
    for first in range(0, o_ref.shape[0], 4):
        x = jnp.concatenate(
            [
                x_ref[:, pl.ds(pl.multiple_of((first + p) * 256 + shift, 128), 128)]
                for p in range(4)
            ],
            axis=1,
        )
        res = (dot(turned, x) * scale).astype(BF16)
        for p in range(4):
            o_ref[first + p] = res[:, p * 128 : p * 128 + 128]


def chip_kernel(a_ref, b_ref, right, left, cu1, cv1, own):
    half = own.shape[1] // 2

    x, _ = place()

    def s(hop):
        i = lax.rem(x + hop, SIDE)
        return (a_ref[i].astype(F32) + b_ref[i].astype(F32)).astype(BF16)

    t = s(2)
    right[0] = t[:, :half]
    left[0] = t[:, half:]
    t = s(1)
    cu1[...] = t[:, :half]
    right[1] = t[:, half:]
    t = s(3)
    left[1] = t[:, :half]
    cv1[...] = t[:, half:]
    own[...] = s(0)


def pair_kernel(r_ref, l_ref, p_ref, a_ref, b_ref, c_ref, d_ref, ro_ref, lo_ref, o_ref, q_ref):
    turn(0, r_ref, l_ref, p_ref, ro_ref, lo_ref)
    o_ref[...] = (wide(a_ref) + b_ref[0].astype(F32)).astype(BF16)
    q_ref[...] = (wide(c_ref) + d_ref[0].astype(F32)).astype(BF16)


def line_kernel(r_ref, l_ref, p_ref, own_ref, ru_ref, left_ref, right_ref, lv_ref, ro_ref, lo_ref, m1, m2, m3, keep):
    turn(2, r_ref, l_ref, p_ref, ro_ref, lo_ref)
    half = ru_ref.shape[1]
    _, y = place()
    for hop, ref in ((1, m1), (2, m2), (3, m3), (0, keep)):
        i = lax.rem(y + hop, SIDE)
        own = own_ref[i].astype(F32)
        u = own[:half] + ru_ref[i].astype(F32) + left_ref[1, i].astype(F32)
        v = own[half:] + right_ref[1, i].astype(F32) + lv_ref[i].astype(F32)
        ref[:half] = u.astype(ref.dtype)
        ref[half:] = v.astype(ref.dtype)


def owner_kernel(keep_ref, a_ref, b_ref, c_ref, o_ref):
    o_ref[...] = (keep_ref[...] + wide(a_ref) + wide(b_ref) + wide(c_ref)).T


def last_kernel(r_ref, l_ref, p_ref, i_ref):
    i_ref[...] = (p_ref[p_ref.shape[0] - 1].astype(F32) + wide(r_ref) + wide(l_ref)).astype(BF16)


def local(layer_input, query_act, key_act, out_grad, value_weight):
    tok, width = layer_input.shape
    rows, cols = value_weight.shape
    square = sds((tok, cols))
    square_f32 = sds((tok, cols), F32)
    states = sds((cols, HDIM))

    w_other = swap(value_weight)
    x_near, part = call(
        value_own_kernel,
        [HBM, HBM],
        [in_hbm(layer_input), in_hbm(value_weight)],
        [sds((tok, width)), square_f32],
        "value_own",
        scratch=[pltpu.VMEM((rows, cols), BF16), pltpu.SemaphoreType.DMA((width // 512 + rows // 512,))],
    )
    halves = sds((cols // 2, HDIM))
    value, keep, give = call(
        value_rest_kernel,
        [VMEM] * 4,
        [x_near, w_other, part, key_act],
        [square, halves, halves],
        "value_rest",
    )
    near, far, (attended,) = exclusive(
        keep,
        give,
        1,
        lambda: call(
            inside_kernel,
            [VMEM] * 3,
            [query_act, key_act, value],
            [square_f32],
            "inside",
        ),
    )
    low, state, keep, give = call(
        norm_kernel,
        [VMEM] * 5,
        [query_act, out_grad, attended, near, far],
        [square, states, halves, halves],
        "norm_grad",
    )
    near, far, (value_part, query_grad, key_part) = exclusive(
        keep,
        give,
        -1,
        lambda: call(
            masked_kernel, [VMEM] * 3, [query_act, key_act, low], [square_f32], "masked"
        ),
        lambda: call(
            cross_kernel,
            [VMEM] * 5,
            [query_act, key_act, value, low, state],
            [square, square_f32],
            "cross",
        ),
    )

    scale = 1.0 / math.sqrt(tok * lax.axis_size(("ctx", "fsdp")))
    half = sds((tok // 2, 512))
    full = sds((tok, 512))
    pieces = sds((width // 256, cols, 128))
    value_grad, state_grad, r, l, other = call(
        lambda *refs: first_kernel(scale, *refs),
        [VMEM] * 7,
        [key_act, value_part, near, far, value_weight, w_other, x_near],
        [square, states, half, half, pieces],
        "value_grad",
    )
    r, l = along_z(r, 1), along_z(l, -1)
    got = swap(other)
    threes, mine = call(
        lambda *refs: work_kernel(scale, *refs),
        [VMEM] * 4,
        [value_grad, value_weight, w_other, x_near],
        [sds((2, tok, 512)), pieces],
        "work",
    )
    square4 = (SIDE, SIDE) + mine.shape[1:]
    piece = sds((SIDE, cols // 2, 128))
    two_pieces = sds((2,) + piece.shape)
    right, left, cu1, cv1, own = call(
        chip_kernel,
        [VMEM] * 2,
        [mine.reshape(square4), got.reshape(square4)],
        [two_pieces] * 2 + [piece] * 2 + [sds((SIDE, cols, 128))],
        "chip",
    )
    right, left = along_x_ring(right, 1), along_x_ring(left, -1)
    r, l = call(open_turn_kernel, [VMEM] * 3 + [ANY], [r, l, threes, own], [full] * 2, "turn")
    after = r
    r, l = along_z(r, 1), along_z(l, -1)
    key_grad, parts = call(
        key_grad_kernel,
        [VMEM] * 6 + [ANY],
        [value, key_part, state_grad, value_grad, value_weight, w_other, after],
        [square, sds((5, tok, 512))],
        "key_grad",
    )
    r, l, ru1, lv1 = call(
        pair_kernel,
        [VMEM] * 7,
        [r, l, parts, cu1, right, cv1, left],
        [full] * 2 + [piece] * 2,
        "pair",
    )
    r, l = along_z(r, 1), along_z(l, -1)
    ru1, lv1 = along_x_ring(ru1, 1), along_x_ring(lv1, -1)
    r, l, m1, m2, m3, keep = call(
        line_kernel,
        [VMEM] * 8,
        [r, l, parts, own, ru1, left, right, lv1],
        [full] * 2 + [sds((cols, 128))] * 3 + [sds((cols, 128), F32)],
        "line",
    )
    r, l = along_z(r, 1), along_z(l, -1)
    got = [along_y_ring(m, k) for m, k in zip((m1, m2, m3), (1, 2, 3))]
    (weight_grad,) = call(
        owner_kernel, [VMEM] * 4, [keep, *got], [sds((128, cols), F32)], "owner"
    )
    (input_grad,) = call(last_kernel, [VMEM] * 3, [r, l, parts], [full], "last")
    return (query_grad, key_grad, input_grad, weight_grad)


def solution(mesh):
    in_specs = (
        P(("ctx", "fsdp"), None),
        P(("ctx", "fsdp"), "head"),
        P(("ctx", "fsdp"), "head"),
        P(("ctx", "fsdp"), "head"),
        P("fsdp", "head"),
    )
    out_specs = (
        P(("ctx", "fsdp"), "head"),
        P(("ctx", "fsdp"), "head"),
        P(("ctx", "fsdp"), "head"),
        P(("ctx", "fsdp"), "head"),
    )
    return jax.shard_map(local, mesh=mesh, in_specs=in_specs, out_specs=out_specs, check_vma=False)
```
